128 devices in a mesh: img: 64 (over y, z, x), grp: 2 (over core).
Axes of the slice: x: 4, y: 4, z: 4, core: 2. Of those that a mesh axis runs over, the one named last changes fastest.
Arguments:
- tokens: bfloat16 [2048, 16, 768], P(('img', 'grp')), may hold values from -6 to 6
- pair_list: int32 [16384, 2], replicated, may hold values from 0 to 2047, as said below
- pair_live: int32 [16384], replicated, may hold values from 0 to 1, as said below
- gain_self: float32 [768], replicated, may hold values from 0.25 to 1.75
- gain_cross: float32 [768], replicated, may hold values from 0.25 to 1.75
- gain_head: float32 [768], replicated, may hold values from 0.25 to 1.75
- self_qkv: bfloat16 [768, 2304], replicated, may hold values from -8 to 8
- self_out: bfloat16 [768, 768], replicated, may hold values from -0.21875 to 0.21875
- cross_qkv: bfloat16 [768, 2304], replicated, may hold values from -8 to 8
- cross_out: bfloat16 [768, 768], replicated, may hold values from -0.21875 to 0.21875
- head_weight: bfloat16 [768, 7168], P(None, 'grp'), may hold values from -0.21875 to 0.21875
Outputs:
- pixel_maps: bfloat16 [2048, 16, 7168], P(('img', 'grp'))
The draws below stay inside these ranges and needn't reach their ends.
Inputs may be any that keep to these rules, and one draw needn't show every extreme that they name: `pair_list`: rows d * 128 to (d + 1) * 128 - 1 belong to device d of img+grp in flat order. Image g is held by device g // 16. The two images of a row are held by different devices. Among the live rows of one device, the images held by any one device are named at most 2 times in all, and exactly 2 times for some device in every draw. `pair_live`: on each device's 128 rows the live ones come first and number at least 96; some device has all its rows live.
All inputs are finite; a program needn't handle non-finite values.
Results may differ from the reference program's by a relative error of at most 0.014.
Values may be sent and summed in bfloat16 or wider, within the bound.
No kernel may reach another device: no remote copies, remote signals or barrier semaphores. Data moves between devices by JAX's collectives and lax.ppermute only.
A program may use at most 256 MiB of HBM per device.

```python
import math
import jax
import jax.numpy as jnp
from jax import lax

D = 768
HEADS = 12
OUTC = 7168
TOK = 16
IMG_DEV = 16
SLOTS = 128
NIMG = 2048
DEVICES = 128


def pair_tables(key):
    perm_key, image_key, count_key, full_key = jax.random.split(key, 4)
    permutes = jax.vmap(lambda inner: jax.random.permutation(inner, DEVICES))(jax.random.split(perm_key, DEVICES))
    request_ids = jnp.arange(2 * SLOTS) % SLOTS
    owners = permutes[:, request_ids]
    picks = jax.random.randint(image_key, (2, DEVICES, 2 * SLOTS), 0, IMG_DEV)
    local_ids = jnp.minimum(picks[0], picks[1])
    images = (owners * IMG_DEV + local_ids).reshape(DEVICES * SLOTS, 2).astype(jnp.int32)
    counts = jax.random.randint(count_key, (DEVICES,), SLOTS * 3 // 4, SLOTS + 1)
    full_device = jax.random.randint(full_key, (), 0, DEVICES)
    counts = jnp.where(jnp.arange(DEVICES) == full_device, SLOTS, counts)
    live_rows = (jnp.arange(SLOTS)[None, :] < counts[:, None]).astype(jnp.int32).reshape(-1)
    return (images, live_rows)


def draw_pair_list(key, part):
    return pair_tables(key)[0]


def draw_pair_live(key, part):
    return pair_tables(key)[1]


def draw_tokens(key, part):
    key = jax.random.fold_in(key, 11)
    base_key = jax.random.fold_in(key, 0)
    base = jax.random.normal(base_key, (NIMG, TOK, D), jnp.float32)
    return jnp.clip(base, -6.0, 6.0).astype(jnp.bfloat16)


def draw_self_qkv(key, part):
    key = jax.random.fold_in(key, 21)
    query_key, rest_key = jax.random.split(key, 2)
    scale = D ** (-0.5)
    query_part = jax.random.normal(query_key, (D, D), jnp.float32) * scale
    rest_part = jax.random.normal(rest_key, (D, 2 * D), jnp.float32) * scale
    return jnp.clip(jnp.concatenate([query_part, rest_part], axis=1), -8.0, 8.0).astype(jnp.bfloat16)


def draw_cross_qkv(key, part):
    key = jax.random.fold_in(key, 22)
    query_key, rest_key = jax.random.split(key, 2)
    scale = D ** (-0.5)
    query_part = jax.random.normal(query_key, (D, D), jnp.float32) * scale
    rest_part = jax.random.normal(rest_key, (D, 2 * D), jnp.float32) * scale
    return jnp.clip(jnp.concatenate([query_part, rest_part], axis=1), -8.0, 8.0).astype(jnp.bfloat16)


def shard_levels(rng, extent, cuts, smallest, largest):
    level = 1.0
    for position, parts in cuts:
        steps = jax.random.uniform(jax.random.fold_in(jax.random.fold_in(rng, 6), position), (parts,), jnp.float32, smallest / len(cuts), largest / len(cuts))
        level = level * jnp.repeat(jnp.exp(steps), extent[position] // parts).reshape((-1,) + (1,) * (len(extent) - 1 - position))
    return level


def bell_draw(rng, dims, deviation, reach, pieces=(), kind=jnp.bfloat16):
    factor_of = shard_levels(rng, dims, pieces, -0.22, 0.18) if pieces else 1.0
    drawn = jax.random.normal(rng, dims, jnp.float32) * deviation * factor_of
    return jnp.minimum(jnp.maximum(drawn, -reach), reach).astype(kind)


def setup_inputs(seed: int = 0) -> dict:
    key_of = jax.random.split(jax.random.key(seed), 12)
    return {
        "tokens": draw_tokens(jax.random.fold_in(key_of[11], 71), 0),
        "pair_list": draw_pair_list(jax.random.fold_in(key_of[11], 71), 0),
        "pair_live": draw_pair_live(jax.random.fold_in(key_of[11], 71), 0),
        "gain_self": jnp.clip(1.0 + 0.15 * jax.random.normal(key_of[3], (D,), jnp.float32), 0.25, 1.75),
        "gain_cross": jnp.clip(1.0 + 0.15 * jax.random.normal(key_of[4], (D,), jnp.float32), 0.25, 1.75),
        "gain_head": jnp.clip(1.0 + 0.15 * jax.random.normal(key_of[5], (D,), jnp.float32), 0.25, 1.75),
        "self_qkv": draw_self_qkv(jax.random.fold_in(key_of[11], 71), 0),
        "self_out": bell_draw(key_of[7], (D, D), D ** -0.5, 0.21875),
        "cross_qkv": draw_cross_qkv(jax.random.fold_in(key_of[11], 71), 0),
        "cross_out": bell_draw(key_of[9], (D, D), D ** -0.5, 0.21875),
        "head_weight": bell_draw(key_of[10], (D, OUTC), D ** -0.5, 0.21875, ((1, 2),)),
    }


EPSILON = 1e-05

def normalize(values, gain_vec):
    mean_val = lax.optimization_barrier(jnp.mean(values, axis=-1, keepdims=True))
    centred = values - mean_val
    variance = lax.optimization_barrier(jnp.mean(centred * centred, axis=-1, keepdims=True))
    return centred / jnp.sqrt(variance + EPSILON) * gain_vec

def project(inputs, matrix):
    lead_shape = inputs.shape[:-1]
    flat_rows = inputs.reshape(-1, inputs.shape[-1])
    result = jnp.dot(flat_rows, matrix, preferred_element_type=jnp.float32)
    return result.astype(jnp.bfloat16).reshape(lead_shape + (matrix.shape[1],))

def attend(queries, key_rows, value_rows):
    batch_size, tok_count, model_width = queries.shape
    head_size = model_width // HEADS
    shaped = (batch_size, tok_count, HEADS, head_size)
    scores = jnp.einsum('bqhd,bkhd->bhqk', queries.reshape(shaped).astype(jnp.float32), key_rows.reshape(shaped).astype(jnp.float32)) * (1.0 / math.sqrt(head_size))
    attn_weights = jax.nn.softmax(scores, axis=-1).astype(jnp.bfloat16)
    mixed_rows = jnp.einsum('bhqk,bkhd->bqhd', attn_weights.astype(jnp.float32), value_rows.reshape(shaped).astype(jnp.float32))
    return mixed_rows.astype(jnp.bfloat16).reshape(batch_size, tok_count, model_width)

def reference(tokens, pair_list, pair_live, gain_self, gain_cross, gain_head, self_qkv, self_out, cross_qkv, cross_out, head_weight):
    token_f32 = tokens.astype(jnp.float32)
    image_count, tok_count, model_width = tokens.shape
    cross_rows = normalize(token_f32, gain_cross).astype(jnp.bfloat16)
    cross_proj = project(cross_rows, cross_qkv)
    queries, key_rows, value_rows = jnp.split(cross_proj, 3, axis=-1)
    first_ids = pair_list[:, 0].astype(jnp.int32)
    second_ids = pair_list[:, 1].astype(jnp.int32)
    mixed_first = attend(queries[first_ids], key_rows[second_ids], value_rows[second_ids])
    mixed_second = attend(queries[second_ids], key_rows[first_ids], value_rows[first_ids])
    live_weight = pair_live.astype(jnp.float32)
    degree = jnp.zeros((image_count,), jnp.float32).at[first_ids].add(live_weight).at[second_ids].add(live_weight)
    cross_sum = jnp.zeros((image_count, tok_count, model_width), jnp.float32)
    cross_sum = cross_sum.at[first_ids].add(mixed_first.astype(jnp.float32) * live_weight[:, None, None])
    cross_sum = cross_sum.at[second_ids].add(mixed_second.astype(jnp.float32) * live_weight[:, None, None])
    cross_mean = (cross_sum / jnp.maximum(degree, 1.0)[:, None, None]).astype(jnp.bfloat16)
    cross_term = jnp.dot(cross_mean.reshape(-1, model_width), cross_out, preferred_element_type=jnp.float32)
    self_rows = normalize(token_f32, gain_self).astype(jnp.bfloat16)
    self_parts = jnp.split(project(self_rows, self_qkv), 3, axis=-1)
    self_mixed = attend(self_parts[0], self_parts[1], self_parts[2])
    self_term = jnp.dot(self_mixed.reshape(-1, model_width), self_out, preferred_element_type=jnp.float32)
    combined = token_f32.reshape(-1, model_width) + self_term + cross_term
    head_rows = normalize(combined, gain_head).astype(jnp.bfloat16)
    pixel_maps = jnp.dot(head_rows, head_weight, preferred_element_type=jnp.float32).astype(jnp.bfloat16)
    return pixel_maps.reshape(image_count, tok_count, -1)
```

```python
import functools

import jax
import jax.numpy as jnp
from jax import lax
from jax.experimental import pallas as pl
from jax.experimental.pallas import tpu as pltpu
from jax.sharding import PartitionSpec as P

HEADS = 12
DH = 64
D = 768
TOK = 16
IMG = 16
HELD = 256
CAP = 80
BLK = 256
PARTS = 3
GROUP = 12
WIDE = 4
EPSILON = 1e-05
STRIDES = (16, 4, 1)
BF = jnp.bfloat16
F32 = jnp.float32
VMEM = pl.BlockSpec(memory_space=pltpu.VMEM)
ANY = pl.BlockSpec(memory_space=pl.ANY)
SMEM = pl.BlockSpec(memory_space=pltpu.SMEM)
BIG = 60 * 1024 * 1024


def dot(a, b, dims=((1,), (0,))):
    return lax.dot_general(a, b, (dims, ((), ())), preferred_element_type=F32)


def norm(values, gain):
    mean_val = jnp.mean(values, axis=-1, keepdims=True)
    centred = values - mean_val
    variance = jnp.mean(centred * centred, axis=-1, keepdims=True)
    return centred * lax.rsqrt(variance + EPSILON) * gain


def sds(*shape, dtype=BF):
    return jax.ShapeDtypeStruct(shape, dtype)


def call(kernel, outs, specs, out_specs, scratch=(), limit=BIG, flops=0, size=0):
    return pl.pallas_call(
        kernel,
        out_shape=outs,
        in_specs=specs,
        out_specs=out_specs,
        scratch_shapes=list(scratch),
        compiler_params=pltpu.CompilerParams(vmem_limit_bytes=limit),
        cost_estimate=pl.CostEstimate(flops=flops, bytes_accessed=size, transcendentals=0),
    )


def norm_kernel(tok_ref, gain_ref, *outs):
    rows = norm(tok_ref[...].astype(F32), gain_ref[...]).astype(BF)
    for r in range(PARTS):
        outs[r][...] = rows[:, r * BLK : (r + 1) * BLK]


def self_kernel(tok_ref, gain_ref, qkv_ref, out_ref, base_ref):
    tok = tok_ref[...].astype(F32)
    rows = norm(tok, gain_ref[...]).astype(BF)
    proj = dot(rows, qkv_ref[...]).astype(BF)
    n = tok.shape[0]
    same = (lax.broadcasted_iota(jnp.int32, (n, n), 0) // TOK) == (
        lax.broadcasted_iota(jnp.int32, (n, n), 1) // TOK
    )
    total = tok
    mixed = []
    for h in range(HEADS):
        q = proj[:, h * DH : (h + 1) * DH]
        k = proj[:, D + h * DH : D + (h + 1) * DH]
        v = proj[:, 2 * D + h * DH : 2 * D + (h + 1) * DH]
        s = dot(q, k, ((1,), (1,))) * 0.125
        s = jnp.where(same, s, -1e30)
        e = jnp.exp(s - jnp.max(s, axis=1, keepdims=True))
        p = (e / jnp.sum(e, axis=1, keepdims=True)).astype(BF)
        mixed.append(dot(p, v).astype(BF))
    base_ref[...] = total + dot(jnp.concatenate(mixed, axis=1), out_ref[...])


def fold_kernel(rows_ref, wq_ref, wk_ref, out_ref):
    q = (dot(rows_ref[...], wq_ref[...]).astype(BF).astype(F32) * 0.125).astype(BF)
    images = rows_ref.shape[0] // TOK
    for h in range(HEADS):
        g = dot(q[:, h * DH : (h + 1) * DH], wk_ref[:, h * DH : (h + 1) * DH], ((1,), (1,)))
        out_ref[:, h * TOK : (h + 1) * TOK, :] = g.astype(BF).reshape(images, TOK, D)


def gather_kernel(cap, list_ref, *refs):
    held, outs, buf, sems = refs[:4], refs[4:8], refs[8], refs[9]
    size = HELD // 4
    copies = [
        pltpu.make_async_copy(held[i], buf.at[pl.ds(i * size, size)], sems.at[i])
        for i in range(4)
    ]
    for c in copies:
        c.start()
    for c in copies:
        c.wait()

    def step(s, carry):
        for d in range(4):
            outs[d][s] = buf[list_ref[d * cap + s]]
        return carry

    lax.fori_loop(0, cap, step, 0, unroll=4)


def cross_kernel(cap, slot_ref, off_ref, g_ref, wv_ref, *refs):
    parts = refs[: 4 * PARTS]
    out_ref, buf, xs, acc, mix, sems = refs[4 * PARTS :]
    entries = slot_ref.shape[0] // PARTS
    copies = [
        pltpu.make_async_copy(
            parts[r * 4 + o], buf.at[r, pl.ds(o * cap, cap)], sems.at[r * 4 + o]
        )
        for r in range(PARTS)
        for o in range(4)
    ]
    for c in copies:
        c.start()
    for c in copies:
        c.wait()
    images = g_ref.shape[0]
    row_pair = lax.broadcasted_iota(jnp.int32, (GROUP * TOK, 1), 0) // TOK

    def attended(a, chunk, i):
        start = off_ref[a] + chunk * GROUP
        left = off_ref[a + 1] - start
        for j in range(GROUP):
            p = jnp.where(j < left, start + j, 0)
            for r in range(PARTS):
                xs[i, j * TOK : (j + 1) * TOK, r * BLK : (r + 1) * BLK] = buf[
                    r, slot_ref[r * entries + p]
                ]
        x = xs[i]
        s = dot(x, g_ref[a], ((1,), (1,))).reshape(GROUP, TOK, HEADS * TOK)
        e = jnp.exp(s - jnp.max(s, axis=1, keepdims=True))
        w = (e / jnp.sum(e, axis=1, keepdims=True)).reshape(GROUP * TOK, HEADS * TOK)
        w = jnp.where(row_pair < left, w, 0.0).astype(BF)
        return dot(w, x, ((0,), (0,)))

    def group(step, carry):
        for i in range(WIDE):
            acc[i] = attended(step * WIDE + i, 0, i)
        for i in range(WIDE):
            a = step * WIDE + i
            chunks = (off_ref[a + 1] - off_ref[a] + GROUP - 1) // GROUP

            def more(c, carry, a=a, i=i):
                acc[i] += attended(a, c, i)
                return carry

            lax.fori_loop(1, chunks, more, 0)
            mix[a] = acc[i].astype(BF)
        return carry

    lax.fori_loop(0, images // WIDE, group, 0)
    for h in range(HEADS):
        u = mix[:, h * TOK : (h + 1) * TOK, :].reshape(images * TOK, D)
        out_ref[:, h * DH : (h + 1) * DH] = dot(u, wv_ref[:, h * DH : (h + 1) * DH])


def tail_kernel(mine_ref, other_ref, inv_ref, base_ref, out_w_ref, gain_ref, rows_ref):
    total = mine_ref[...] + other_ref[...].astype(F32)
    mean = (total / inv_ref[...]).astype(BF)
    combined = base_ref[...] + dot(mean, out_w_ref[...])
    rows_ref[...] = norm(combined, gain_ref[...]).astype(BF)


def coords(chip):
    return [(chip // s) % 4 for s in STRIDES]


def moved(axis, shift):
    pairs = []
    for chip in range(64):
        c = (chip // STRIDES[axis]) % 4
        pairs.append((chip, chip + ((c + shift) % 4 - c) * STRIDES[axis]))
    return pairs


def from_offset(x, axis, offset):
    return lax.ppermute(x, "img", moved(axis, -offset))


def axes_of(r):
    return r % 3, (r + 1) % 3, (r + 2) % 3


def body(
    tokens, pair_list, pair_live, gain_self, gain_cross, gain_head,
    self_qkv, self_out, cross_qkv, cross_out, head_weight,
):
    chip = lax.axis_index("img")
    core = lax.axis_index("grp")
    flat_tokens = tokens.reshape(IMG * TOK, D)
    rows = call(norm_kernel, [sds(IMG * TOK, BLK)] * PARTS, [VMEM] * 2, [VMEM] * PARTS)(
        flat_tokens, gain_cross[None]
    )
    blocks = [x.reshape(IMG, TOK, BLK) for x in rows]
    near = [[blocks[r]] + [None] * 3 for r in range(PARTS)]
    for o in (1, 3, 2):
        for r in range(PARTS):
            near[r][o] = from_offset(blocks[r], axes_of(r)[0], o)
    lines = [jnp.concatenate(near[r], axis=0) for r in range(PARTS)]
    held = [[lines[r]] + [None] * 3 for r in range(PARTS)]
    for o in (1, 3, 2):
        for r in range(PARTS):
            held[r][o] = from_offset(lines[r], axes_of(r)[1], o)

    first, second = [x.reshape(128, 128) for x in (pair_list[:, 0], pair_list[:, 1])]
    own = jnp.concatenate([first, second], axis=1)
    partner = jnp.concatenate([second, first], axis=1)
    live = jnp.concatenate([pair_live.reshape(128, 128)] * 2, axis=1) == 1
    my_coords = coords(chip)
    chips = [chip]
    for r in range(PARTS):
        axis = axes_of(r)[2]
        c = my_coords[axis]
        for o in (1, 2, 3):
            chips.append(chip + ((c - o) % 4 - c) * STRIDES[axis])
    chips = jnp.stack(chips)
    devices = (2 * chips[:, None] + jnp.arange(2)[None, :]).reshape(-1)
    usable = live & ((partner // IMG) % 2 == core)
    owner = jnp.where(usable, own // IMG, -1)
    mine = owner[None] == devices[:, None, None]
    before = (jnp.arange(256)[:, None] < jnp.arange(256)[None, :]).astype(BF)
    rank = jnp.dot(mine.astype(BF).reshape(-1, 256), before, preferred_element_type=F32)
    rank = jnp.where(mine, rank.reshape(mine.shape), -1.0)
    code = (own % 32) * 2048 + partner + 1
    table = jnp.stack(
        [jnp.sum(jnp.where(rank == float(k), code[None], 0), axis=2) for k in range(2)], axis=-1
    ).reshape(chips.shape[0], -1) - 1
    valid = table >= 0
    partners = table & 2047
    pcoords = coords(partners // 32)
    local = partners % IMG
    ids = jnp.arange(HELD)

    def place(r, sel, ref_coords):
        a1, a2, a3 = axes_of(r)
        o1, o2, o3 = [(pcoords[a][sel] - ref_coords[a]) % 4 for a in (a1, a2, a3)]
        return (o2 * 4 + o1) * IMG + local[sel], o3

    wanted = []
    own_place = []
    for r in range(PARTS):
        where, off = place(r, 0, my_coords)
        own_place.append(off * HELD + where)
        rows_wanted = [jnp.any((where[:, None] == ids) & (valid[0] & (off == 0))[:, None], axis=0)]
        for o in (1, 2, 3):
            sel = 1 + 3 * r + o - 1
            where, off = place(r, sel, my_coords)
            rows_wanted.append(
                jnp.any((where[:, None] == ids) & (valid[sel] & (off == 0))[:, None], axis=0)
            )
        wanted.append(jnp.stack(rows_wanted))
    wanted = jnp.stack(wanted)
    sent_rank = jnp.dot(
        wanted.astype(BF).reshape(-1, HELD), before, preferred_element_type=F32
    ).reshape(wanted.shape)
    sent_rank = jnp.where(wanted, sent_rank, -1.0)
    longest = lax.pmax(jnp.max(sent_rank), ("img", "grp"))

    own_place = jnp.stack(own_place)
    needed = jnp.any(
        (own_place[:, :, None] == jnp.arange(4 * HELD)) & valid[0][None, :, None], axis=1
    )
    need_rank = jnp.dot(
        needed.astype(BF).reshape(-1, HELD), before, preferred_element_type=F32
    ).reshape(PARTS, 4 * HELD)
    my_rank = jnp.sum(
        jnp.where(own_place[:, :, None] == jnp.arange(4 * HELD), need_rank[:, None, :], 0.0), axis=2
    ).astype(jnp.int32)
    my_off = own_place // HELD
    key = jnp.where(valid[0], table[0] >> 11, 32)
    entry = jnp.arange(key.shape[0])
    ahead = (key[None, :] < key[:, None]) | (
        (key[None, :] == key[:, None]) & (entry[None, :] < entry[:, None])
    )
    position = jnp.sum(ahead.astype(jnp.int32), axis=1)
    offsets = jnp.sum((key[None, :] < jnp.arange(40)[:, None]).astype(jnp.int32), axis=1)

    own_rows = jnp.concatenate(rows, axis=1)
    other_rows = lax.ppermute(own_rows, "grp", [(0, 1), (1, 0)])
    chip_rows = jnp.where(
        core == 0,
        jnp.concatenate([own_rows, other_rows], axis=0),
        jnp.concatenate([other_rows, own_rows], axis=0),
    )
    wq, wk, wv = [cross_qkv[:, i * D : (i + 1) * D] for i in range(3)]
    folded = call(fold_kernel, sds(2 * IMG, HEADS * TOK, D), [VMEM] * 3, VMEM)(chip_rows, wq, wk)
    base = call(self_kernel, sds(IMG * TOK, D, dtype=F32), [VMEM] * 4, VMEM)(
        flat_tokens, gain_self[None], self_qkv, self_out
    )

    def last_phase(cap, held, sent_rank, my_off, my_rank, position, valid_own, offsets, folded, wv):
        lists = jnp.sum(
            jnp.where(
                sent_rank[:, :, None, :] == jnp.arange(cap, dtype=F32)[:, None], ids, 0
            ),
            axis=-1,
        ).reshape(PARTS, 4 * cap)
        slots = jnp.where(valid_own, my_off * cap + my_rank, 0)
        slots = jnp.sum(
            jnp.where(position[None, :, None] == entry, slots[:, :, None], 0), axis=1
        ).reshape(-1)
        arrived = []
        for r in range(PARTS):
            out = call(
                functools.partial(gather_kernel, cap),
                [sds(cap, TOK, BLK)] * 4,
                [SMEM] + [ANY] * 4,
                [VMEM] * 4,
                [pltpu.VMEM((HELD, TOK, BLK), BF), pltpu.SemaphoreType.DMA((4,))],
            )(lists[r], *held[r])
            arrived.append(list(out))
        for o in (1, 3, 2):
            for r in range(PARTS):
                arrived[r][o] = from_offset(arrived[r][o], axes_of(r)[2], o)
        return call(
            functools.partial(cross_kernel, cap),
            sds(2 * IMG * TOK, D, dtype=F32),
            [SMEM] * 2 + [VMEM] * 2 + [ANY] * 12,
            VMEM,
            [
                pltpu.VMEM((PARTS, 4 * cap, TOK, BLK), BF),
                pltpu.VMEM((WIDE, GROUP * TOK, D), BF),
                pltpu.VMEM((WIDE, HEADS * TOK, D), F32),
                pltpu.VMEM((2 * IMG, HEADS * TOK, D), BF),
                pltpu.SemaphoreType.DMA((12,)),
            ],
        )(slots, offsets, folded, wv, *arrived[0], *arrived[1], *arrived[2])

    summed = lax.cond(
        longest < CAP,
        functools.partial(last_phase, CAP),
        functools.partial(last_phase, HELD),
        held, sent_rank, my_off, my_rank, position, valid[0][None], offsets, folded, wv,
    )
    size = IMG * TOK
    mine_sum = lax.dynamic_slice_in_dim(summed, core * size, size, 0)
    other_sum = lax.dynamic_slice_in_dim(summed, (1 - core) * size, size, 0).astype(BF)
    other_sum = lax.ppermute(other_sum, "grp", [(0, 1), (1, 0)])
    my_images = (2 * chip + core) * IMG + jnp.arange(IMG)
    degree = jnp.sum(
        ((own[None] == my_images[:, None, None]) & live[None]).astype(F32), axis=(1, 2)
    )
    divisor = jnp.repeat(jnp.maximum(degree, 1.0), TOK)[:, None]
    head_rows = call(tail_kernel, sds(size, D), [VMEM] * 6, VMEM)(
        mine_sum, other_sum, divisor, base, cross_out, gain_head[None]
    )
    pixel_maps = jnp.dot(
        head_rows,
        lax.all_gather(head_weight, "grp", axis=1, tiled=True),
        preferred_element_type=F32,
    ).astype(BF)
    return pixel_maps.reshape(IMG, TOK, -1)


def solution(mesh):
    placed = (P(("img", "grp"), None, None),) + (P(),) * 9 + (P(None, "grp"),)
    return jax.shard_map(
        body, mesh=mesh, in_specs=placed, out_specs=P(("img", "grp"), None, None), check_vma=False
    )
```

```python
import functools

import jax
import jax.numpy as jnp
from jax import lax
from jax.experimental import pallas as pl
from jax.experimental.pallas import tpu as pltpu
from jax.sharding import PartitionSpec as P

HEADS = 12
DH = 64
D = 768
TOK = 16
IMG = 16
HELD = 256
CAP = 88
BLK = 256
PARTS = 3
GROUP = 12
WIDE = 4
HEAD_TILES = 7
EPSILON = 1e-05
STRIDES = (16, 4, 1)
BF = jnp.bfloat16
F32 = jnp.float32
VMEM = pl.BlockSpec(memory_space=pltpu.VMEM)
ANY = pl.BlockSpec(memory_space=pl.ANY)
SMEM = pl.BlockSpec(memory_space=pltpu.SMEM)
MIB = 1024 * 1024


def axes_of(r):
    return r % 3, (r + 1) % 3, (r + 2) % 3


def dot(a, b, dims=((1,), (0,))):
    return lax.dot_general(a, b, (dims, ((), ())), preferred_element_type=F32)


def norm(values, gain):
    mean_val = jnp.mean(values, axis=-1, keepdims=True)
    centred = values - mean_val
    variance = jnp.mean(centred * centred, axis=-1, keepdims=True)
    return centred * lax.rsqrt(variance + EPSILON) * gain


def sds(*shape, dtype=BF):
    return jax.ShapeDtypeStruct(shape, dtype)


def call(kernel, outs, specs, out_specs, scratch=(), limit=16, flops=0, size=0):
    return pl.pallas_call(
        kernel,
        out_shape=outs,
        in_specs=specs,
        out_specs=out_specs,
        scratch_shapes=list(scratch),
        compiler_params=pltpu.CompilerParams(vmem_limit_bytes=limit * MIB),
        cost_estimate=pl.CostEstimate(flops=flops, bytes_accessed=size, transcendentals=0),
    )


def norm_kernel(tok_ref, gain_ref, *outs):
    rows = norm(tok_ref[...].astype(F32), gain_ref[...].reshape(1, D)).astype(BF)
    for r in range(PARTS):
        outs[r][...] = rows[:, r * BLK : (r + 1) * BLK]
    outs[PARTS][...] = rows


def self_kernel(tok_ref, gain_ref, qkv_ref, out_ref, base_ref):
    tok = tok_ref[...].astype(F32)
    rows = norm(tok, gain_ref[...].reshape(1, D)).astype(BF)
    proj = dot(rows, qkv_ref[...]).astype(BF)
    n = tok.shape[0]
    same = (lax.broadcasted_iota(jnp.int32, (n, n), 0) // TOK) == (
        lax.broadcasted_iota(jnp.int32, (n, n), 1) // TOK
    )
    total = tok
    mixed = []
    for h in range(HEADS):
        q = proj[:, h * DH : (h + 1) * DH]
        k = proj[:, D + h * DH : D + (h + 1) * DH]
        v = proj[:, 2 * D + h * DH : 2 * D + (h + 1) * DH]
        s = dot(q, k, ((1,), (1,))) * 0.125
        s = jnp.where(same, s, -1e30)
        e = jnp.exp(s - jnp.max(s, axis=1, keepdims=True))
        p = (e / jnp.sum(e, axis=1, keepdims=True)).astype(BF)
        mixed.append(dot(p, v).astype(BF))
    base_ref[...] = total + dot(jnp.concatenate(mixed, axis=1), out_ref[...])


def fold_kernel(own_ref, other_ref, qkv_ref, out_ref):
    rows = jnp.concatenate([own_ref[...], other_ref[...]], axis=0)
    q = (dot(rows, qkv_ref[:, :D]).astype(BF).astype(F32) * 0.125).astype(BF)
    images = rows.shape[0] // TOK
    for h in range(HEADS):
        keys = qkv_ref[:, D + h * DH : D + (h + 1) * DH]
        g = dot(q[:, h * DH : (h + 1) * DH], keys, ((1,), (1,)))
        out_ref[:, h * TOK : (h + 1) * TOK, :] = g.astype(BF).reshape(images, TOK, D)


def plan_kernel(
    ids_ref, first_ref, second_ref, live_ref, lists_ref, codes_ref, offs_ref, div_ref
):
    chip, core = ids_ref[0], ids_ref[1]
    own = jnp.concatenate([first_ref[...], second_ref[...]], axis=1)
    partner = jnp.concatenate([second_ref[...], first_ref[...]], axis=1)
    live = jnp.concatenate([live_ref[...]] * 2, axis=1)
    groups, sides = own.shape

    def iota(shape, axis):
        return lax.broadcasted_iota(jnp.int32, shape, axis)

    before = (iota((sides, sides), 0) < iota((sides, sides), 1)).astype(F32).astype(BF)
    usable = (live == 1) & (((partner >> 4) & 1) == core)
    owner = jnp.where(usable, own >> 4, -1)
    code = ((((((own >> 4) & 1) ^ core) * IMG + (own & 15)) << 11) + partner + 1).astype(F32)
    my = [(chip >> 4) & 3, (chip >> 2) & 3, chip & 3]
    steps = (16, 4, 1)
    lane = iota((groups, 128), 1)
    table = jnp.zeros((groups, 128), F32)
    for sel in range(1 + 3 * PARTS):
        target = chip
        if sel:
            r, o = (sel - 1) // 3, (sel - 1) % 3 + 1
            axis = axes_of(r)[2]
            target = chip + (((my[axis] - o) & 3) - my[axis]) * steps[axis]
        for dev in range(2):
            mine = owner == 2 * target + dev
            rank = dot(mine.astype(F32).astype(BF), before)
            for k in range(2):
                col = jnp.sum(jnp.where(mine & (rank == float(k)), code, 0.0), axis=1, keepdims=True)
                table = jnp.where(lane == sel * 4 + dev * 2 + k, col, table)
    table = table.astype(jnp.int32) - 1
    valid = table >= 0
    partners = table & 2047
    local = partners & 15
    sel = lane >> 2
    lane_r = jnp.where(sel > 6, 2, jnp.where(sel > 3, 1, 0))
    lane_o = jnp.where(sel > 0, sel - 3 * lane_r, 0)
    places, offsets = [], []
    for r in range(PARTS):
        offs = []
        for axis in axes_of(r):
            shift = 0
            for q in range(PARTS):
                if axes_of(q)[2] == axis:
                    shift = jnp.where((lane_r == q) & (sel > 0), lane_o, 0)
            here = (my[axis] - shift) & 3
            offs.append((((partners >> (5 + (4, 2, 0)[axis])) & 3) - here) & 3)
        places.append((offs[1] * 4 + offs[0]) * IMG + local)
        offsets.append(offs[2])
    ids = iota((groups, HELD), 1)

    def present(r, sel, o):
        spot = jnp.where(valid & (offsets[r] == o), places[r], -1)
        hits = jnp.zeros((groups, HELD), F32)
        for c in range(sel * 4, sel * 4 + 4):
            hits = jnp.where(spot[:, c : c + 1] == ids, 1.0, hits)
        return jnp.max(hits, axis=0, keepdims=True)

    pad = jnp.zeros((4, HELD), F32)
    sent = jnp.concatenate(
        [present(r, 1 + 3 * r + o - 1 if o else 0, o) for r in range(PARTS) for o in range(4)] + [pad],
        axis=0,
    )
    sent_rank = jnp.where(sent > 0.0, dot(sent.astype(BF), before), -1.0)
    spots = iota((HELD, HELD), 0).astype(F32)
    images = iota((HELD, HELD), 1).astype(F32)
    for c in range(4 * PARTS):
        col = jnp.sum(jnp.where(sent_rank[c : c + 1, :] == spots, images, 0.0), axis=1, keepdims=True)
        lists_ref[:, c : c + 1] = col.astype(jnp.int32)
    got = jnp.concatenate(
        [present(r, 0, o) for r in range(PARTS) for o in range(4)] + [pad], axis=0
    )
    got_rank = dot(got.astype(BF), before)
    key = jnp.where(valid, table >> 11, 127)
    small = iota((groups, 128), 1)
    earlier = (iota((groups, groups), 1) < iota((groups, groups), 0)).astype(F32).astype(BF)
    marks = [(key[:, c : c + 1] == small).astype(F32) for c in range(4)]
    starts = jnp.zeros((1, 128), F32)
    for c in range(4):
        starts = starts + jnp.sum((key[:, c : c + 1] < small).astype(F32), axis=0, keepdims=True)
    offs_ref[...] = jnp.broadcast_to(starts, (8, 128)).astype(jnp.int32)
    long_ids = iota((groups, 512), 1)
    ahead = starts
    ordered = [jnp.zeros((1, 512), F32) for _ in range(PARTS)]
    for c in range(4):
        pos = jnp.sum(marks[c] * (ahead + dot(earlier, marks[c].astype(BF))), axis=1, keepdims=True)
        ahead = ahead + jnp.sum(marks[c], axis=0, keepdims=True)
        pos = jnp.where(valid[:, c : c + 1], pos.astype(jnp.int32), -1)
        chosen = pos == long_ids
        for r in range(PARTS):
            slot = (offsets[r][:, c : c + 1] * HELD).astype(F32)
            for o in range(4):
                spot = jnp.where(valid & (offsets[r] == o), places[r], -1)[:, c : c + 1]
                row = got_rank[r * 4 + o : r * 4 + o + 1, :]
                slot = slot + jnp.sum(jnp.where(spot == ids, row, 0.0), axis=1, keepdims=True)
            ordered[r] = ordered[r] + jnp.sum(jnp.where(chosen, slot, 0.0), axis=0, keepdims=True)
    codes_ref[...] = jnp.concatenate(ordered + [jnp.zeros((5, 512), F32)], axis=0).astype(jnp.int32)
    named = jnp.where(live == 1, own, -1) - (2 * chip + core) * IMG
    for i in range(IMG):
        count = jnp.sum((named == i).astype(F32))
        div_ref[i * TOK : (i + 1) * TOK, :] = jnp.full((TOK, 128), jnp.maximum(count, 1.0), F32)


def count_kernel(first_ref, second_ref, live_ref, longest_ref, seen):
    chips, sources, fields = 64, 128, 4
    width = first_ref.shape[1]

    def iota(shape, axis):
        return lax.broadcasted_iota(jnp.int32, shape, axis)

    wide = iota((chips * fields, width), 0)
    plain = iota((chips, width), 0)
    source = iota((sources, width), 0)
    seen[...] = jnp.zeros_like(seen)

    def step(i, carry):
        one, two = first_ref[pl.ds(i, 1), :], second_ref[pl.ds(i, 1), :]
        live = live_ref[pl.ds(i, 1), :] == 1
        for own, partner in ((one, two), (two, one)):
            chip = jnp.where(live, own >> 5, -8)
            local = partner & 15
            weight = jnp.where(
                (local & 2) == 0,
                jnp.where((local & 1) == 0, 1.0, 64.0),
                jnp.where((local & 1) == 0, 4096.0, 262144.0),
            )
            left = jnp.concatenate(
                [
                    jnp.where(chip * fields + (local >> 2) == wide, weight, 0.0).astype(BF),
                    jnp.where(chip == plain, 1.0, 0.0).astype(BF),
                ],
                axis=0,
            )
            right = jnp.where((partner >> 4) == source, 1.0, 0.0).astype(BF)
            seen[...] += dot(right, left, ((1,), (1,)))
        return carry

    lax.fori_loop(0, first_ref.shape[0], step, 0)
    packed = seen[:, : chips * fields].astype(jnp.int32)
    found = jnp.zeros(packed.shape, F32)
    for f in range(fields):
        found = found + jnp.where(((packed >> (6 * f)) & 63) > 0, 1.0, 0.0)
    row, col = iota((128, sources), 0), iota((128, sources), 1)
    axis, coord = row >> 3, (row >> 1) & 3
    moved_by = jnp.where(axis == 0, 5, jnp.where(axis == 1, 3, 1))
    member = ((col & 1) == (row & 1)) & (((col >> moved_by) & 3) == coord) & (axis < 3)
    groups = dot(member.astype(F32).astype(BF), found.astype(BF))
    merge = (iota((chips * fields, 128), 0) >> 2) == iota((chips * fields, 128), 1)
    totals = dot(groups.astype(BF), merge.astype(F32).astype(BF))
    crowded = jnp.max(seen[:, chips * fields :]) >= 64.0
    longest_ref[...] = jnp.full(
        longest_ref.shape, jnp.where(crowded, 1000.0, jnp.max(totals)), F32
    )


def gather_kernel(cap, r, list_ref, *refs):
    held, outs, buf = refs[:4], refs[4:8], refs[8]
    size = HELD // 4
    for i in range(4):
        buf[i * size : (i + 1) * size] = held[i][...]

    def step(s, carry):
        for d in range(4):
            outs[d][s] = buf[list_ref[s, r * 4 + d]]
        return carry

    lax.fori_loop(0, cap, step, 0, unroll=4)


def cross_kernel(cap, code_ref, off_ref, g_ref, qkv_ref, *refs):
    parts = refs[: 4 * PARTS]
    mine_ref, other_ref, buf, wv, xs, acc, mix, sems = refs[4 * PARTS :]
    copies = [
        pltpu.make_async_copy(
            parts[r * 4 + o], buf.at[r, pl.ds(o * cap, cap)], sems.at[r * 4 + o]
        )
        for r in range(PARTS)
        for o in range(4)
    ]
    copies.append(
        pltpu.make_async_copy(qkv_ref.at[:, pl.ds(2 * D, D)], wv, sems.at[4 * PARTS])
    )
    for c in copies:
        c.start()
    for c in copies:
        c.wait()
    images = g_ref.shape[0]
    row_pair = lax.broadcasted_iota(jnp.int32, (GROUP * TOK, 1), 0) // TOK

    def attended(a, chunk, i):
        start = off_ref[0, a] + chunk * GROUP
        left = off_ref[0, a + 1] - start
        for j in range(GROUP):
            p = jnp.where(j < left, start + j, 0)
            for r in range(PARTS):
                code = code_ref[r, p]
                xs[i, j * TOK : (j + 1) * TOK, r * BLK : (r + 1) * BLK] = buf[
                    r, (code >> 8) * cap + (code & 255)
                ]
        x = xs[i]
        s = dot(x, g_ref[a], ((1,), (1,))).reshape(GROUP, TOK, HEADS * TOK)
        e = jnp.exp(s - jnp.max(s, axis=1, keepdims=True))
        w = (e / jnp.sum(e, axis=1, keepdims=True)).reshape(GROUP * TOK, HEADS * TOK)
        w = jnp.where(row_pair < left, w, 0.0).astype(BF)
        return dot(w, x, ((0,), (0,)))

    def group(step, carry):
        for i in range(WIDE):
            acc[i] = attended(step * WIDE + i, 0, i)
        for i in range(WIDE):
            a = step * WIDE + i
            chunks = (off_ref[0, a + 1] - off_ref[0, a] + GROUP - 1) // GROUP

            def more(c, carry, a=a, i=i):
                acc[i] += attended(a, c, i)
                return carry

            lax.fori_loop(1, chunks, more, 0)
            mix[a] = acc[i].astype(BF)
        return carry

    lax.fori_loop(0, images // WIDE, group, 0)
    for h in range(HEADS):
        u = mix[:, h * TOK : (h + 1) * TOK, :].reshape(images * TOK, D)
        o = dot(u, wv[:, h * DH : (h + 1) * DH])
        mine_ref[:, h * DH : (h + 1) * DH] = o[: IMG * TOK]
        other_ref[:, h * DH : (h + 1) * DH] = o[IMG * TOK :].astype(BF)


def head_kernel(
    mine_ref, other_ref, div_ref, base_ref, cross_out_ref, gain_ref, weight_ref,
    out_ref, weights, staged, in_sems, out_sems,
):
    tile = weight_ref.shape[1] // HEAD_TILES
    loads = [
        pltpu.make_async_copy(
            weight_ref.at[:, pl.ds(t * tile, tile)], weights.at[t], in_sems.at[t]
        )
        for t in range(HEAD_TILES)
    ]
    for c in loads:
        c.start()
    total = mine_ref[...] + other_ref[...].astype(F32)
    mean = (total / div_ref[:, :1]).astype(BF)
    combined = base_ref[...] + dot(mean, cross_out_ref[...])
    rows = norm(combined, gain_ref[...].reshape(1, D)).astype(BF)
    stores = [
        pltpu.make_async_copy(
            staged.at[t], out_ref.at[:, pl.ds(t * tile, tile)], out_sems.at[t]
        )
        for t in range(HEAD_TILES)
    ]
    for t in range(HEAD_TILES):
        loads[t].wait()
        staged[t] = dot(rows, weights[t]).astype(BF)
        stores[t].start()
    for c in stores:
        c.wait()


def moved(axis, shift):
    pairs = []
    for chip in range(64):
        c = (chip // STRIDES[axis]) % 4
        pairs.append((chip, chip + ((c + shift) % 4 - c) * STRIDES[axis]))
    return pairs


def from_offset(x, axis, offset):
    return lax.ppermute(x, "img", moved(axis, -offset))


def tied(values, others):
    values, _ = lax.optimization_barrier((values, others))
    return values


def exchange(blocks, phase, meanwhile=None):
    got = [[b[0], None, None, None] for b in blocks]

    def send(r, o, block):
        got[r][o] = from_offset(block, axes_of(r)[phase], o)

    for r, o in ((0, 2), (1, 2), (2, 1), (2, 3)):
        send(r, o, blocks[r][o])
    for r, early, late in ((0, (2,), (1, 3)), (1, (2,), (1, 3)), (2, (1, 3), (2,))):
        for o in late:
            waits = [got[r][e] for e in early] + ([] if meanwhile is None else [meanwhile])
            send(r, o, tied(blocks[r][o], waits) if phase else blocks[r][o])
    return got


def body(
    tokens, pair_list, pair_live, gain_self, gain_cross, gain_head,
    self_qkv, self_out, cross_qkv, cross_out, head_weight,
):
    chip = lax.axis_index("img")
    core = lax.axis_index("grp")
    flat_tokens = tokens.reshape(IMG * TOK, D)
    *rows, own_rows = call(
        norm_kernel,
        [sds(IMG * TOK, BLK)] * PARTS + [sds(IMG * TOK, D)],
        [VMEM] * 2,
        [VMEM] * (PARTS + 1),
    )(flat_tokens, gain_cross)
    blocks = [x.reshape(IMG, TOK, BLK) for x in rows]
    near = exchange([[blocks[r]] * 4 for r in range(PARTS)], 0)
    lines = [jnp.concatenate(near[r], axis=0) for r in range(PARTS)]

    ids = jnp.stack([chip, core]).astype(jnp.int32)
    first, second = pair_list[:, 0], pair_list[:, 1]
    square = [x.reshape(128, 128) for x in (first, second, pair_live)]
    flat = [x.reshape(16, 1024) for x in (first, second, pair_live)]
    lists, codes, offsets, divisor = call(
        plan_kernel,
        [
            sds(HELD, 16, dtype=jnp.int32),
            sds(8, 512, dtype=jnp.int32),
            sds(8, 128, dtype=jnp.int32),
            sds(IMG * TOK, 128, dtype=F32),
        ],
        [SMEM] + [VMEM] * 3,
        [VMEM] * 4,
        limit=24,
    )(ids, *tied(square, lines))
    held = exchange([[lines[r]] * 4 for r in range(PARTS)], 1, lists)
    longest = call(
        count_kernel,
        sds(8, 128, dtype=F32),
        [VMEM] * 3,
        VMEM,
        [pltpu.VMEM((128, 320), F32)],
    )(*tied(flat, [held[0][2], held[1][2], held[2][1]]))[0, 0]
    other_rows = lax.ppermute(own_rows, "grp", [(0, 1), (1, 0)])

    all_weight = lax.all_gather(head_weight, "grp", axis=1, tiled=True)

    def last_phase(cap, held, lists, codes, offsets, own, other, cross, tokens, gain, qkv, out_weight):
        arrived = []
        for r in range(PARTS):
            out = call(
                functools.partial(gather_kernel, cap, r),
                [sds(cap, TOK, BLK)] * 4,
                [SMEM] + [VMEM] * 4,
                [VMEM] * 4,
                [pltpu.VMEM((HELD, TOK, BLK), BF)],
                limit=16 if cap < HELD else 32,
            )(lists, *held[r])
            arrived.append(list(out))
        arrived = exchange(arrived, 2)
        folded = call(
            fold_kernel, sds(2 * IMG, HEADS * TOK, D), [VMEM] * 3, VMEM, limit=24
        )(own, other, cross)
        base = call(self_kernel, sds(IMG * TOK, D, dtype=F32), [VMEM] * 4, VMEM, limit=24)(
            tokens, gain, qkv, out_weight
        )
        mine_sum, other_sum = call(
            functools.partial(cross_kernel, cap),
            [sds(IMG * TOK, D, dtype=F32), sds(IMG * TOK, D)],
            [SMEM] * 2 + [VMEM] + [ANY] * 13,
            [VMEM] * 2,
            [
                pltpu.VMEM((PARTS, 4 * cap, TOK, BLK), BF),
                pltpu.VMEM((D, D), BF),
                pltpu.VMEM((WIDE, GROUP * TOK, D), BF),
                pltpu.VMEM((WIDE, HEADS * TOK, D), F32),
                pltpu.VMEM((2 * IMG, HEADS * TOK, D), BF),
                pltpu.SemaphoreType.DMA((4 * PARTS + 1,)),
            ],
            limit=44 if cap < HELD else 62,
        )(codes, offsets, folded, cross, *arrived[0], *arrived[1], *arrived[2])
        return mine_sum, other_sum, base

    mine_sum, other_sum, base = lax.cond(
        longest <= CAP,
        functools.partial(last_phase, CAP),
        functools.partial(last_phase, HELD),
        held, lists, codes, offsets, own_rows, other_rows, cross_qkv, flat_tokens, gain_self,
        self_qkv, self_out,
    )
    size = IMG * TOK
    other_sum = lax.ppermute(other_sum, "grp", [(0, 1), (1, 0)])
    outc = all_weight.shape[1]
    pixel_maps = call(
        head_kernel,
        sds(size, outc),
        [VMEM] * 6 + [ANY],
        ANY,
        [
            pltpu.VMEM((HEAD_TILES, D, outc // HEAD_TILES), BF),
            pltpu.VMEM((HEAD_TILES, size, outc // HEAD_TILES), BF),
            pltpu.SemaphoreType.DMA((HEAD_TILES,)),
            pltpu.SemaphoreType.DMA((HEAD_TILES,)),
        ],
        limit=32,
    )(mine_sum, other_sum, divisor, base, cross_out, gain_head, all_weight)
    return pixel_maps.reshape(IMG, TOK, -1)


def solution(mesh):
    placed = (P(("img", "grp"), None, None),) + (P(),) * 9 + (P(None, "grp"),)
    return jax.shard_map(
        body, mesh=mesh, in_specs=placed, out_specs=P(("img", "grp"), None, None), check_vma=False
    )
```

```python
import functools

import jax
import jax.numpy as jnp
from jax import lax
from jax.experimental import pallas as pl
from jax.experimental.pallas import tpu as pltpu
from jax.sharding import PartitionSpec as P

HEADS = 12
DH = 64
D = 768
TOK = 16
IMG = 16
HELD = 256
CAP = 88
BLK = 256
PARTS = 3
GROUP = 12
WIDE = 8
HEAD_TILES = 7
EPSILON = 1e-05
STRIDES = (16, 4, 1)
BF = jnp.bfloat16
F32 = jnp.float32
VMEM = pl.BlockSpec(memory_space=pltpu.VMEM)
ANY = pl.BlockSpec(memory_space=pl.ANY)
SMEM = pl.BlockSpec(memory_space=pltpu.SMEM)
MIB = 1024 * 1024


def axes_of(r):
    return r % 3, (r + 1) % 3, (r + 2) % 3


def dot(a, b, dims=((1,), (0,))):
    return lax.dot_general(a, b, (dims, ((), ())), preferred_element_type=F32)


def norm(values, gain):
    mean_val = jnp.mean(values, axis=-1, keepdims=True)
    centred = values - mean_val
    variance = jnp.mean(centred * centred, axis=-1, keepdims=True)
    return centred * lax.rsqrt(variance + EPSILON) * gain


def sds(*shape, dtype=BF):
    return jax.ShapeDtypeStruct(shape, dtype)


def call(kernel, outs, specs, out_specs, scratch=(), limit=16, flops=0, size=0):
    return pl.pallas_call(
        kernel,
        out_shape=outs,
        in_specs=specs,
        out_specs=out_specs,
        scratch_shapes=list(scratch),
        compiler_params=pltpu.CompilerParams(vmem_limit_bytes=limit * MIB),
        cost_estimate=pl.CostEstimate(flops=flops, bytes_accessed=size, transcendentals=0),
    )


def norm_kernel(tok_ref, gain_ref, *outs):
    rows = norm(tok_ref[...].astype(F32), gain_ref[...].reshape(1, D)).astype(BF)
    for r in range(PARTS):
        outs[r][...] = rows[:, r * BLK : (r + 1) * BLK]
    outs[PARTS][...] = rows


def self_kernel(tok_ref, gain_ref, qkv_ref, out_ref, base_ref):
    tok = tok_ref[...].astype(F32)
    rows = norm(tok, gain_ref[...].reshape(1, D)).astype(BF)
    proj = dot(rows, qkv_ref[...]).astype(BF)
    n = tok.shape[0]
    same = (lax.broadcasted_iota(jnp.int32, (n, n), 0) // TOK) == (
        lax.broadcasted_iota(jnp.int32, (n, n), 1) // TOK
    )
    total = tok
    mixed = []
    for h in range(HEADS):
        q = proj[:, h * DH : (h + 1) * DH]
        k = proj[:, D + h * DH : D + (h + 1) * DH]
        v = proj[:, 2 * D + h * DH : 2 * D + (h + 1) * DH]
        s = dot(q, k, ((1,), (1,))) * 0.125
        s = jnp.where(same, s, -1e30)
        e = jnp.exp(s - jnp.max(s, axis=1, keepdims=True))
        p = (e / jnp.sum(e, axis=1, keepdims=True)).astype(BF)
        mixed.append(dot(p, v).astype(BF))
    base_ref[...] = total + dot(jnp.concatenate(mixed, axis=1), out_ref[...])


def fold_kernel(own_ref, other_ref, qkv_ref, out_ref):
    rows = jnp.concatenate([own_ref[...], other_ref[...]], axis=0)
    q = (dot(rows, qkv_ref[:, :D]).astype(BF).astype(F32) * 0.125).astype(BF)
    images = rows.shape[0] // TOK
    for h in range(HEADS):
        keys = qkv_ref[:, D + h * DH : D + (h + 1) * DH]
        g = dot(q[:, h * DH : (h + 1) * DH], keys, ((1,), (1,)))
        out_ref[:, h * TOK : (h + 1) * TOK, :] = g.astype(BF).reshape(images, TOK, D)


def plan_kernel(
    ids_ref, first_ref, second_ref, live_ref, lists_ref, codes_ref, offs_ref, div_ref
):
    chip, core = ids_ref[0], ids_ref[1]
    own = jnp.concatenate([first_ref[...], second_ref[...]], axis=1)
    partner = jnp.concatenate([second_ref[...], first_ref[...]], axis=1)
    live = jnp.concatenate([live_ref[...]] * 2, axis=1)
    groups, sides = own.shape

    def iota(shape, axis):
        return lax.broadcasted_iota(jnp.int32, shape, axis)

    before = (iota((sides, sides), 0) < iota((sides, sides), 1)).astype(F32).astype(BF)
    usable = (live == 1) & (((partner >> 4) & 1) == core)
    owner = jnp.where(usable, own >> 4, -1)
    code = ((((((own >> 4) & 1) ^ core) * IMG + (own & 15)) << 11) + partner + 1).astype(F32)
    my = [(chip >> 4) & 3, (chip >> 2) & 3, chip & 3]
    steps = (16, 4, 1)
    lane = iota((groups, 128), 1)
    table = jnp.zeros((groups, 128), F32)
    for sel in range(1 + 3 * PARTS):
        target = chip
        if sel:
            r, o = (sel - 1) // 3, (sel - 1) % 3 + 1
            axis = axes_of(r)[2]
            target = chip + (((my[axis] - o) & 3) - my[axis]) * steps[axis]
        for dev in range(2):
            mine = owner == 2 * target + dev
            rank = dot(mine.astype(F32).astype(BF), before)
            for k in range(2):
                col = jnp.sum(jnp.where(mine & (rank == float(k)), code, 0.0), axis=1, keepdims=True)
                table = jnp.where(lane == sel * 4 + dev * 2 + k, col, table)
    table = table.astype(jnp.int32) - 1
    valid = table >= 0
    partners = table & 2047
    local = partners & 15
    sel = lane >> 2
    lane_r = jnp.where(sel > 6, 2, jnp.where(sel > 3, 1, 0))
    lane_o = jnp.where(sel > 0, sel - 3 * lane_r, 0)
    places, offsets = [], []
    for r in range(PARTS):
        offs = []
        for axis in axes_of(r):
            shift = 0
            for q in range(PARTS):
                if axes_of(q)[2] == axis:
                    shift = jnp.where((lane_r == q) & (sel > 0), lane_o, 0)
            here = (my[axis] - shift) & 3
            offs.append((((partners >> (5 + (4, 2, 0)[axis])) & 3) - here) & 3)
        places.append((offs[1] * 4 + offs[0]) * IMG + local)
        offsets.append(offs[2])
    ids = iota((groups, HELD), 1)

    def present(r, sel, o):
        spot = jnp.where(valid & (offsets[r] == o), places[r], -1)
        hits = jnp.zeros((groups, HELD), F32)
        for c in range(sel * 4, sel * 4 + 4):
            hits = jnp.where(spot[:, c : c + 1] == ids, 1.0, hits)
        return jnp.max(hits, axis=0, keepdims=True)

    pad = jnp.zeros((4, HELD), F32)
    sent = jnp.concatenate(
        [present(r, 1 + 3 * r + o - 1 if o else 0, o) for r in range(PARTS) for o in range(4)] + [pad],
        axis=0,
    )
    sent_rank = jnp.where(sent > 0.0, dot(sent.astype(BF), before), -1.0)
    spots = iota((HELD, HELD), 0).astype(F32)
    images = iota((HELD, HELD), 1).astype(F32)
    for c in range(4 * PARTS):
        col = jnp.sum(jnp.where(sent_rank[c : c + 1, :] == spots, images, 0.0), axis=1, keepdims=True)
        lists_ref[:, c : c + 1] = col.astype(jnp.int32)
    got = jnp.concatenate(
        [present(r, 0, o) for r in range(PARTS) for o in range(4)] + [pad], axis=0
    )
    got_rank = dot(got.astype(BF), before)
    key = jnp.where(valid, table >> 11, 127)
    small = iota((groups, 128), 1)
    earlier = (iota((groups, groups), 1) < iota((groups, groups), 0)).astype(F32).astype(BF)
    marks = [(key[:, c : c + 1] == small).astype(F32) for c in range(4)]
    starts = jnp.zeros((1, 128), F32)
    for c in range(4):
        starts = starts + jnp.sum((key[:, c : c + 1] < small).astype(F32), axis=0, keepdims=True)
    offs_ref[...] = jnp.broadcast_to(starts, (8, 128)).astype(jnp.int32)
    long_ids = iota((groups, 512), 1)
    ahead = starts
    ordered = [jnp.zeros((1, 512), F32) for _ in range(PARTS)]
    for c in range(4):
        pos = jnp.sum(marks[c] * (ahead + dot(earlier, marks[c].astype(BF))), axis=1, keepdims=True)
        ahead = ahead + jnp.sum(marks[c], axis=0, keepdims=True)
        pos = jnp.where(valid[:, c : c + 1], pos.astype(jnp.int32), -1)
        chosen = pos == long_ids
        for r in range(PARTS):
            slot = (offsets[r][:, c : c + 1] * HELD).astype(F32)
            for o in range(4):
                spot = jnp.where(valid & (offsets[r] == o), places[r], -1)[:, c : c + 1]
                row = got_rank[r * 4 + o : r * 4 + o + 1, :]
                slot = slot + jnp.sum(jnp.where(spot == ids, row, 0.0), axis=1, keepdims=True)
            ordered[r] = ordered[r] + jnp.sum(jnp.where(chosen, slot, 0.0), axis=0, keepdims=True)
    codes_ref[...] = jnp.concatenate(ordered + [jnp.zeros((5, 512), F32)], axis=0).astype(jnp.int32)
    named = jnp.where(live == 1, own, -1) - (2 * chip + core) * IMG
    for i in range(IMG):
        count = jnp.sum((named == i).astype(F32))
        div_ref[i * TOK : (i + 1) * TOK, :] = jnp.full((TOK, 128), jnp.maximum(count, 1.0), F32)


def count_kernel(first_ref, second_ref, live_ref, longest_ref, seen):
    chips, sources, fields = 64, 128, 4
    width = first_ref.shape[1]

    def iota(shape, axis):
        return lax.broadcasted_iota(jnp.int32, shape, axis)

    wide = iota((chips * fields, width), 0)
    source = iota((sources, width), 0)
    seen[...] = jnp.zeros_like(seen)

    def step(i, carry):
        one, two = first_ref[pl.ds(i, 1), :], second_ref[pl.ds(i, 1), :]
        live = live_ref[pl.ds(i, 1), :] == 1
        for own, partner in ((one, two), (two, one)):
            chip = jnp.where(live, own >> 5, -8)
            local = partner & 15
            weight = jnp.where(
                (local & 2) == 0,
                jnp.where((local & 1) == 0, 1.0, 64.0),
                jnp.where((local & 1) == 0, 4096.0, 262144.0),
            )
            left = jnp.where(chip * fields + (local >> 2) == wide, weight, 0.0).astype(BF)
            right = jnp.where((partner >> 4) == source, 1.0, 0.0).astype(BF)
            seen[...] += dot(right, left, ((1,), (1,)))
        return carry

    lax.fori_loop(0, first_ref.shape[0], step, 0)
    packed = seen[...].astype(jnp.int32)
    found = jnp.zeros(packed.shape, F32)
    digits = jnp.zeros(packed.shape, F32)
    for f in range(fields):
        digit = (packed >> (6 * f)) & 63
        found = found + jnp.where(digit > 0, 1.0, 0.0)
        digits = digits + digit.astype(F32)
    row, col = iota((128, sources), 0), iota((128, sources), 1)
    axis, coord = row >> 3, (row >> 1) & 3
    moved_by = jnp.where(axis == 0, 5, jnp.where(axis == 1, 3, 1))
    member = ((col & 1) == (row & 1)) & (((col >> moved_by) & 3) == coord) & (axis < 3)
    groups = dot(member.astype(F32).astype(BF), found.astype(BF))
    merge = (iota((chips * fields, 128), 0) >> 2) == iota((chips * fields, 128), 1)
    totals = dot(groups.astype(BF), merge.astype(F32).astype(BF))
    named = 2.0 * jnp.sum(live_ref[...].astype(F32))
    crowded = (jnp.max(seen[...]) >= 2.0**24) | (jnp.sum(digits) != named)
    longest_ref[...] = jnp.full(
        longest_ref.shape, jnp.where(crowded, 1000.0, jnp.max(totals)), F32
    )


def gather_kernel(cap, list_ref, *refs):
    held, outs = refs[: 4 * PARTS], refs[4 * PARTS : 8 * PARTS]
    buf, staged, in_sems, out_sems = refs[8 * PARTS :]
    size = HELD // 4
    loads = [
        pltpu.make_async_copy(held[n], buf.at[n // 4, pl.ds(n % 4 * size, size)], in_sems.at[n])
        for n in range(4 * PARTS)
    ]
    stores = [
        pltpu.make_async_copy(staged.at[n], outs[n], out_sems.at[n]) for n in range(4 * PARTS)
    ]
    for c in loads:
        c.start()
    for r in range(PARTS):
        for o in range(4):
            loads[r * 4 + o].wait()

        def step(s, carry, r=r):
            for o in range(4):
                staged[r * 4 + o, s] = buf[r, list_ref[s, r * 4 + o]]
            return carry

        lax.fori_loop(0, cap, step, 0, unroll=8)
        for o in range(4):
            stores[r * 4 + o].start()
    for c in stores:
        c.wait()


def cross_kernel(cap, code_ref, off_ref, g_ref, qkv_ref, *refs):
    parts = refs[: 4 * PARTS]
    mine_ref, other_ref, buf, wv, folded, xs, acc, mix, sems, g_sems = refs[4 * PARTS :]
    images = folded.shape[0]
    groups = images // WIDE
    copies = [
        pltpu.make_async_copy(
            parts[r * 4 + o], buf.at[r, pl.ds(o * cap, cap)], sems.at[r * 4 + o]
        )
        for r in range(PARTS)
        for o in range(4)
    ]
    loads = [
        pltpu.make_async_copy(
            g_ref.at[pl.ds(i * WIDE, WIDE)], folded.at[pl.ds(i * WIDE, WIDE)], g_sems.at[i]
        )
        for i in range(groups)
    ]
    value_load = pltpu.make_async_copy(qkv_ref.at[:, pl.ds(2 * D, D)], wv, sems.at[4 * PARTS])
    for c in copies + loads + [value_load]:
        c.start()
    for c in copies:
        c.wait()
    row_pair = lax.broadcasted_iota(jnp.int32, (GROUP * TOK, 1), 0) // TOK

    def attended(a, chunk, i):
        start = off_ref[0, a] + chunk * GROUP
        left = off_ref[0, a + 1] - start
        for j in range(GROUP):
            p = jnp.where(j < left, start + j, 0)
            for r in range(PARTS):
                code = code_ref[r, p]
                xs[i, j * TOK : (j + 1) * TOK, r * BLK : (r + 1) * BLK] = buf[
                    r, (code >> 8) * cap + jnp.minimum(code & 255, cap - 1)
                ]
        x = xs[i]
        s = dot(x, folded[a], ((1,), (1,))).reshape(GROUP, TOK, HEADS * TOK)
        e = jnp.exp(s - jnp.max(s, axis=1, keepdims=True))
        w = (e / jnp.sum(e, axis=1, keepdims=True)).reshape(GROUP * TOK, HEADS * TOK)
        w = jnp.where(row_pair < left, w, 0.0).astype(BF)
        return dot(w, x, ((0,), (0,)))

    def group(step, carry):
        for i in range(WIDE):
            mix[step * WIDE + i] = attended(step * WIDE + i, 0, i).astype(BF)
        return carry

    if cap < HELD:
        for step in range(groups):
            loads[step].wait()
            group(step, 0)
    else:
        for c in loads:
            c.wait()
        lax.fori_loop(0, groups, group, 0)

    def longer(a, carry):
        chunks = (off_ref[0, a + 1] - off_ref[0, a] + GROUP - 1) // GROUP

        @pl.when(chunks > 1)
        def _():
            acc[...] = jnp.zeros_like(acc)

            def more(c, carry):
                acc[...] += attended(a, c, 0)
                return carry

            lax.fori_loop(0, chunks, more, 0)
            mix[a] = acc[...].astype(BF)

        return carry

    lax.fori_loop(0, images, longer, 0)
    value_load.wait()
    for h in range(HEADS):
        u = mix[:, h * TOK : (h + 1) * TOK, :].reshape(images * TOK, D)
        o = dot(u, wv[:, h * DH : (h + 1) * DH])
        mine_ref[:, h * DH : (h + 1) * DH] = o[: IMG * TOK]
        other_ref[:, h * DH : (h + 1) * DH] = o[IMG * TOK :].astype(BF)


def head_kernel(
    mine_ref, other_ref, div_ref, base_ref, cross_out_ref, gain_ref, weight_ref,
    out_ref, weights, staged, in_sems, out_sems,
):
    tile = weight_ref.shape[1] // HEAD_TILES
    loads = [
        pltpu.make_async_copy(
            weight_ref.at[:, pl.ds(t * tile, tile)], weights.at[t], in_sems.at[t]
        )
        for t in range(HEAD_TILES)
    ]
    for c in loads:
        c.start()
    total = mine_ref[...] + other_ref[...].astype(F32)
    mean = (total / div_ref[:, :1]).astype(BF)
    combined = base_ref[...] + dot(mean, cross_out_ref[...])
    rows = norm(combined, gain_ref[...].reshape(1, D)).astype(BF)
    stores = [
        pltpu.make_async_copy(
            staged.at[t], out_ref.at[:, pl.ds(t * tile, tile)], out_sems.at[t]
        )
        for t in range(HEAD_TILES)
    ]
    for t in range(HEAD_TILES):
        loads[t].wait()
        staged[t] = dot(rows, weights[t]).astype(BF)
        stores[t].start()
    for c in stores:
        c.wait()


def moved(axis, shift):
    pairs = []
    for chip in range(64):
        c = (chip // STRIDES[axis]) % 4
        pairs.append((chip, chip + ((c + shift) % 4 - c) * STRIDES[axis]))
    return pairs


def from_offset(x, axis, offset):
    return lax.ppermute(x, "img", moved(axis, -offset))


def tied(values, others):
    values, _ = lax.optimization_barrier((values, others))
    return values


def exchange(blocks, phase, meanwhile=None):
    got = [[b[0], None, None, None] for b in blocks]

    def send(r, o, block):
        got[r][o] = from_offset(block, axes_of(r)[phase], o)

    for r, o in ((0, 2), (1, 2), (2, 1), (2, 3)):
        send(r, o, blocks[r][o])
    for r, early, late in ((0, (2,), (1, 3)), (1, (2,), (1, 3)), (2, (1, 3), (2,))):
        for o in late:
            waits = [got[r][e] for e in early] + ([] if meanwhile is None else [meanwhile])
            send(r, o, tied(blocks[r][o], waits) if phase else blocks[r][o])
    return got


def body(
    tokens, pair_list, pair_live, gain_self, gain_cross, gain_head,
    self_qkv, self_out, cross_qkv, cross_out, head_weight,
):
    chip = lax.axis_index("img")
    core = lax.axis_index("grp")
    flat_tokens = tokens.reshape(IMG * TOK, D)
    *rows, own_rows = call(
        norm_kernel,
        [sds(IMG * TOK, BLK)] * PARTS + [sds(IMG * TOK, D)],
        [VMEM] * 2,
        [VMEM] * (PARTS + 1),
    )(flat_tokens, gain_cross)
    blocks = [x.reshape(IMG, TOK, BLK) for x in rows]
    near = exchange([[blocks[r]] * 4 for r in range(PARTS)], 0)
    lines = [jnp.concatenate(near[r], axis=0) for r in range(PARTS)]

    ids = jnp.stack([chip, core]).astype(jnp.int32)
    first, second = pair_list[:, 0], pair_list[:, 1]
    square = [x.reshape(128, 128) for x in (first, second, pair_live)]
    flat = [x.reshape(16, 1024) for x in (first, second, pair_live)]
    lists, codes, offsets, divisor = call(
        plan_kernel,
        [
            sds(HELD, 16, dtype=jnp.int32),
            sds(8, 512, dtype=jnp.int32),
            sds(8, 128, dtype=jnp.int32),
            sds(IMG * TOK, 128, dtype=F32),
        ],
        [SMEM] + [VMEM] * 3,
        [VMEM] * 4,
        limit=24,
    )(ids, *tied(square, lines))
    held = exchange([[lines[r]] * 4 for r in range(PARTS)], 1, lists)
    other_rows = lax.ppermute(own_rows, "grp", [(0, 1), (1, 0)])
    all_weight = lax.all_gather(head_weight, "grp", axis=1, tiled=True)

    def gathered(cap, lists, held):
        out = call(
            functools.partial(gather_kernel, cap),
            [sds(cap, TOK, BLK)] * (4 * PARTS),
            [SMEM] + [ANY] * (4 * PARTS),
            [ANY] * (4 * PARTS),
            [
                pltpu.VMEM((PARTS, HELD, TOK, BLK), BF),
                pltpu.VMEM((4 * PARTS, cap, TOK, BLK), BF),
                pltpu.SemaphoreType.DMA((4 * PARTS,)),
                pltpu.SemaphoreType.DMA((4 * PARTS,)),
            ],
            limit=24 if cap < HELD else 44,
        )(lists, *[x for row in held for x in row])
        return [list(out[r * 4 : r * 4 + 4]) for r in range(PARTS)]

    def crossed(cap, codes, offsets, folded, cross, arrived):
        return call(
            functools.partial(cross_kernel, cap),
            [sds(IMG * TOK, D, dtype=F32), sds(IMG * TOK, D)],
            [SMEM] * 2 + [ANY] * (2 + 4 * PARTS),
            [VMEM] * 2,
            [
                pltpu.VMEM((PARTS, 4 * cap, TOK, BLK), BF),
                pltpu.VMEM((D, D), BF),
                pltpu.VMEM((2 * IMG, HEADS * TOK, D), BF),
                pltpu.VMEM((WIDE, GROUP * TOK, D), BF),
                pltpu.VMEM((HEADS * TOK, D), F32),
                pltpu.VMEM((2 * IMG, HEADS * TOK, D), BF),
                pltpu.SemaphoreType.DMA((4 * PARTS + 1,)),
                pltpu.SemaphoreType.DMA((2 * IMG // WIDE,)),
            ],
            limit=44 if cap < HELD else 62,
        )(codes, offsets, folded, cross, *[x for row in arrived for x in row])

    chosen = gathered(CAP, tied(lists, other_rows), held)
    own_rows, other_rows, flat_tokens = tied(
        [own_rows, other_rows, flat_tokens], chosen[0][0]
    )
    folded = call(fold_kernel, sds(2 * IMG, HEADS * TOK, D), [VMEM] * 3, VMEM, limit=24)(
        own_rows, other_rows, cross_qkv
    )
    base = call(self_kernel, sds(IMG * TOK, D, dtype=F32), [VMEM] * 4, VMEM, limit=24)(
        flat_tokens, gain_self, self_qkv, self_out
    )
    arrived = exchange(chosen, 2, [folded, base])
    longest = call(
        count_kernel,
        sds(8, 128, dtype=F32),
        [VMEM] * 3,
        VMEM,
        [pltpu.VMEM((128, 256), F32)],
    )(*tied(flat, [arrived[0][2], arrived[1][2], arrived[2][1]]))[0, 0]
    sums = crossed(CAP, codes, offsets, folded, cross_qkv, arrived)

    def redo(state):
        again = exchange(gathered(HELD, lists, held), 2)
        return (jnp.zeros((), F32), *crossed(HELD, codes, offsets, folded, cross_qkv, again))

    _, mine_sum, other_sum = lax.while_loop(lambda state: state[0] > CAP, redo, (longest, *sums))
    size = IMG * TOK
    other_sum = lax.ppermute(other_sum, "grp", [(0, 1), (1, 0)])
    outc = all_weight.shape[1]
    pixel_maps = call(
        head_kernel,
        sds(size, outc),
        [VMEM] * 6 + [ANY],
        ANY,
        [
            pltpu.VMEM((HEAD_TILES, D, outc // HEAD_TILES), BF),
            pltpu.VMEM((HEAD_TILES, size, outc // HEAD_TILES), BF),
            pltpu.SemaphoreType.DMA((HEAD_TILES,)),
            pltpu.SemaphoreType.DMA((HEAD_TILES,)),
        ],
        limit=60,
    )(mine_sum, other_sum, divisor, base, cross_out, gain_head, all_weight)
    return pixel_maps.reshape(IMG, TOK, -1)


def solution(mesh):
    placed = (P(("img", "grp"), None, None),) + (P(),) * 9 + (P(None, "grp"),)
    return jax.shard_map(
        body, mesh=mesh, in_specs=placed, out_specs=P(("img", "grp"), None, None), check_vma=False
    )
```

```python
import functools

import jax
import jax.numpy as jnp
from jax import lax
from jax.experimental import pallas as pl
from jax.experimental.pallas import tpu as pltpu
from jax.sharding import PartitionSpec as P

HEADS = 12
DH = 64
D = 768
TOK = 16
IMG = 16
HELD = 256
CAP = 88
PARTS = 2
WIDTHS = (512, 256)
STARTS = (0, 512)
ORDERS = (((2, 0, 1), (0, 1, 2)), ((1, 2, 0), (1, 2, 0)))
GROUP = 12
WIDE = 8
HEAD_TILES = 7
EPSILON = 1e-05
STRIDES = (16, 4, 1)
BF = jnp.bfloat16
F32 = jnp.float32
VMEM = pl.BlockSpec(memory_space=pltpu.VMEM)
ANY = pl.BlockSpec(memory_space=pl.ANY)
SMEM = pl.BlockSpec(memory_space=pltpu.SMEM)
MIB = 1024 * 1024


def dot(a, b, dims=((1,), (0,))):
    return lax.dot_general(a, b, (dims, ((), ())), preferred_element_type=F32)


def norm(values, gain):
    mean_val = jnp.mean(values, axis=-1, keepdims=True)
    centred = values - mean_val
    variance = jnp.mean(centred * centred, axis=-1, keepdims=True)
    return centred * lax.rsqrt(variance + EPSILON) * gain


def sds(*shape, dtype=BF):
    return jax.ShapeDtypeStruct(shape, dtype)


def call(kernel, outs, specs, out_specs, scratch=(), limit=16, flops=0, size=0):
    return pl.pallas_call(
        kernel,
        out_shape=outs,
        in_specs=specs,
        out_specs=out_specs,
        scratch_shapes=list(scratch),
        compiler_params=pltpu.CompilerParams(vmem_limit_bytes=limit * MIB),
        cost_estimate=pl.CostEstimate(flops=flops, bytes_accessed=size, transcendentals=0),
    )


def norm_kernel(tok_ref, gain_ref, *outs):
    rows = norm(tok_ref[...].astype(F32), gain_ref[...].reshape(1, D)).astype(BF)
    for r in range(PARTS):
        outs[r][...] = rows[:, STARTS[r] : STARTS[r] + WIDTHS[r]]
    outs[PARTS][...] = rows


def join_kernel(*refs):
    outs = refs[4 * PARTS :]
    for r in range(PARTS):
        for o in range(4):
            outs[r][o * IMG : (o + 1) * IMG] = refs[r * 4 + o][...]


def self_kernel(tok_ref, gain_ref, qkv_ref, out_ref, base_ref):
    tok = tok_ref[...].astype(F32)
    rows = norm(tok, gain_ref[...].reshape(1, D)).astype(BF)
    proj = dot(rows, qkv_ref[...]).astype(BF)
    n = tok.shape[0]
    same = (lax.broadcasted_iota(jnp.int32, (n, n), 0) // TOK) == (
        lax.broadcasted_iota(jnp.int32, (n, n), 1) // TOK
    )
    total = tok
    mixed = []
    for h in range(HEADS):
        q = proj[:, h * DH : (h + 1) * DH]
        k = proj[:, D + h * DH : D + (h + 1) * DH]
        v = proj[:, 2 * D + h * DH : 2 * D + (h + 1) * DH]
        s = dot(q, k, ((1,), (1,))) * 0.125
        s = jnp.where(same, s, -1e30)
        e = jnp.exp(s - jnp.max(s, axis=1, keepdims=True))
        p = (e / jnp.sum(e, axis=1, keepdims=True)).astype(BF)
        mixed.append(dot(p, v).astype(BF))
    base_ref[...] = total + dot(jnp.concatenate(mixed, axis=1), out_ref[...])


def fold_kernel(own_ref, other_ref, qkv_ref, out_ref):
    rows = jnp.concatenate([own_ref[...], other_ref[...]], axis=0)
    q = (dot(rows, qkv_ref[:, :D]).astype(BF).astype(F32) * 0.125).astype(BF)
    images = rows.shape[0] // TOK
    for h in range(HEADS):
        keys = qkv_ref[:, D + h * DH : D + (h + 1) * DH]
        g = dot(q[:, h * DH : (h + 1) * DH], keys, ((1,), (1,)))
        out_ref[:, h * TOK : (h + 1) * TOK, :] = g.astype(BF).reshape(images, TOK, D)


def plan_kernel(
    ids_ref, first_ref, second_ref, live_ref, lists_ref, codes_ref, offs_ref, div_ref
):
    chip, core = ids_ref[0], ids_ref[1]
    own = jnp.concatenate([first_ref[...], second_ref[...]], axis=1)
    partner = jnp.concatenate([second_ref[...], first_ref[...]], axis=1)
    live = jnp.concatenate([live_ref[...]] * 2, axis=1)
    groups, sides = own.shape

    def iota(shape, axis):
        return lax.broadcasted_iota(jnp.int32, shape, axis)

    before = (iota((sides, sides), 0) < iota((sides, sides), 1)).astype(F32).astype(BF)
    usable = (live == 1) & (((partner >> 4) & 1) == core)
    owner = jnp.where(usable, own >> 4, -1)
    code = ((((((own >> 4) & 1) ^ core) * IMG + (own & 15)) << 11) + partner + 1).astype(F32)
    my = [(chip >> 4) & 3, (chip >> 2) & 3, chip & 3]

    def pick(r, phase, values):
        zero, one = values[ORDERS[r][0][phase]], values[ORDERS[r][1][phase]]
        return jnp.where(core == 0, zero, one)

    lane = iota((groups, 128), 1)
    table = jnp.zeros((groups, 128), F32)
    for sel in range(1 + 3 * PARTS):
        target = chip
        if sel:
            r, o = (sel - 1) // 3, (sel - 1) % 3 + 1
            at = pick(r, 2, my)
            target = chip + (((at - o) & 3) - at) * pick(r, 2, STRIDES)
        for dev in range(2):
            mine = owner == 2 * target + dev
            rank = dot(mine.astype(F32).astype(BF), before)
            for k in range(2):
                col = jnp.sum(jnp.where(mine & (rank == float(k)), code, 0.0), axis=1, keepdims=True)
                table = jnp.where(lane == sel * 4 + dev * 2 + k, col, table)
    table = table.astype(jnp.int32) - 1
    valid = table >= 0
    partners = table & 2047
    local = partners & 15
    sel = lane >> 2
    lane_r = jnp.where(sel > 3, 1, 0)
    lane_o = jnp.where(sel > 0, sel - 3 * lane_r, 0)
    places, offsets = [], []
    for r in range(PARTS):
        offs = []
        for phase in range(3):
            here = pick(r, phase, my)
            if phase == 2:
                here = here - jnp.where(lane_r == r, lane_o, 0)
            offs.append((((partners >> pick(r, phase, (9, 7, 5))) & 3) - here) & 3)
        places.append((offs[1] * 4 + offs[0]) * IMG + local)
        offsets.append(offs[2])
    ids = iota((groups, HELD), 1)

    def present(r, sel, o):
        spot = jnp.where(valid & (offsets[r] == o), places[r], -1)
        hits = jnp.zeros((groups, HELD), F32)
        for c in range(sel * 4, sel * 4 + 4):
            hits = jnp.where(spot[:, c : c + 1] == ids, 1.0, hits)
        return jnp.max(hits, axis=0, keepdims=True)

    sent = jnp.concatenate(
        [present(r, 1 + 3 * r + o - 1 if o else 0, o) for r in range(PARTS) for o in range(4)],
        axis=0,
    )
    sent_rank = jnp.where(sent > 0.0, dot(sent.astype(BF), before), -1.0)
    spots = iota((HELD, HELD), 0).astype(F32)
    images = iota((HELD, HELD), 1).astype(F32)
    for c in range(4 * PARTS):
        col = jnp.sum(jnp.where(sent_rank[c : c + 1, :] == spots, images, 0.0), axis=1, keepdims=True)
        lists_ref[:, c : c + 1] = col.astype(jnp.int32)
    got = jnp.concatenate(
        [present(r, 0, o) for r in range(PARTS) for o in range(4)], axis=0
    )
    got_rank = dot(got.astype(BF), before)
    key = jnp.where(valid, table >> 11, 127)
    small = iota((groups, 128), 1)
    earlier = (iota((groups, groups), 1) < iota((groups, groups), 0)).astype(F32).astype(BF)
    marks = [(key[:, c : c + 1] == small).astype(F32) for c in range(4)]
    starts = jnp.zeros((1, 128), F32)
    for c in range(4):
        starts = starts + jnp.sum((key[:, c : c + 1] < small).astype(F32), axis=0, keepdims=True)
    offs_ref[...] = jnp.broadcast_to(starts, (8, 128)).astype(jnp.int32)
    long_ids = iota((groups, 512), 1)
    ahead = starts
    ordered = [jnp.zeros((1, 512), F32) for _ in range(PARTS)]
    for c in range(4):
        pos = jnp.sum(marks[c] * (ahead + dot(earlier, marks[c].astype(BF))), axis=1, keepdims=True)
        ahead = ahead + jnp.sum(marks[c], axis=0, keepdims=True)
        pos = jnp.where(valid[:, c : c + 1], pos.astype(jnp.int32), -1)
        chosen = pos == long_ids
        for r in range(PARTS):
            slot = (offsets[r][:, c : c + 1] * HELD).astype(F32)
            for o in range(4):
                spot = jnp.where(valid & (offsets[r] == o), places[r], -1)[:, c : c + 1]
                row = got_rank[r * 4 + o : r * 4 + o + 1, :]
                slot = slot + jnp.sum(jnp.where(spot == ids, row, 0.0), axis=1, keepdims=True)
            ordered[r] = ordered[r] + jnp.sum(jnp.where(chosen, slot, 0.0), axis=0, keepdims=True)
    codes_ref[...] = jnp.concatenate(ordered + [jnp.zeros((8 - PARTS, 512), F32)], axis=0).astype(jnp.int32)
    named = jnp.where(live == 1, own, -1) - (2 * chip + core) * IMG
    for i in range(IMG):
        count = jnp.sum((named == i).astype(F32))
        div_ref[i * TOK : (i + 1) * TOK, :] = jnp.full((TOK, 128), jnp.maximum(count, 1.0), F32)


def count_kernel(first_ref, second_ref, live_ref, longest_ref, seen):
    chips, sources, fields = 64, 128, 4
    width = first_ref.shape[1]

    def iota(shape, axis):
        return lax.broadcasted_iota(jnp.int32, shape, axis)

    wide = iota((chips * fields, width), 0)
    source = iota((sources, width), 0)
    seen[...] = jnp.zeros_like(seen)

    def step(i, carry):
        one, two = first_ref[pl.ds(i, 1), :], second_ref[pl.ds(i, 1), :]
        live = live_ref[pl.ds(i, 1), :] == 1
        for own, partner in ((one, two), (two, one)):
            chip = jnp.where(live, own >> 5, -8)
            local = partner & 15
            weight = jnp.where(
                (local & 2) == 0,
                jnp.where((local & 1) == 0, 1.0, 64.0),
                jnp.where((local & 1) == 0, 4096.0, 262144.0),
            )
            left = jnp.where(chip * fields + (local >> 2) == wide, weight, 0.0).astype(BF)
            right = jnp.where((partner >> 4) == source, 1.0, 0.0).astype(BF)
            seen[...] += dot(right, left, ((1,), (1,)))
        return carry

    lax.fori_loop(0, first_ref.shape[0], step, 0)
    packed = seen[...].astype(jnp.int32)
    found = jnp.zeros(packed.shape, F32)
    digits = jnp.zeros(packed.shape, F32)
    for f in range(fields):
        digit = (packed >> (6 * f)) & 63
        found = found + jnp.where(digit > 0, 1.0, 0.0)
        digits = digits + digit.astype(F32)
    row, col = iota((128, sources), 0), iota((128, sources), 1)
    axis, coord = row >> 3, (row >> 1) & 3
    moved_by = jnp.where(axis == 0, 5, jnp.where(axis == 1, 3, 1))
    member = ((col & 1) == (row & 1)) & (((col >> moved_by) & 3) == coord) & (axis < 3)
    groups = dot(member.astype(F32).astype(BF), found.astype(BF))
    merge = (iota((chips * fields, 128), 0) >> 2) == iota((chips * fields, 128), 1)
    totals = dot(groups.astype(BF), merge.astype(F32).astype(BF))
    named = 2.0 * jnp.sum(live_ref[...].astype(F32))
    crowded = (jnp.max(seen[...]) >= 2.0**24) | (jnp.sum(digits) != named)
    longest_ref[...] = jnp.full(
        longest_ref.shape, jnp.where(crowded, 1000.0, jnp.max(totals)), F32
    )


def gather_kernel(cap, list_ref, *refs):
    held, outs = refs[: 4 * PARTS], refs[4 * PARTS : 8 * PARTS]
    bufs, staged = refs[8 * PARTS : 9 * PARTS], refs[9 * PARTS : 10 * PARTS]
    in_sems, out_sems = refs[10 * PARTS :]
    size = HELD // 4
    loads = [
        pltpu.make_async_copy(held[n], bufs[n // 4].at[pl.ds(n % 4 * size, size)], in_sems.at[n])
        for n in range(4 * PARTS)
    ]
    stores = [
        pltpu.make_async_copy(staged[n // 4].at[n % 4], outs[n], out_sems.at[n])
        for n in range(4 * PARTS)
    ]
    for c in loads:
        c.start()
    for r in range(PARTS):
        for o in range(4):
            loads[r * 4 + o].wait()

        def step(s, carry, r=r):
            for o in range(4):
                staged[r][o, s] = bufs[r][list_ref[s, r * 4 + o]]
            return carry

        lax.fori_loop(0, cap, step, 0, unroll=8)
        for o in range(4):
            stores[r * 4 + o].start()
    for c in stores:
        c.wait()


def cross_kernel(cap, code_ref, off_ref, g_ref, qkv_ref, *refs):
    parts = refs[: 4 * PARTS]
    mine_ref, other_ref = refs[4 * PARTS : 4 * PARTS + 2]
    bufs = refs[4 * PARTS + 2 : 5 * PARTS + 2]
    wv, folded, xs, acc, mix, sems, g_sems = refs[5 * PARTS + 2 :]
    images = folded.shape[0]
    groups = images // WIDE
    copies = [
        pltpu.make_async_copy(
            parts[r * 4 + o], bufs[r].at[pl.ds(o * cap, cap)], sems.at[r * 4 + o]
        )
        for r in range(PARTS)
        for o in range(4)
    ]
    loads = [
        pltpu.make_async_copy(
            g_ref.at[pl.ds(i * WIDE, WIDE)], folded.at[pl.ds(i * WIDE, WIDE)], g_sems.at[i]
        )
        for i in range(groups)
    ]
    value_load = pltpu.make_async_copy(qkv_ref.at[:, pl.ds(2 * D, D)], wv, sems.at[4 * PARTS])
    for c in copies + loads + [value_load]:
        c.start()
    for c in copies:
        c.wait()
    row_pair = lax.broadcasted_iota(jnp.int32, (GROUP * TOK, 1), 0) // TOK

    def attended(a, chunk, i):
        start = off_ref[0, a] + chunk * GROUP
        left = off_ref[0, a + 1] - start
        for j in range(GROUP):
            p = jnp.where(j < left, start + j, 0)
            for r in range(PARTS):
                code = code_ref[r, p]
                xs[i, j * TOK : (j + 1) * TOK, STARTS[r] : STARTS[r] + WIDTHS[r]] = bufs[r][
                    (code >> 8) * cap + jnp.minimum(code & 255, cap - 1)
                ]
        x = xs[i]
        s = dot(x, folded[a], ((1,), (1,))).reshape(GROUP, TOK, HEADS * TOK)
        e = jnp.exp(s - jnp.max(s, axis=1, keepdims=True))
        w = (e / jnp.sum(e, axis=1, keepdims=True)).reshape(GROUP * TOK, HEADS * TOK)
        w = jnp.where(row_pair < left, w, 0.0).astype(BF)
        return dot(w, x, ((0,), (0,)))

    def group(step, carry):
        for i in range(WIDE):
            mix[step * WIDE + i] = attended(step * WIDE + i, 0, i).astype(BF)
        return carry

    if cap < HELD:
        for step in range(groups):
            loads[step].wait()
            group(step, 0)
    else:
        for c in loads:
            c.wait()
        lax.fori_loop(0, groups, group, 0)

    def longer(a, carry):
        chunks = (off_ref[0, a + 1] - off_ref[0, a] + GROUP - 1) // GROUP

        @pl.when(chunks > 1)
        def _():
            acc[...] = jnp.zeros_like(acc)

            def more(c, carry):
                acc[...] += attended(a, c, 0)
                return carry

            lax.fori_loop(0, chunks, more, 0)
            mix[a] = acc[...].astype(BF)

        return carry

    lax.fori_loop(0, images, longer, 0)
    value_load.wait()
    for h in range(HEADS):
        u = mix[:, h * TOK : (h + 1) * TOK, :].reshape(images * TOK, D)
        o = dot(u, wv[:, h * DH : (h + 1) * DH])
        mine_ref[:, h * DH : (h + 1) * DH] = o[: IMG * TOK]
        other_ref[:, h * DH : (h + 1) * DH] = o[IMG * TOK :].astype(BF)


def head_kernel(
    mine_ref, other_ref, div_ref, base_ref, cross_out_ref, gain_ref, weight_ref,
    out_ref, weights, staged, in_sems, out_sems,
):
    tile = weight_ref.shape[1] // HEAD_TILES
    loads = [
        pltpu.make_async_copy(
            weight_ref.at[:, pl.ds(t * tile, tile)], weights.at[t], in_sems.at[t]
        )
        for t in range(HEAD_TILES)
    ]
    for c in loads:
        c.start()
    total = mine_ref[...] + other_ref[...].astype(F32)
    mean = (total / div_ref[:, :1]).astype(BF)
    combined = base_ref[...] + dot(mean, cross_out_ref[...])
    rows = norm(combined, gain_ref[...].reshape(1, D)).astype(BF)
    stores = [
        pltpu.make_async_copy(
            staged.at[t], out_ref.at[:, pl.ds(t * tile, tile)], out_sems.at[t]
        )
        for t in range(HEAD_TILES)
    ]
    for t in range(HEAD_TILES):
        loads[t].wait()
        staged[t] = dot(rows, weights[t]).astype(BF)
        stores[t].start()
    for c in stores:
        c.wait()


def from_offset(x, r, phase, offset):
    pairs = []
    for chip in range(64):
        for core in range(2):
            stride = STRIDES[ORDERS[r][core][phase]]
            c = (chip // stride) % 4
            to = chip + ((c - offset) % 4 - c) * stride
            pairs.append((2 * chip + core, 2 * to + core))
    return lax.ppermute(x, ("img", "grp"), pairs)


def tied(values, others):
    values, _ = lax.optimization_barrier((values, others))
    return values


def exchange(blocks, phase, meanwhile=None):
    got = [[b[0], None, None, None] for b in blocks]

    def send(r, o, block):
        got[r][o] = from_offset(block, r, phase, o)

    for r, o in ((0, 2), (1, 1), (1, 3)):
        send(r, o, blocks[r][o])
    for r, early, late in ((0, (2,), (1, 3)), (1, (1, 3), (2,))):
        for o in late:
            waits = [got[r][e] for e in early] + ([] if meanwhile is None else [meanwhile])
            send(r, o, tied(blocks[r][o], waits) if phase else blocks[r][o])
    return got


def body(
    tokens, pair_list, pair_live, gain_self, gain_cross, gain_head,
    self_qkv, self_out, cross_qkv, cross_out, head_weight,
):
    chip = lax.axis_index("img")
    core = lax.axis_index("grp")
    flat_tokens = tokens.reshape(IMG * TOK, D)
    *rows, own_rows = call(
        norm_kernel,
        [sds(IMG * TOK, w) for w in WIDTHS + (D,)],
        [VMEM] * 2,
        [VMEM] * (PARTS + 1),
    )(flat_tokens, gain_cross)
    blocks = [x.reshape(IMG, TOK, -1) for x in rows]
    near = exchange([[blocks[r]] * 4 for r in range(PARTS)], 0)
    other_rows = lax.ppermute(own_rows, "grp", [(0, 1), (1, 0)])
    near, other_rows = lax.optimization_barrier((near, other_rows))
    lines = call(
        join_kernel, [sds(4 * IMG, TOK, w) for w in WIDTHS], [VMEM] * (4 * PARTS), [VMEM] * PARTS
    )(*[x for row in near for x in row])

    ids = jnp.stack([chip, core]).astype(jnp.int32)
    first, second = pair_list[:, 0], pair_list[:, 1]
    square = [x.reshape(128, 128) for x in (first, second, pair_live)]
    flat = [x.reshape(16, 1024) for x in (first, second, pair_live)]
    lists, codes, offsets, divisor = call(
        plan_kernel,
        [
            sds(HELD, 4 * PARTS, dtype=jnp.int32),
            sds(8, 512, dtype=jnp.int32),
            sds(8, 128, dtype=jnp.int32),
            sds(IMG * TOK, 128, dtype=F32),
        ],
        [SMEM] + [VMEM] * 3,
        [VMEM] * 4,
        limit=24,
    )(ids, *tied(square, lines))
    held = exchange([[lines[r]] * 4 for r in range(PARTS)], 1, lists)
    all_weight = lax.all_gather(head_weight, "grp", axis=1, tiled=True)

    def gathered(cap, lists, held):
        out = call(
            functools.partial(gather_kernel, cap),
            [sds(cap, TOK, w) for w in WIDTHS for o in range(4)],
            [SMEM] + [ANY] * (4 * PARTS),
            [ANY] * (4 * PARTS),
            [
                *[pltpu.VMEM((HELD, TOK, w), BF) for w in WIDTHS],
                *[pltpu.VMEM((4, cap, TOK, w), BF) for w in WIDTHS],
                pltpu.SemaphoreType.DMA((4 * PARTS,)),
                pltpu.SemaphoreType.DMA((4 * PARTS,)),
            ],
            limit=60,
        )(lists, *[x for row in held for x in row])
        return [list(out[r * 4 : r * 4 + 4]) for r in range(PARTS)]

    def crossed(cap, codes, offsets, folded, cross, arrived):
        return call(
            functools.partial(cross_kernel, cap),
            [sds(IMG * TOK, D, dtype=F32), sds(IMG * TOK, D)],
            [SMEM] * 2 + [ANY] * (2 + 4 * PARTS),
            [VMEM] * 2,
            [
                *[pltpu.VMEM((4 * cap, TOK, w), BF) for w in WIDTHS],
                pltpu.VMEM((D, D), BF),
                pltpu.VMEM((2 * IMG, HEADS * TOK, D), BF),
                pltpu.VMEM((WIDE, GROUP * TOK, D), BF),
                pltpu.VMEM((HEADS * TOK, D), F32),
                pltpu.VMEM((2 * IMG, HEADS * TOK, D), BF),
                pltpu.SemaphoreType.DMA((4 * PARTS + 1,)),
                pltpu.SemaphoreType.DMA((2 * IMG // WIDE,)),
            ],
            limit=60,
        )(codes, offsets, folded, cross, *[x for row in arrived for x in row])

    chosen = gathered(CAP, lists, held)
    own_rows, other_rows, flat_tokens = tied(
        [own_rows, other_rows, flat_tokens], chosen[0][0]
    )
    folded = call(fold_kernel, sds(2 * IMG, HEADS * TOK, D), [VMEM] * 3, VMEM, limit=24)(
        own_rows, other_rows, cross_qkv
    )
    base = call(self_kernel, sds(IMG * TOK, D, dtype=F32), [VMEM] * 4, VMEM, limit=24)(
        flat_tokens, gain_self, self_qkv, self_out
    )
    arrived = exchange(chosen, 2, [folded, base])
    longest = call(
        count_kernel,
        sds(8, 128, dtype=F32),
        [VMEM] * 3,
        VMEM,
        [pltpu.VMEM((128, 256), F32)],
    )(*tied(flat, [arrived[0][2], arrived[1][1]]))[0, 0]
    sums = crossed(CAP, codes, offsets, folded, cross_qkv, arrived)

    def redo(state):
        again = exchange(gathered(HELD, lists, held), 2)
        return (jnp.zeros((), F32), *crossed(HELD, codes, offsets, folded, cross_qkv, again))

    _, mine_sum, other_sum = lax.while_loop(lambda state: state[0] > CAP, redo, (longest, *sums))
    size = IMG * TOK
    other_sum = lax.ppermute(other_sum, "grp", [(0, 1), (1, 0)])
    outc = all_weight.shape[1]
    pixel_maps = call(
        head_kernel,
        sds(size, outc),
        [VMEM] * 6 + [ANY],
        ANY,
        [
            pltpu.VMEM((HEAD_TILES, D, outc // HEAD_TILES), BF),
            pltpu.VMEM((HEAD_TILES, size, outc // HEAD_TILES), BF),
            pltpu.SemaphoreType.DMA((HEAD_TILES,)),
            pltpu.SemaphoreType.DMA((HEAD_TILES,)),
        ],
        limit=60,
    )(mine_sum, other_sum, divisor, base, cross_out, gain_head, all_weight)
    return pixel_maps.reshape(IMG, TOK, -1)


def solution(mesh):
    placed = (P(("img", "grp"), None, None),) + (P(),) * 9 + (P(None, "grp"),)
    return jax.shard_map(
        body, mesh=mesh, in_specs=placed, out_specs=P(("img", "grp"), None, None), check_vma=False
    )
```

```python
import functools

import jax
import jax.numpy as jnp
from jax import lax
from jax.experimental import pallas as pl
from jax.experimental.pallas import tpu as pltpu
from jax.sharding import PartitionSpec as P

HEADS = 12
DH = 64
D = 768
TOK = 16
IMG = 16
HELD = 256
CAP = 88
PARTS = 2
WIDTHS = (512, 256)
STARTS = (0, 512)
ORDERS = (((2, 0, 1), (0, 1, 2)), ((1, 2, 0), (1, 2, 0)))
GROUP = 12
WIDE = 8
HEAD_TILES = 7
EPSILON = 1e-05
STRIDES = (16, 4, 1)
BF = jnp.bfloat16
F32 = jnp.float32
VMEM = pl.BlockSpec(memory_space=pltpu.VMEM)
ANY = pl.BlockSpec(memory_space=pl.ANY)
SMEM = pl.BlockSpec(memory_space=pltpu.SMEM)
MIB = 1024 * 1024


def dot(a, b, dims=((1,), (0,))):
    return lax.dot_general(a, b, (dims, ((), ())), preferred_element_type=F32)


def norm(values, gain):
    mean_val = jnp.mean(values, axis=-1, keepdims=True)
    centred = values - mean_val
    variance = jnp.mean(centred * centred, axis=-1, keepdims=True)
    return centred * lax.rsqrt(variance + EPSILON) * gain


def sds(*shape, dtype=BF):
    return jax.ShapeDtypeStruct(shape, dtype)


def call(kernel, outs, specs, out_specs, scratch=(), limit=16, flops=0, size=0):
    return pl.pallas_call(
        kernel,
        out_shape=outs,
        in_specs=specs,
        out_specs=out_specs,
        scratch_shapes=list(scratch),
        compiler_params=pltpu.CompilerParams(vmem_limit_bytes=limit * MIB),
        cost_estimate=pl.CostEstimate(flops=flops, bytes_accessed=size, transcendentals=0),
    )


def norm_kernel(tok_ref, gain_ref, *outs):
    rows = norm(tok_ref[...].astype(F32), gain_ref[...].reshape(1, D)).astype(BF)
    for r in range(PARTS):
        outs[r][...] = rows[:, STARTS[r] : STARTS[r] + WIDTHS[r]]
    outs[PARTS][...] = rows


def join_kernel(*refs):
    outs = refs[4 * PARTS :]
    for r in range(PARTS):
        for o in range(4):
            outs[r][o * IMG : (o + 1) * IMG] = refs[r * 4 + o][...]


def self_kernel(tok_ref, gain_ref, qkv_ref, out_ref, base_ref):
    tok = tok_ref[...].astype(F32)
    rows = norm(tok, gain_ref[...].reshape(1, D)).astype(BF)
    proj = dot(rows, qkv_ref[...]).astype(BF)
    n = tok.shape[0]
    same = (lax.broadcasted_iota(jnp.int32, (n, n), 0) // TOK) == (
        lax.broadcasted_iota(jnp.int32, (n, n), 1) // TOK
    )
    total = tok
    mixed = []
    for h in range(HEADS):
        q = proj[:, h * DH : (h + 1) * DH]
        k = proj[:, D + h * DH : D + (h + 1) * DH]
        v = proj[:, 2 * D + h * DH : 2 * D + (h + 1) * DH]
        s = dot(q, k, ((1,), (1,))) * 0.125
        s = jnp.where(same, s, -1e30)
        e = jnp.exp(s - jnp.max(s, axis=1, keepdims=True))
        p = (e / jnp.sum(e, axis=1, keepdims=True)).astype(BF)
        mixed.append(dot(p, v).astype(BF))
    base_ref[...] = total + dot(jnp.concatenate(mixed, axis=1), out_ref[...])


def fold_kernel(own_ref, other_ref, qkv_ref, out_ref):
    rows = jnp.concatenate([own_ref[...], other_ref[...]], axis=0)
    q = (dot(rows, qkv_ref[:, :D]).astype(BF).astype(F32) * 0.125).astype(BF)
    images = rows.shape[0] // TOK
    for h in range(HEADS):
        keys = qkv_ref[:, D + h * DH : D + (h + 1) * DH]
        g = dot(q[:, h * DH : (h + 1) * DH], keys, ((1,), (1,)))
        out_ref[:, h * TOK : (h + 1) * TOK, :] = g.astype(BF).reshape(images, TOK, D)


def plan_kernel(
    ids_ref, first_ref, second_ref, live_ref, lists_ref, codes_ref, offs_ref, div_ref
):
    chip, core = ids_ref[0], ids_ref[1]
    own = jnp.concatenate([first_ref[...], second_ref[...]], axis=1)
    partner = jnp.concatenate([second_ref[...], first_ref[...]], axis=1)
    live = jnp.concatenate([live_ref[...]] * 2, axis=1)
    groups, sides = own.shape

    def iota(shape, axis):
        return lax.broadcasted_iota(jnp.int32, shape, axis)

    before = (iota((sides, sides), 0) < iota((sides, sides), 1)).astype(F32).astype(BF)
    usable = (live == 1) & (((partner >> 4) & 1) == core)
    owner = jnp.where(usable, own >> 4, -1)
    code = ((((((own >> 4) & 1) ^ core) * IMG + (own & 15)) << 11) + partner + 1).astype(F32)
    my = [(chip >> 4) & 3, (chip >> 2) & 3, chip & 3]

    def pick(r, phase, values):
        zero, one = values[ORDERS[r][0][phase]], values[ORDERS[r][1][phase]]
        return jnp.where(core == 0, zero, one)

    lane = iota((groups, 128), 1)
    table = jnp.zeros((groups, 128), F32)
    for sel in range(1 + 3 * PARTS):
        target = chip
        if sel:
            r, o = (sel - 1) // 3, (sel - 1) % 3 + 1
            at = pick(r, 2, my)
            target = chip + (((at - o) & 3) - at) * pick(r, 2, STRIDES)
        for dev in range(2):
            mine = owner == 2 * target + dev
            rank = dot(mine.astype(F32).astype(BF), before)
            for k in range(2):
                col = jnp.sum(jnp.where(mine & (rank == float(k)), code, 0.0), axis=1, keepdims=True)
                table = jnp.where(lane == sel * 4 + dev * 2 + k, col, table)
    table = table.astype(jnp.int32) - 1
    valid = table >= 0
    partners = table & 2047
    local = partners & 15
    sel = lane >> 2
    lane_r = jnp.where(sel > 3, 1, 0)
    lane_o = jnp.where(sel > 0, sel - 3 * lane_r, 0)
    places, offsets = [], []
    for r in range(PARTS):
        offs = []
        for phase in range(3):
            here = pick(r, phase, my)
            if phase == 2:
                here = here - jnp.where(lane_r == r, lane_o, 0)
            offs.append((((partners >> pick(r, phase, (9, 7, 5))) & 3) - here) & 3)
        places.append((offs[1] * 4 + offs[0]) * IMG + local)
        offsets.append(offs[2])
    ids = iota((groups, HELD), 1)

    def present(r, sel, o):
        spot = jnp.where(valid & (offsets[r] == o), places[r], -1)
        hits = jnp.zeros((groups, HELD), F32)
        for c in range(sel * 4, sel * 4 + 4):
            hits = jnp.where(spot[:, c : c + 1] == ids, 1.0, hits)
        return jnp.max(hits, axis=0, keepdims=True)

    sent = jnp.concatenate(
        [present(r, 1 + 3 * r + o - 1 if o else 0, o) for r in range(PARTS) for o in range(4)],
        axis=0,
    )
    sent_rank = jnp.where(sent > 0.0, dot(sent.astype(BF), before), -1.0)
    spots = iota((HELD, HELD), 0).astype(F32)
    images = iota((HELD, HELD), 1).astype(F32)
    for c in range(4 * PARTS):
        col = jnp.sum(jnp.where(sent_rank[c : c + 1, :] == spots, images, 0.0), axis=1, keepdims=True)
        lists_ref[:, c : c + 1] = col.astype(jnp.int32)
    got = jnp.concatenate(
        [present(r, 0, o) for r in range(PARTS) for o in range(4)], axis=0
    )
    got_rank = dot(got.astype(BF), before)
    key = jnp.where(valid, table >> 11, 127)
    small = iota((groups, 128), 1)
    earlier = (iota((groups, groups), 1) < iota((groups, groups), 0)).astype(F32).astype(BF)
    marks = [(key[:, c : c + 1] == small).astype(F32) for c in range(4)]
    starts = jnp.zeros((1, 128), F32)
    for c in range(4):
        starts = starts + jnp.sum((key[:, c : c + 1] < small).astype(F32), axis=0, keepdims=True)
    offs_ref[...] = jnp.broadcast_to(starts, (8, 128)).astype(jnp.int32)
    long_ids = iota((groups, 512), 1)
    ahead = starts
    ordered = [jnp.zeros((1, 512), F32) for _ in range(PARTS)]
    for c in range(4):
        pos = jnp.sum(marks[c] * (ahead + dot(earlier, marks[c].astype(BF))), axis=1, keepdims=True)
        ahead = ahead + jnp.sum(marks[c], axis=0, keepdims=True)
        pos = jnp.where(valid[:, c : c + 1], pos.astype(jnp.int32), -1)
        chosen = pos == long_ids
        for r in range(PARTS):
            slot = (offsets[r][:, c : c + 1] * HELD).astype(F32)
            for o in range(4):
                spot = jnp.where(valid & (offsets[r] == o), places[r], -1)[:, c : c + 1]
                row = got_rank[r * 4 + o : r * 4 + o + 1, :]
                slot = slot + jnp.sum(jnp.where(spot == ids, row, 0.0), axis=1, keepdims=True)
            ordered[r] = ordered[r] + jnp.sum(jnp.where(chosen, slot, 0.0), axis=0, keepdims=True)
    codes_ref[...] = jnp.concatenate(ordered + [jnp.zeros((8 - PARTS, 512), F32)], axis=0).astype(jnp.int32)
    named = jnp.where(live == 1, own, -1) - (2 * chip + core) * IMG
    for i in range(IMG):
        count = jnp.sum((named == i).astype(F32))
        div_ref[i * TOK : (i + 1) * TOK, :] = jnp.full((TOK, 128), jnp.maximum(count, 1.0), F32)


def count_kernel(first_ref, second_ref, live_ref, longest_ref, seen):
    chips, sources, fields = 64, 128, 4
    width = first_ref.shape[1]

    def iota(shape, axis):
        return lax.broadcasted_iota(jnp.int32, shape, axis)

    wide = iota((chips * fields, width), 0)
    source = iota((sources, width), 0)
    seen[...] = jnp.zeros_like(seen)

    def step(i, carry):
        one, two = first_ref[pl.ds(i, 1), :], second_ref[pl.ds(i, 1), :]
        live = live_ref[pl.ds(i, 1), :] == 1
        for own, partner in ((one, two), (two, one)):
            chip = jnp.where(live, own >> 5, -8)
            local = partner & 15
            weight = jnp.where(
                (local & 2) == 0,
                jnp.where((local & 1) == 0, 1.0, 64.0),
                jnp.where((local & 1) == 0, 4096.0, 262144.0),
            )
            left = jnp.where(chip * fields + (local >> 2) == wide, weight, 0.0).astype(BF)
            right = jnp.where((partner >> 4) == source, 1.0, 0.0).astype(BF)
            seen[...] += dot(right, left, ((1,), (1,)))
        return carry

    lax.fori_loop(0, first_ref.shape[0], step, 0)
    packed = seen[...].astype(jnp.int32)
    found = jnp.zeros(packed.shape, F32)
    digits = jnp.zeros(packed.shape, F32)
    for f in range(fields):
        digit = (packed >> (6 * f)) & 63
        found = found + jnp.where(digit > 0, 1.0, 0.0)
        digits = digits + digit.astype(F32)
    row, col = iota((128, sources), 0), iota((128, sources), 1)
    axis, coord = row >> 3, (row >> 1) & 3
    moved_by = jnp.where(axis == 0, 5, jnp.where(axis == 1, 3, 1))
    member = ((col & 1) == (row & 1)) & (((col >> moved_by) & 3) == coord) & (axis < 3)
    groups = dot(member.astype(F32).astype(BF), found.astype(BF))
    merge = (iota((chips * fields, 128), 0) >> 2) == iota((chips * fields, 128), 1)
    totals = dot(groups.astype(BF), merge.astype(F32).astype(BF))
    named = 2.0 * jnp.sum(live_ref[...].astype(F32))
    crowded = (jnp.max(seen[...]) >= 2.0**24) | (jnp.sum(digits) != named)
    longest_ref[...] = jnp.full(
        longest_ref.shape, jnp.where(crowded, 1000.0, jnp.max(totals)), F32
    )


def gather_kernel(cap, list_ref, *refs):
    held, outs = refs[: 4 * PARTS], refs[4 * PARTS : 8 * PARTS]
    bufs, staged = refs[8 * PARTS : 9 * PARTS], refs[9 * PARTS : 10 * PARTS]
    in_sems, out_sems = refs[10 * PARTS :]
    size = HELD // 4
    loads = [
        pltpu.make_async_copy(held[n], bufs[n // 4].at[pl.ds(n % 4 * size, size)], in_sems.at[n])
        for n in range(4 * PARTS)
    ]
    stores = [
        pltpu.make_async_copy(staged[n // 4].at[n % 4], outs[n], out_sems.at[n])
        for n in range(4 * PARTS)
    ]
    for c in loads:
        c.start()
    for r in range(PARTS):
        for o in range(4):
            loads[r * 4 + o].wait()

        def step(s, carry, r=r):
            for o in range(4):
                staged[r][o, s] = bufs[r][list_ref[s, r * 4 + o]]
            return carry

        lax.fori_loop(0, cap, step, 0, unroll=8)
        for o in range(4):
            stores[r * 4 + o].start()
    for c in stores:
        c.wait()


def cross_kernel(cap, code_ref, off_ref, g_ref, qkv_ref, *refs):
    parts = refs[: 4 * PARTS]
    mine_ref, other_ref = refs[4 * PARTS : 4 * PARTS + 2]
    bufs = refs[4 * PARTS + 2 : 5 * PARTS + 2]
    wv, folded, xs, acc, mix, sems, g_sems = refs[5 * PARTS + 2 :]
    images = folded.shape[0]
    groups = images // WIDE
    copies = [
        pltpu.make_async_copy(
            parts[r * 4 + o], bufs[r].at[pl.ds(o * cap, cap)], sems.at[r * 4 + o]
        )
        for r in range(PARTS)
        for o in range(4)
    ]
    loads = [
        pltpu.make_async_copy(
            g_ref.at[pl.ds(i * WIDE, WIDE)], folded.at[pl.ds(i * WIDE, WIDE)], g_sems.at[i]
        )
        for i in range(groups)
    ]
    value_load = pltpu.make_async_copy(qkv_ref.at[:, pl.ds(2 * D, D)], wv, sems.at[4 * PARTS])
    for c in copies + loads + [value_load]:
        c.start()
    for c in copies:
        c.wait()
    row_pair = lax.broadcasted_iota(jnp.int32, (GROUP * TOK, 1), 0) // TOK

    def attended(a, chunk, i):
        start = off_ref[0, a] + chunk * GROUP
        left = off_ref[0, a + 1] - start
        for j in range(GROUP):
            p = jnp.where(j < left, start + j, 0)
            for r in range(PARTS):
                code = code_ref[r, p]
                xs[i, j * TOK : (j + 1) * TOK, STARTS[r] : STARTS[r] + WIDTHS[r]] = bufs[r][
                    (code >> 8) * cap + jnp.minimum(code & 255, cap - 1)
                ]
        x = xs[i]
        s = dot(x, folded[a], ((1,), (1,))).reshape(GROUP, TOK, HEADS * TOK)
        e = jnp.exp(s - jnp.max(s, axis=1, keepdims=True))
        w = (e / jnp.sum(e, axis=1, keepdims=True)).reshape(GROUP * TOK, HEADS * TOK)
        w = jnp.where(row_pair < left, w, 0.0).astype(BF)
        return dot(w, x, ((0,), (0,)))

    def group(step, carry):
        for i in range(WIDE):
            mix[step * WIDE + i] = attended(step * WIDE + i, 0, i).astype(BF)
        return carry

    if cap < HELD:
        for step in range(groups):
            loads[step].wait()
            group(step, 0)
    else:
        for c in loads:
            c.wait()
        lax.fori_loop(0, groups, group, 0)

    def longer(a, carry):
        chunks = (off_ref[0, a + 1] - off_ref[0, a] + GROUP - 1) // GROUP

        @pl.when(chunks > 1)
        def _():
            acc[...] = jnp.zeros_like(acc)

            def more(c, carry):
                acc[...] += attended(a, c, 0)
                return carry

            lax.fori_loop(0, chunks, more, 0)
            mix[a] = acc[...].astype(BF)

        return carry

    lax.fori_loop(0, images, longer, 0)
    value_load.wait()
    for h in range(HEADS):
        u = mix[:, h * TOK : (h + 1) * TOK, :].reshape(images * TOK, D)
        o = dot(u, wv[:, h * DH : (h + 1) * DH])
        mine_ref[:, h * DH : (h + 1) * DH] = o[: IMG * TOK]
        other_ref[:, h * DH : (h + 1) * DH] = o[IMG * TOK :].astype(BF)


def head_kernel(
    mine_ref, other_ref, div_ref, base_ref, cross_out_ref, gain_ref, weight_ref,
    out_ref, weights, staged, in_sems, out_sems,
):
    tile = weight_ref.shape[1] // HEAD_TILES
    loads = [
        pltpu.make_async_copy(
            weight_ref.at[:, pl.ds(t * tile, tile)], weights.at[t], in_sems.at[t]
        )
        for t in range(HEAD_TILES)
    ]
    for c in loads:
        c.start()
    total = mine_ref[...] + other_ref[...].astype(F32)
    mean = (total / div_ref[:, :1]).astype(BF)
    combined = base_ref[...] + dot(mean, cross_out_ref[...])
    rows = norm(combined, gain_ref[...].reshape(1, D)).astype(BF)
    stores = [
        pltpu.make_async_copy(
            staged.at[t], out_ref.at[:, pl.ds(t * tile, tile)], out_sems.at[t]
        )
        for t in range(HEAD_TILES)
    ]
    for t in range(HEAD_TILES):
        loads[t].wait()
        staged[t] = dot(rows, weights[t]).astype(BF)
        stores[t].start()
    for c in stores:
        c.wait()


def from_offset(x, r, phase, offset):
    pairs = []
    for chip in range(64):
        for core in range(2):
            stride = STRIDES[ORDERS[r][core][phase]]
            c = (chip // stride) % 4
            to = chip + ((c - offset) % 4 - c) * stride
            pairs.append((2 * chip + core, 2 * to + core))
    return lax.ppermute(x, ("img", "grp"), pairs)


def tied(values, others):
    values, _ = lax.optimization_barrier((values, others))
    return values


def exchange(blocks, phase, meanwhile=None):
    got = [[b[0], None, None, None] for b in blocks]
    for r, o in ((1, 1), (1, 3), (0, 2), (0, 1), (0, 3)):
        got[r][o] = from_offset(blocks[r][o], r, phase, o)
    last = blocks[1][2]
    if phase:
        last = tied(last, [got[1][1], got[1][3]] + ([] if meanwhile is None else [meanwhile]))
    got[1][2] = from_offset(last, 1, phase, 2)
    return got


def body(
    tokens, pair_list, pair_live, gain_self, gain_cross, gain_head,
    self_qkv, self_out, cross_qkv, cross_out, head_weight,
):
    chip = lax.axis_index("img")
    core = lax.axis_index("grp")
    flat_tokens = tokens.reshape(IMG * TOK, D)

    def first_phase(flat_tokens):
        *rows, own_rows = call(
            norm_kernel,
            [sds(IMG * TOK, w) for w in WIDTHS + (D,)],
            [VMEM] * 2,
            [VMEM] * (PARTS + 1),
        )(flat_tokens, gain_cross)
        blocks = [x.reshape(IMG, TOK, -1) for x in rows]
        near = exchange([[blocks[r]] * 4 for r in range(PARTS)], 0)
        other_rows = lax.ppermute(own_rows, "grp", [(0, 1), (1, 0)])
        near, other_rows = lax.optimization_barrier((near, other_rows))
        lines = call(
            join_kernel,
            [sds(4 * IMG, TOK, w) for w in WIDTHS],
            [VMEM] * (4 * PARTS),
            [VMEM] * PARTS,
        )(*[x for row in near for x in row])
        return lines, own_rows, other_rows

    def second_phase(lines, meanwhile=None):
        return exchange([[lines[r]] * 4 for r in range(PARTS)], 1, meanwhile)

    lines, own_rows, other_rows = first_phase(flat_tokens)

    ids = jnp.stack([chip, core]).astype(jnp.int32)
    first, second = pair_list[:, 0], pair_list[:, 1]
    square = [x.reshape(128, 128) for x in (first, second, pair_live)]
    flat = [x.reshape(16, 1024) for x in (first, second, pair_live)]
    lists, codes, offsets, divisor = call(
        plan_kernel,
        [
            sds(HELD, 4 * PARTS, dtype=jnp.int32),
            sds(8, 512, dtype=jnp.int32),
            sds(8, 128, dtype=jnp.int32),
            sds(IMG * TOK, 128, dtype=F32),
        ],
        [SMEM] + [VMEM] * 3,
        [VMEM] * 4,
        limit=24,
    )(ids, *tied(square, lines))
    held = second_phase(lines, lists)
    all_weight = lax.all_gather(head_weight, "grp", axis=1, tiled=True)

    def gathered(cap, lists, held):
        out = call(
            functools.partial(gather_kernel, cap),
            [sds(cap, TOK, w) for w in WIDTHS for o in range(4)],
            [SMEM] + [ANY] * (4 * PARTS),
            [ANY] * (4 * PARTS),
            [
                *[pltpu.VMEM((HELD, TOK, w), BF) for w in WIDTHS],
                *[pltpu.VMEM((4, cap, TOK, w), BF) for w in WIDTHS],
                pltpu.SemaphoreType.DMA((4 * PARTS,)),
                pltpu.SemaphoreType.DMA((4 * PARTS,)),
            ],
            limit=20 if cap < HELD else 60,
        )(lists, *[x for row in held for x in row])
        return [list(out[r * 4 : r * 4 + 4]) for r in range(PARTS)]

    def crossed(cap, codes, offsets, folded, cross, arrived):
        return call(
            functools.partial(cross_kernel, cap),
            [sds(IMG * TOK, D, dtype=F32), sds(IMG * TOK, D)],
            [SMEM] * 2 + [ANY] * (2 + 4 * PARTS),
            [VMEM] * 2,
            [
                *[pltpu.VMEM((4 * cap, TOK, w), BF) for w in WIDTHS],
                pltpu.VMEM((D, D), BF),
                pltpu.VMEM((2 * IMG, HEADS * TOK, D), BF),
                pltpu.VMEM((WIDE, GROUP * TOK, D), BF),
                pltpu.VMEM((HEADS * TOK, D), F32),
                pltpu.VMEM((2 * IMG, HEADS * TOK, D), BF),
                pltpu.SemaphoreType.DMA((4 * PARTS + 1,)),
                pltpu.SemaphoreType.DMA((2 * IMG // WIDE,)),
            ],
            limit=40 if cap < HELD else 60,
        )(codes, offsets, folded, cross, *[x for row in arrived for x in row])

    chosen = gathered(CAP, lists, held)
    own_rows, other_rows, late_tokens = tied(
        [own_rows, other_rows, flat_tokens], chosen[0][0]
    )
    def fold(own_rows, other_rows):
        return call(
            fold_kernel, sds(2 * IMG, HEADS * TOK, D), [VMEM] * 3, VMEM, limit=24
        )(own_rows, other_rows, cross_qkv)

    folded = fold(own_rows, other_rows)
    base = call(self_kernel, sds(IMG * TOK, D, dtype=F32), [VMEM] * 4, VMEM, limit=24)(
        late_tokens, gain_self, self_qkv, self_out
    )
    arrived = exchange(chosen, 2, [folded, base])
    longest = call(
        count_kernel,
        sds(8, 128, dtype=F32),
        [VMEM] * 3,
        VMEM,
        [pltpu.VMEM((128, 256), F32)],
    )(*tied(flat, [arrived[0][2], arrived[1][1]]))[0, 0]
    sums = crossed(CAP, codes, offsets, folded, cross_qkv, arrived)

    def redo(state):
        again, own, other = first_phase(tied(flat_tokens, state))
        again = exchange(gathered(HELD, lists, second_phase(again)), 2)
        return (
            jnp.zeros((), F32),
            *crossed(HELD, codes, offsets, fold(own, other), cross_qkv, again),
        )

    _, mine_sum, other_sum = lax.while_loop(lambda state: state[0] > CAP, redo, (longest, *sums))
    size = IMG * TOK
    other_sum = lax.ppermute(other_sum, "grp", [(0, 1), (1, 0)])
    outc = all_weight.shape[1]
    pixel_maps = call(
        head_kernel,
        sds(size, outc),
        [VMEM] * 6 + [ANY],
        ANY,
        [
            pltpu.VMEM((HEAD_TILES, D, outc // HEAD_TILES), BF),
            pltpu.VMEM((HEAD_TILES, size, outc // HEAD_TILES), BF),
            pltpu.SemaphoreType.DMA((HEAD_TILES,)),
            pltpu.SemaphoreType.DMA((HEAD_TILES,)),
        ],
        limit=60,
    )(mine_sum, other_sum, divisor, base, cross_out, gain_head, all_weight)
    return pixel_maps.reshape(IMG, TOK, -1)


def solution(mesh):
    placed = (P(("img", "grp"), None, None),) + (P(),) * 9 + (P(None, "grp"),)
    return jax.shard_map(
        body, mesh=mesh, in_specs=placed, out_specs=P(("img", "grp"), None, None), check_vma=False
    )
```

```python
import functools

import jax
import jax.numpy as jnp
from jax import lax
from jax.experimental import pallas as pl
from jax.experimental.pallas import tpu as pltpu
from jax.sharding import PartitionSpec as P

HEADS = 12
DH = 64
D = 768
TOK = 16
IMG = 16
HELD = 256
CAP = 88
PARTS = 2
WIDTHS = (512, 256)
STARTS = (0, 512)
ORDERS = (((2, 0, 1), (0, 1, 2)), ((1, 2, 0), (1, 2, 0)))
GROUP = 12
WIDE = 8
HEAD_TILES = 7
EPSILON = 1e-05
STRIDES = (16, 4, 1)
BF = jnp.bfloat16
F32 = jnp.float32
VMEM = pl.BlockSpec(memory_space=pltpu.VMEM)
HBM = pl.BlockSpec(memory_space=pltpu.HBM)
SMEM = pl.BlockSpec(memory_space=pltpu.SMEM)
MIB = 1024 * 1024
FULL = 62


def dot(a, b, dims=((1,), (0,))):
    return lax.dot_general(a, b, (dims, ((), ())), preferred_element_type=F32)


def norm(values, gain):
    mean_val = jnp.mean(values, axis=-1, keepdims=True)
    centred = values - mean_val
    variance = jnp.mean(centred * centred, axis=-1, keepdims=True)
    return centred * lax.rsqrt(variance + EPSILON) * gain


def sds(*shape, dtype=BF):
    return jax.ShapeDtypeStruct(shape, dtype)


def call(kernel, outs, specs, out_specs, scratch=(), limit=16, flops=0, size=0):
    return pl.pallas_call(
        kernel,
        out_shape=outs,
        in_specs=specs,
        out_specs=out_specs,
        scratch_shapes=list(scratch),
        compiler_params=pltpu.CompilerParams(vmem_limit_bytes=limit * MIB),
        cost_estimate=pl.CostEstimate(flops=flops, bytes_accessed=size, transcendentals=0),
    )


def norm_kernel(tok_ref, gain_ref, *outs):
    rows = norm(tok_ref[...].astype(F32), gain_ref[...].reshape(1, D)).astype(BF)
    for r in range(PARTS):
        outs[r][...] = rows[:, STARTS[r] : STARTS[r] + WIDTHS[r]]
    outs[PARTS][...] = rows


def join_kernel(*refs):
    outs = refs[4 * PARTS :]
    for r in range(PARTS):
        for o in range(4):
            outs[r][o * IMG : (o + 1) * IMG] = refs[r * 4 + o][...]


def self_kernel(tok_ref, gain_ref, qkv_ref, out_ref, base_ref, staged, sem):
    tok = tok_ref[...].astype(F32)
    rows = norm(tok, gain_ref[...].reshape(1, D)).astype(BF)
    proj = dot(rows, qkv_ref[...]).astype(BF)
    n = tok.shape[0]
    same = (lax.broadcasted_iota(jnp.int32, (n, n), 0) // TOK) == (
        lax.broadcasted_iota(jnp.int32, (n, n), 1) // TOK
    )
    total = tok
    mixed = []
    for h in range(HEADS):
        q = proj[:, h * DH : (h + 1) * DH]
        k = proj[:, D + h * DH : D + (h + 1) * DH]
        v = proj[:, 2 * D + h * DH : 2 * D + (h + 1) * DH]
        s = dot(q, k, ((1,), (1,))) * 0.125
        s = jnp.where(same, s, -1e30)
        e = jnp.exp(s - jnp.max(s, axis=1, keepdims=True))
        p = (e / jnp.sum(e, axis=1, keepdims=True)).astype(BF)
        mixed.append(dot(p, v).astype(BF))
    staged[...] = total + dot(jnp.concatenate(mixed, axis=1), out_ref[...])
    copy = pltpu.make_async_copy(staged, base_ref, sem)
    copy.start()
    copy.wait()


def fold_kernel(own_ref, other_ref, qkv_ref, out_ref, staged, sem):
    rows = jnp.concatenate([own_ref[...], other_ref[...]], axis=0)
    q = (dot(rows, qkv_ref[:, :D]).astype(BF).astype(F32) * 0.125).astype(BF)
    images = rows.shape[0] // TOK
    for h in range(HEADS):
        keys = qkv_ref[:, D + h * DH : D + (h + 1) * DH]
        g = dot(q[:, h * DH : (h + 1) * DH], keys, ((1,), (1,)))
        staged[:, h * TOK : (h + 1) * TOK, :] = g.astype(BF).reshape(images, TOK, D)
    copy = pltpu.make_async_copy(staged, out_ref, sem)
    copy.start()
    copy.wait()


def plan_kernel(
    ids_ref, first_ref, second_ref, live_ref, lists_ref, codes_ref, offs_ref, div_ref
):
    chip, core = ids_ref[0], ids_ref[1]
    own = jnp.concatenate([first_ref[...], second_ref[...]], axis=1)
    partner = jnp.concatenate([second_ref[...], first_ref[...]], axis=1)
    live = jnp.concatenate([live_ref[...]] * 2, axis=1)
    groups, sides = own.shape

    def iota(shape, axis):
        return lax.broadcasted_iota(jnp.int32, shape, axis)

    before = (iota((sides, sides), 0) < iota((sides, sides), 1)).astype(F32).astype(BF)
    usable = (live == 1) & (((partner >> 4) & 1) == core)
    owner = jnp.where(usable, own >> 4, -1)
    code = ((((((own >> 4) & 1) ^ core) * IMG + (own & 15)) << 11) + partner + 1).astype(F32)
    my = [(chip >> 4) & 3, (chip >> 2) & 3, chip & 3]

    def pick(r, phase, values):
        zero, one = values[ORDERS[r][0][phase]], values[ORDERS[r][1][phase]]
        return jnp.where(core == 0, zero, one)

    lane = iota((groups, 128), 1)
    table = jnp.zeros((groups, 128), F32)
    for sel in range(1 + 3 * PARTS):
        target = chip
        if sel:
            r, o = (sel - 1) // 3, (sel - 1) % 3 + 1
            at = pick(r, 2, my)
            target = chip + (((at - o) & 3) - at) * pick(r, 2, STRIDES)
        for dev in range(2):
            mine = owner == 2 * target + dev
            rank = dot(mine.astype(F32).astype(BF), before)
            for k in range(2):
                col = jnp.sum(jnp.where(mine & (rank == float(k)), code, 0.0), axis=1, keepdims=True)
                table = jnp.where(lane == sel * 4 + dev * 2 + k, col, table)
    table = table.astype(jnp.int32) - 1
    valid = table >= 0
    partners = table & 2047
    local = partners & 15
    sel = lane >> 2
    lane_r = jnp.where(sel > 3, 1, 0)
    lane_o = jnp.where(sel > 0, sel - 3 * lane_r, 0)
    places, offsets = [], []
    for r in range(PARTS):
        offs = []
        for phase in range(3):
            here = pick(r, phase, my)
            if phase == 2:
                here = here - jnp.where(lane_r == r, lane_o, 0)
            offs.append((((partners >> pick(r, phase, (9, 7, 5))) & 3) - here) & 3)
        places.append((offs[1] * 4 + offs[0]) * IMG + local)
        offsets.append(offs[2])
    ids = iota((groups, HELD), 1)

    def present(r, sel, o):
        spot = jnp.where(valid & (offsets[r] == o), places[r], -1)
        hits = jnp.zeros((groups, HELD), F32)
        for c in range(sel * 4, sel * 4 + 4):
            hits = jnp.where(spot[:, c : c + 1] == ids, 1.0, hits)
        return jnp.max(hits, axis=0, keepdims=True)

    sent = jnp.concatenate(
        [present(r, 1 + 3 * r + o - 1 if o else 0, o) for r in range(PARTS) for o in range(4)],
        axis=0,
    )
    sent_rank = jnp.where(sent > 0.0, dot(sent.astype(BF), before), -1.0)
    spots = iota((HELD, HELD), 0).astype(F32)
    images = iota((HELD, HELD), 1).astype(F32)
    for c in range(4 * PARTS):
        col = jnp.sum(jnp.where(sent_rank[c : c + 1, :] == spots, images, 0.0), axis=1, keepdims=True)
        lists_ref[:, c : c + 1] = col.astype(jnp.int32)
    got = jnp.concatenate(
        [present(r, 0, o) for r in range(PARTS) for o in range(4)], axis=0
    )
    got_rank = dot(got.astype(BF), before)
    key = jnp.where(valid, table >> 11, 127)
    small = iota((groups, 128), 1)
    earlier = (iota((groups, groups), 1) < iota((groups, groups), 0)).astype(F32).astype(BF)
    marks = [(key[:, c : c + 1] == small).astype(F32) for c in range(4)]
    starts = jnp.zeros((1, 128), F32)
    for c in range(4):
        starts = starts + jnp.sum((key[:, c : c + 1] < small).astype(F32), axis=0, keepdims=True)
    offs_ref[...] = jnp.broadcast_to(starts, (8, 128)).astype(jnp.int32)
    long_ids = iota((groups, 512), 1)
    ahead = starts
    ordered = [jnp.zeros((1, 512), F32) for _ in range(PARTS)]
    for c in range(4):
        pos = jnp.sum(marks[c] * (ahead + dot(earlier, marks[c].astype(BF))), axis=1, keepdims=True)
        ahead = ahead + jnp.sum(marks[c], axis=0, keepdims=True)
        pos = jnp.where(valid[:, c : c + 1], pos.astype(jnp.int32), -1)
        chosen = pos == long_ids
        for r in range(PARTS):
            slot = (offsets[r][:, c : c + 1] * HELD).astype(F32)
            for o in range(4):
                spot = jnp.where(valid & (offsets[r] == o), places[r], -1)[:, c : c + 1]
                row = got_rank[r * 4 + o : r * 4 + o + 1, :]
                slot = slot + jnp.sum(jnp.where(spot == ids, row, 0.0), axis=1, keepdims=True)
            ordered[r] = ordered[r] + jnp.sum(jnp.where(chosen, slot, 0.0), axis=0, keepdims=True)
    codes_ref[...] = jnp.concatenate(ordered + [jnp.zeros((8 - PARTS, 512), F32)], axis=0).astype(jnp.int32)
    named = jnp.where(live == 1, own, -1) - (2 * chip + core) * IMG
    for i in range(IMG):
        count = jnp.sum((named == i).astype(F32))
        div_ref[i * TOK : (i + 1) * TOK, :] = jnp.full((TOK, 128), jnp.maximum(count, 1.0), F32)


def count_kernel(first_ref, second_ref, live_ref, longest_ref, seen):
    chips, sources, fields = 64, 128, 4
    width = first_ref.shape[1]

    def iota(shape, axis):
        return lax.broadcasted_iota(jnp.int32, shape, axis)

    wide = iota((chips * fields, width), 0)
    source = iota((sources, width), 0)
    seen[...] = jnp.zeros_like(seen)

    def step(i, carry):
        one, two = first_ref[pl.ds(i, 1), :], second_ref[pl.ds(i, 1), :]
        live = live_ref[pl.ds(i, 1), :] == 1
        for own, partner in ((one, two), (two, one)):
            chip = jnp.where(live, own >> 5, -8)
            local = partner & 15
            weight = jnp.where(
                (local & 2) == 0,
                jnp.where((local & 1) == 0, 1.0, 64.0),
                jnp.where((local & 1) == 0, 4096.0, 262144.0),
            )
            left = jnp.where(chip * fields + (local >> 2) == wide, weight, 0.0).astype(BF)
            right = jnp.where((partner >> 4) == source, 1.0, 0.0).astype(BF)
            seen[...] += dot(right, left, ((1,), (1,)))
        return carry

    lax.fori_loop(0, first_ref.shape[0], step, 0)
    packed = seen[...].astype(jnp.int32)
    found = jnp.zeros(packed.shape, F32)
    digits = jnp.zeros(packed.shape, F32)
    for f in range(fields):
        digit = (packed >> (6 * f)) & 63
        found = found + jnp.where(digit > 0, 1.0, 0.0)
        digits = digits + digit.astype(F32)
    row, col = iota((128, sources), 0), iota((128, sources), 1)
    axis, coord = row >> 3, (row >> 1) & 3
    moved_by = jnp.where(axis == 0, 5, jnp.where(axis == 1, 3, 1))
    member = ((col & 1) == (row & 1)) & (((col >> moved_by) & 3) == coord) & (axis < 3)
    groups = dot(member.astype(F32).astype(BF), found.astype(BF))
    merge = (iota((chips * fields, 128), 0) >> 2) == iota((chips * fields, 128), 1)
    totals = dot(groups.astype(BF), merge.astype(F32).astype(BF))
    named = 2.0 * jnp.sum(live_ref[...].astype(F32))
    crowded = (jnp.max(seen[...]) >= 2.0**24) | (jnp.sum(digits) != named)
    longest_ref[...] = jnp.full(
        longest_ref.shape, jnp.where(crowded, 1000.0, jnp.max(totals)), F32
    )


def gather_kernel(cap, list_ref, *refs):
    held, outs = refs[: 4 * PARTS], refs[4 * PARTS : 8 * PARTS]
    bufs, staged = refs[8 * PARTS : 9 * PARTS], refs[9 * PARTS : 10 * PARTS]
    in_sems, out_sems = refs[10 * PARTS :]
    size = HELD // 4
    loads = [
        pltpu.make_async_copy(held[n], bufs[n // 4].at[pl.ds(n % 4 * size, size)], in_sems.at[n])
        for n in range(4 * PARTS)
    ]
    stores = [
        pltpu.make_async_copy(staged[n // 4].at[n % 4], outs[n], out_sems.at[n])
        for n in range(4 * PARTS)
    ]
    for c in loads:
        c.start()
    for r in range(PARTS):
        for o in range(4):
            loads[r * 4 + o].wait()

        def step(s, carry, r=r):
            for o in range(4):
                staged[r][o, s] = bufs[r][list_ref[s, r * 4 + o]]
            return carry

        lax.fori_loop(0, cap, step, 0, unroll=8)
        for o in range(4):
            stores[r * 4 + o].start()
    for c in stores:
        c.wait()


def cross_kernel(cap, code_ref, off_ref, g_ref, qkv_ref, *refs):
    parts = refs[: 4 * PARTS]
    mine_ref, other_ref = refs[4 * PARTS : 4 * PARTS + 2]
    bufs = refs[4 * PARTS + 2 : 5 * PARTS + 2]
    wv, folded, xs, acc, mix, sems, g_sems = refs[5 * PARTS + 2 :]
    images = folded.shape[0]
    groups = images // WIDE
    copies = [
        pltpu.make_async_copy(
            parts[r * 4 + o], bufs[r].at[pl.ds(o * cap, cap)], sems.at[r * 4 + o]
        )
        for r in range(PARTS)
        for o in range(4)
    ]
    loads = [
        pltpu.make_async_copy(
            g_ref.at[pl.ds(i * WIDE, WIDE)], folded.at[pl.ds(i * WIDE, WIDE)], g_sems.at[i]
        )
        for i in range(groups)
    ]
    value_load = pltpu.make_async_copy(qkv_ref.at[:, pl.ds(2 * D, D)], wv, sems.at[4 * PARTS])
    for c in copies + loads + [value_load]:
        c.start()
    for c in copies:
        c.wait()
    row_pair = lax.broadcasted_iota(jnp.int32, (GROUP * TOK, 1), 0) // TOK

    def attended(a, chunk, i):
        start = off_ref[0, a] + chunk * GROUP
        left = off_ref[0, a + 1] - start
        for j in range(GROUP):
            p = jnp.where(j < left, start + j, 0)
            for r in range(PARTS):
                code = code_ref[r, p]
                xs[i, j * TOK : (j + 1) * TOK, STARTS[r] : STARTS[r] + WIDTHS[r]] = bufs[r][
                    (code >> 8) * cap + jnp.minimum(code & 255, cap - 1)
                ]
        x = xs[i]
        s = dot(x, folded[a], ((1,), (1,))).reshape(GROUP, TOK, HEADS * TOK)
        e = jnp.exp(s - jnp.max(s, axis=1, keepdims=True))
        w = (e / jnp.sum(e, axis=1, keepdims=True)).reshape(GROUP * TOK, HEADS * TOK)
        w = jnp.where(row_pair < left, w, 0.0).astype(BF)
        return dot(w, x, ((0,), (0,)))

    def group(step, carry):
        for i in range(WIDE):
            mix[step * WIDE + i] = attended(step * WIDE + i, 0, i).astype(BF)
        return carry

    if cap < HELD:
        for step in range(groups):
            loads[step].wait()
            group(step, 0)
    else:
        for c in loads:
            c.wait()
        lax.fori_loop(0, groups, group, 0)

    def longer(a, carry):
        chunks = (off_ref[0, a + 1] - off_ref[0, a] + GROUP - 1) // GROUP

        @pl.when(chunks > 1)
        def _():
            acc[...] = jnp.zeros_like(acc)

            def more(c, carry):
                acc[...] += attended(a, c, 0)
                return carry

            lax.fori_loop(0, chunks, more, 0)
            mix[a] = acc[...].astype(BF)

        return carry

    lax.fori_loop(0, images, longer, 0)
    value_load.wait()
    for h in range(HEADS):
        u = mix[:, h * TOK : (h + 1) * TOK, :].reshape(images * TOK, D)
        o = dot(u, wv[:, h * DH : (h + 1) * DH])
        mine_ref[:, h * DH : (h + 1) * DH] = o[: IMG * TOK]
        other_ref[:, h * DH : (h + 1) * DH] = o[IMG * TOK :].astype(BF)


def head_kernel(
    mine_ref, other_ref, div_ref, base_ref, cross_out_ref, gain_ref, weight_ref,
    out_ref, weights, staged, in_sems, out_sems,
):
    tile = weight_ref.shape[1] // HEAD_TILES
    loads = [
        pltpu.make_async_copy(
            weight_ref.at[:, pl.ds(t * tile, tile)], weights.at[t], in_sems.at[t]
        )
        for t in range(HEAD_TILES)
    ]
    for c in loads:
        c.start()
    total = mine_ref[...] + other_ref[...].astype(F32)
    mean = (total / div_ref[:, :1]).astype(BF)
    combined = base_ref[...] + dot(mean, cross_out_ref[...])
    rows = norm(combined, gain_ref[...].reshape(1, D)).astype(BF)
    stores = [
        pltpu.make_async_copy(
            staged.at[t], out_ref.at[:, pl.ds(t * tile, tile)], out_sems.at[t]
        )
        for t in range(HEAD_TILES)
    ]
    for t in range(HEAD_TILES):
        loads[t].wait()
        staged[t] = dot(rows, weights[t]).astype(BF)
        stores[t].start()
    for c in stores:
        c.wait()


def from_offset(x, r, phase, offset):
    pairs = []
    for chip in range(64):
        for core in range(2):
            stride = STRIDES[ORDERS[r][core][phase]]
            c = (chip // stride) % 4
            to = chip + ((c - offset) % 4 - c) * stride
            pairs.append((2 * chip + core, 2 * to + core))
    return lax.ppermute(x, ("img", "grp"), pairs)


def tied(values, others):
    values, _ = lax.optimization_barrier((values, others))
    return values


def exchange(blocks, phase, meanwhile=None):
    got = [[b[0], None, None, None] for b in blocks]

    def send(r, o, block):
        got[r][o] = from_offset(block, r, phase, o)

    for r, o in ((0, 2), (1, 1), (1, 3)):
        send(r, o, blocks[r][o])
    for r, early, late in ((0, (2,), (1, 3)), (1, (1, 3), (2,))):
        for o in late:
            waits = [got[r][e] for e in early] + ([] if meanwhile is None else [meanwhile])
            send(r, o, tied(blocks[r][o], waits) if phase else blocks[r][o])
    return got


def body(
    tokens, pair_list, pair_live, gain_self, gain_cross, gain_head,
    self_qkv, self_out, cross_qkv, cross_out, head_weight,
):
    chip = lax.axis_index("img")
    core = lax.axis_index("grp")
    flat_tokens = tokens.reshape(IMG * TOK, D)
    *rows, own_rows = call(
        norm_kernel,
        [sds(IMG * TOK, w) for w in WIDTHS + (D,)],
        [VMEM] * 2,
        [VMEM] * (PARTS + 1),
    )(flat_tokens, gain_cross)
    blocks = [x.reshape(IMG, TOK, -1) for x in rows]
    near = exchange([[blocks[r]] * 4 for r in range(PARTS)], 0)
    other_rows = lax.ppermute(own_rows, "grp", [(0, 1), (1, 0)])
    near, other_rows = lax.optimization_barrier((near, other_rows))
    lines = call(
        join_kernel, [sds(4 * IMG, TOK, w) for w in WIDTHS], [VMEM] * (4 * PARTS), [VMEM] * PARTS
    )(*[x for row in near for x in row])

    ids = jnp.stack([chip, core]).astype(jnp.int32)
    first, second = pair_list[:, 0], pair_list[:, 1]
    square = [x.reshape(128, 128) for x in (first, second, pair_live)]
    flat = [x.reshape(16, 1024) for x in (first, second, pair_live)]
    lists, codes, offsets, divisor = call(
        plan_kernel,
        [
            sds(HELD, 4 * PARTS, dtype=jnp.int32),
            sds(8, 512, dtype=jnp.int32),
            sds(8, 128, dtype=jnp.int32),
            sds(IMG * TOK, 128, dtype=F32),
        ],
        [SMEM] + [VMEM] * 3,
        [VMEM] * 4,
        limit=FULL,
    )(ids, *tied(square, lines))
    held = exchange([[lines[r]] * 4 for r in range(PARTS)], 1, lists)
    late_tokens = tied(flat_tokens, [held[0][2], held[1][1]])
    base = call(
        self_kernel,
        sds(IMG * TOK, D, dtype=F32),
        [VMEM] * 4,
        HBM,
        [pltpu.VMEM((IMG * TOK, D), F32), pltpu.SemaphoreType.DMA],
        limit=FULL,
    )(late_tokens, gain_self, self_qkv, self_out)
    all_weight = lax.all_gather(head_weight, "grp", axis=1, tiled=True)

    def gathered(cap, lists, held):
        out = call(
            functools.partial(gather_kernel, cap),
            [sds(cap, TOK, w) for w in WIDTHS for o in range(4)],
            [SMEM] + [HBM] * (4 * PARTS),
            [HBM] * (4 * PARTS),
            [
                *[pltpu.VMEM((HELD, TOK, w), BF) for w in WIDTHS],
                *[pltpu.VMEM((4, cap, TOK, w), BF) for w in WIDTHS],
                pltpu.SemaphoreType.DMA((4 * PARTS,)),
                pltpu.SemaphoreType.DMA((4 * PARTS,)),
            ],
            limit=60,
        )(lists, *[x for row in held for x in row])
        return [list(out[r * 4 : r * 4 + 4]) for r in range(PARTS)]

    def crossed(cap, codes, offsets, folded, cross, arrived):
        return call(
            functools.partial(cross_kernel, cap),
            [sds(IMG * TOK, D, dtype=F32), sds(IMG * TOK, D)],
            [SMEM] * 2 + [HBM] * (2 + 4 * PARTS),
            [VMEM] * 2,
            [
                *[pltpu.VMEM((4 * cap, TOK, w), BF) for w in WIDTHS],
                pltpu.VMEM((D, D), BF),
                pltpu.VMEM((2 * IMG, HEADS * TOK, D), BF),
                pltpu.VMEM((WIDE, GROUP * TOK, D), BF),
                pltpu.VMEM((HEADS * TOK, D), F32),
                pltpu.VMEM((2 * IMG, HEADS * TOK, D), BF),
                pltpu.SemaphoreType.DMA((4 * PARTS + 1,)),
                pltpu.SemaphoreType.DMA((2 * IMG // WIDE,)),
            ],
            limit=60,
        )(codes, offsets, folded, cross, *[x for row in arrived for x in row])

    chosen = gathered(CAP, tied(lists, base), held)
    own_rows, other_rows = tied([own_rows, other_rows], chosen[0][0])
    folded = call(
        fold_kernel,
        sds(2 * IMG, HEADS * TOK, D),
        [VMEM] * 3,
        HBM,
        [pltpu.VMEM((2 * IMG, HEADS * TOK, D), BF), pltpu.SemaphoreType.DMA],
        limit=FULL,
    )(
        own_rows, other_rows, cross_qkv
    )
    arrived = exchange(chosen, 2, folded)
    longest = call(
        count_kernel,
        sds(8, 128, dtype=F32),
        [VMEM] * 3,
        VMEM,
        [pltpu.VMEM((128, 256), F32)],
        limit=FULL,
    )(*tied(flat, [arrived[0][2], arrived[1][1]]))[0, 0]
    sums = crossed(CAP, codes, offsets, folded, cross_qkv, arrived)

    def redo(state):
        again = exchange(gathered(HELD, lists, held), 2)
        return (jnp.zeros((), F32), *crossed(HELD, codes, offsets, folded, cross_qkv, again))

    _, mine_sum, other_sum = lax.while_loop(lambda state: state[0] > CAP, redo, (longest, *sums))
    size = IMG * TOK
    other_sum = lax.ppermute(other_sum, "grp", [(0, 1), (1, 0)])
    outc = all_weight.shape[1]
    pixel_maps = call(
        head_kernel,
        sds(size, outc),
        [VMEM] * 6 + [HBM],
        HBM,
        [
            pltpu.VMEM((HEAD_TILES, D, outc // HEAD_TILES), BF),
            pltpu.VMEM((HEAD_TILES, size, outc // HEAD_TILES), BF),
            pltpu.SemaphoreType.DMA((HEAD_TILES,)),
            pltpu.SemaphoreType.DMA((HEAD_TILES,)),
        ],
        limit=FULL,
    )(mine_sum, other_sum, divisor, base, cross_out, gain_head, all_weight)
    return pixel_maps.reshape(IMG, TOK, -1)


def solution(mesh):
    placed = (P(("img", "grp"), None, None),) + (P(),) * 9 + (P(None, "grp"),)
    return jax.shard_map(
        body, mesh=mesh, in_specs=placed, out_specs=P(("img", "grp"), None, None), check_vma=False
    )
```

```python
import functools

import jax
import jax.numpy as jnp
from jax import lax
from jax.experimental import pallas as pl
from jax.experimental.pallas import tpu as pltpu
from jax.sharding import PartitionSpec as P

HEADS = 12
DH = 64
D = 768
TOK = 16
IMG = 16
HELD = 256
CAP = 88
PARTS = 2
WIDTHS = (512, 256)
STARTS = (0, 512)
ORDERS = (((2, 0, 1), (0, 1, 2)), ((1, 2, 0), (1, 2, 0)))
GROUP = 12
WIDE = 8
HEAD_TILES = 7
EPSILON = 1e-05
STRIDES = (16, 4, 1)
BF = jnp.bfloat16
F32 = jnp.float32
VMEM = pl.BlockSpec(memory_space=pltpu.VMEM)
HBM = pl.BlockSpec(memory_space=pltpu.HBM)
SMEM = pl.BlockSpec(memory_space=pltpu.SMEM)
MIB = 1024 * 1024
FULL = 62
GATHER_MIB, CROSS_MIB, FOLD_MIB = 16, 40, 8


def dot(a, b, dims=((1,), (0,))):
    return lax.dot_general(a, b, (dims, ((), ())), preferred_element_type=F32)


def norm(values, gain):
    mean_val = jnp.mean(values, axis=-1, keepdims=True)
    centred = values - mean_val
    variance = jnp.mean(centred * centred, axis=-1, keepdims=True)
    return centred * lax.rsqrt(variance + EPSILON) * gain


def sds(*shape, dtype=BF):
    return jax.ShapeDtypeStruct(shape, dtype)


def call(kernel, outs, specs, out_specs, scratch=(), limit=4, flops=0, size=0):
    return pl.pallas_call(
        kernel,
        out_shape=outs,
        in_specs=specs,
        out_specs=out_specs,
        scratch_shapes=list(scratch),
        compiler_params=pltpu.CompilerParams(vmem_limit_bytes=limit * MIB),
        cost_estimate=pl.CostEstimate(flops=flops, bytes_accessed=size, transcendentals=0),
    )


def norm_kernel(tok_ref, gain_ref, *outs):
    rows = norm(tok_ref[...].astype(F32), gain_ref[...].reshape(1, D)).astype(BF)
    for r in range(PARTS):
        outs[r][...] = rows[:, STARTS[r] : STARTS[r] + WIDTHS[r]]
    outs[PARTS][...] = rows


def join_kernel(*refs):
    outs = refs[4 * PARTS :]
    for r in range(PARTS):
        for o in range(4):
            outs[r][o * IMG : (o + 1) * IMG] = refs[r * 4 + o][...]


def self_kernel(tok_ref, gain_ref, qkv_ref, out_ref, base_ref, staged, sem):
    tok = tok_ref[...].astype(F32)
    rows = norm(tok, gain_ref[...].reshape(1, D)).astype(BF)
    proj = dot(rows, qkv_ref[...]).astype(BF)
    n = tok.shape[0]
    same = (lax.broadcasted_iota(jnp.int32, (n, n), 0) // TOK) == (
        lax.broadcasted_iota(jnp.int32, (n, n), 1) // TOK
    )
    total = tok
    mixed = []
    for h in range(HEADS):
        q = proj[:, h * DH : (h + 1) * DH]
        k = proj[:, D + h * DH : D + (h + 1) * DH]
        v = proj[:, 2 * D + h * DH : 2 * D + (h + 1) * DH]
        s = dot(q, k, ((1,), (1,))) * 0.125
        s = jnp.where(same, s, -1e30)
        e = jnp.exp(s - jnp.max(s, axis=1, keepdims=True))
        p = (e / jnp.sum(e, axis=1, keepdims=True)).astype(BF)
        mixed.append(dot(p, v).astype(BF))
    staged[...] = total + dot(jnp.concatenate(mixed, axis=1), out_ref[...])
    copy = pltpu.make_async_copy(staged, base_ref, sem)
    copy.start()
    copy.wait()


def fold_kernel(own_ref, other_ref, qkv_ref, out_ref):
    rows = jnp.concatenate([own_ref[...], other_ref[...]], axis=0)
    q = (dot(rows, qkv_ref[:, :D]).astype(BF).astype(F32) * 0.125).astype(BF)
    images = rows.shape[0] // TOK
    for h in range(HEADS):
        keys = qkv_ref[:, D + h * DH : D + (h + 1) * DH]
        g = dot(q[:, h * DH : (h + 1) * DH], keys, ((1,), (1,)))
        out_ref[:, h * TOK : (h + 1) * TOK, :] = g.astype(BF).reshape(images, TOK, D)


def plan_kernel(
    ids_ref, first_ref, second_ref, live_ref, lists_ref, codes_ref, offs_ref, div_ref
):
    chip, core = ids_ref[0], ids_ref[1]
    own = jnp.concatenate([first_ref[...], second_ref[...]], axis=1)
    partner = jnp.concatenate([second_ref[...], first_ref[...]], axis=1)
    live = jnp.concatenate([live_ref[...]] * 2, axis=1)
    groups, sides = own.shape

    def iota(shape, axis):
        return lax.broadcasted_iota(jnp.int32, shape, axis)

    before = (iota((sides, sides), 0) < iota((sides, sides), 1)).astype(F32).astype(BF)
    usable = (live == 1) & (((partner >> 4) & 1) == core)
    owner = jnp.where(usable, own >> 4, -1)
    code = ((((((own >> 4) & 1) ^ core) * IMG + (own & 15)) << 11) + partner + 1).astype(F32)
    my = [(chip >> 4) & 3, (chip >> 2) & 3, chip & 3]

    def pick(r, phase, values):
        zero, one = values[ORDERS[r][0][phase]], values[ORDERS[r][1][phase]]
        return jnp.where(core == 0, zero, one)

    lane = iota((groups, 128), 1)
    table = jnp.zeros((groups, 128), F32)
    for sel in range(1 + 3 * PARTS):
        target = chip
        if sel:
            r, o = (sel - 1) // 3, (sel - 1) % 3 + 1
            at = pick(r, 2, my)
            target = chip + (((at - o) & 3) - at) * pick(r, 2, STRIDES)
        for dev in range(2):
            mine = owner == 2 * target + dev
            rank = dot(mine.astype(F32).astype(BF), before)
            for k in range(2):
                col = jnp.sum(jnp.where(mine & (rank == float(k)), code, 0.0), axis=1, keepdims=True)
                table = jnp.where(lane == sel * 4 + dev * 2 + k, col, table)
    table = table.astype(jnp.int32) - 1
    valid = table >= 0
    partners = table & 2047
    local = partners & 15
    sel = lane >> 2
    lane_r = jnp.where(sel > 3, 1, 0)
    lane_o = jnp.where(sel > 0, sel - 3 * lane_r, 0)
    places, offsets = [], []
    for r in range(PARTS):
        offs = []
        for phase in range(3):
            here = pick(r, phase, my)
            if phase == 2:
                here = here - jnp.where(lane_r == r, lane_o, 0)
            offs.append((((partners >> pick(r, phase, (9, 7, 5))) & 3) - here) & 3)
        places.append((offs[1] * 4 + offs[0]) * IMG + local)
        offsets.append(offs[2])
    ids = iota((groups, HELD), 1)

    def present(r, sel, o):
        spot = jnp.where(valid & (offsets[r] == o), places[r], -1)
        hits = jnp.zeros((groups, HELD), F32)
        for c in range(sel * 4, sel * 4 + 4):
            hits = jnp.where(spot[:, c : c + 1] == ids, 1.0, hits)
        return jnp.max(hits, axis=0, keepdims=True)

    sent = jnp.concatenate(
        [present(r, 1 + 3 * r + o - 1 if o else 0, o) for r in range(PARTS) for o in range(4)],
        axis=0,
    )
    sent_rank = jnp.where(sent > 0.0, dot(sent.astype(BF), before), -1.0)
    spots = iota((HELD, HELD), 0).astype(F32)
    images = iota((HELD, HELD), 1).astype(F32)
    for c in range(4 * PARTS):
        col = jnp.sum(jnp.where(sent_rank[c : c + 1, :] == spots, images, 0.0), axis=1, keepdims=True)
        lists_ref[:, c : c + 1] = col.astype(jnp.int32)
    got = jnp.concatenate(
        [present(r, 0, o) for r in range(PARTS) for o in range(4)], axis=0
    )
    got_rank = dot(got.astype(BF), before)
    key = jnp.where(valid, table >> 11, 127)
    small = iota((groups, 128), 1)
    earlier = (iota((groups, groups), 1) < iota((groups, groups), 0)).astype(F32).astype(BF)
    marks = [(key[:, c : c + 1] == small).astype(F32) for c in range(4)]
    starts = jnp.zeros((1, 128), F32)
    for c in range(4):
        starts = starts + jnp.sum((key[:, c : c + 1] < small).astype(F32), axis=0, keepdims=True)
    offs_ref[...] = jnp.broadcast_to(starts, (8, 128)).astype(jnp.int32)
    long_ids = iota((groups, 512), 1)
    ahead = starts
    ordered = [jnp.zeros((1, 512), F32) for _ in range(PARTS)]
    for c in range(4):
        pos = jnp.sum(marks[c] * (ahead + dot(earlier, marks[c].astype(BF))), axis=1, keepdims=True)
        ahead = ahead + jnp.sum(marks[c], axis=0, keepdims=True)
        pos = jnp.where(valid[:, c : c + 1], pos.astype(jnp.int32), -1)
        chosen = pos == long_ids
        for r in range(PARTS):
            slot = (offsets[r][:, c : c + 1] * HELD).astype(F32)
            for o in range(4):
                spot = jnp.where(valid & (offsets[r] == o), places[r], -1)[:, c : c + 1]
                row = got_rank[r * 4 + o : r * 4 + o + 1, :]
                slot = slot + jnp.sum(jnp.where(spot == ids, row, 0.0), axis=1, keepdims=True)
            ordered[r] = ordered[r] + jnp.sum(jnp.where(chosen, slot, 0.0), axis=0, keepdims=True)
    codes_ref[...] = jnp.concatenate(ordered + [jnp.zeros((8 - PARTS, 512), F32)], axis=0).astype(jnp.int32)
    named = jnp.where(live == 1, own, -1) - (2 * chip + core) * IMG
    for i in range(IMG):
        count = jnp.sum((named == i).astype(F32))
        div_ref[i * TOK : (i + 1) * TOK, :] = jnp.full((TOK, 128), jnp.maximum(count, 1.0), F32)


def count_kernel(first_ref, second_ref, live_ref, longest_ref, seen):
    chips, sources, fields = 64, 128, 4
    width = first_ref.shape[1]

    def iota(shape, axis):
        return lax.broadcasted_iota(jnp.int32, shape, axis)

    wide = iota((chips * fields, width), 0)
    source = iota((sources, width), 0)
    seen[...] = jnp.zeros_like(seen)

    def step(i, carry):
        one, two = first_ref[pl.ds(i, 1), :], second_ref[pl.ds(i, 1), :]
        live = live_ref[pl.ds(i, 1), :] == 1
        for own, partner in ((one, two), (two, one)):
            chip = jnp.where(live, own >> 5, -8)
            local = partner & 15
            weight = jnp.where(
                (local & 2) == 0,
                jnp.where((local & 1) == 0, 1.0, 64.0),
                jnp.where((local & 1) == 0, 4096.0, 262144.0),
            )
            left = jnp.where(chip * fields + (local >> 2) == wide, weight, 0.0).astype(BF)
            right = jnp.where((partner >> 4) == source, 1.0, 0.0).astype(BF)
            seen[...] += dot(right, left, ((1,), (1,)))
        return carry

    lax.fori_loop(0, first_ref.shape[0], step, 0)
    packed = seen[...].astype(jnp.int32)
    found = jnp.zeros(packed.shape, F32)
    digits = jnp.zeros(packed.shape, F32)
    for f in range(fields):
        digit = (packed >> (6 * f)) & 63
        found = found + jnp.where(digit > 0, 1.0, 0.0)
        digits = digits + digit.astype(F32)
    row, col = iota((128, sources), 0), iota((128, sources), 1)
    axis, coord = row >> 3, (row >> 1) & 3
    moved_by = jnp.where(axis == 0, 5, jnp.where(axis == 1, 3, 1))
    member = ((col & 1) == (row & 1)) & (((col >> moved_by) & 3) == coord) & (axis < 3)
    groups = dot(member.astype(F32).astype(BF), found.astype(BF))
    merge = (iota((chips * fields, 128), 0) >> 2) == iota((chips * fields, 128), 1)
    totals = dot(groups.astype(BF), merge.astype(F32).astype(BF))
    named = 2.0 * jnp.sum(live_ref[...].astype(F32))
    crowded = (jnp.max(seen[...]) >= 2.0**24) | (jnp.sum(digits) != named)
    longest_ref[...] = jnp.full(
        longest_ref.shape, jnp.where(crowded, 1000.0, jnp.max(totals)), F32
    )


def gather_kernel(cap, list_ref, *refs):
    held, outs, bufs = refs[: 4 * PARTS], refs[4 * PARTS : 8 * PARTS], refs[8 * PARTS :]
    size = HELD // 4

    def join(s, carry):
        for n in range(4 * PARTS):
            bufs[n // 4][n % 4 * size + s] = held[n][s]
        return carry

    def step(s, carry):
        for n in range(4 * PARTS):
            outs[n][s] = bufs[n // 4][list_ref[s, n]]
        return carry

    lax.fori_loop(0, size, join, 0, unroll=4)
    lax.fori_loop(0, cap, step, 0, unroll=4)


def gather_all_kernel(list_ref, *refs):
    held, outs = refs[: 4 * PARTS], refs[4 * PARTS : 8 * PARTS]
    bufs, staged = refs[8 * PARTS : 9 * PARTS], refs[9 * PARTS : 10 * PARTS]
    in_sems, out_sems = refs[10 * PARTS :]
    size = HELD // 4
    loads = [
        pltpu.make_async_copy(held[n], bufs[n // 4].at[pl.ds(n % 4 * size, size)], in_sems.at[n])
        for n in range(4 * PARTS)
    ]
    stores = [
        pltpu.make_async_copy(staged[n // 4].at[n % 4], outs[n], out_sems.at[n])
        for n in range(4 * PARTS)
    ]
    for c in loads:
        c.start()
    for c in loads:
        c.wait()

    def step(s, carry):
        for n in range(4 * PARTS):
            staged[n // 4][n % 4, s] = bufs[n // 4][list_ref[s, n]]
        return carry

    lax.fori_loop(0, HELD, step, 0)
    for c in stores:
        c.start()
    for c in stores:
        c.wait()


def cross_kernel(cap, code_ref, off_ref, g_ref, qkv_ref, *refs):
    parts = refs[: 4 * PARTS]
    mine_ref, other_ref = refs[4 * PARTS : 4 * PARTS + 2]
    bufs = refs[4 * PARTS + 2 : 5 * PARTS + 2]
    wv, folded, xs, acc, mix, sems, g_sems = refs[5 * PARTS + 2 :]
    images = mix.shape[0]
    groups = images // WIDE
    loads = [
        pltpu.make_async_copy(
            g_ref.at[pl.ds(i * WIDE, WIDE)], folded.at[pl.ds(i * WIDE, WIDE)], g_sems.at[i]
        )
        for i in range(groups)
    ]
    value_load = pltpu.make_async_copy(qkv_ref.at[:, pl.ds(2 * D, D)], wv, sems.at[4 * PARTS])
    for c in loads + [value_load]:
        c.start()
    if cap < HELD:

        def join(s, carry):
            for n in range(4 * PARTS):
                bufs[n // 4][n % 4 * cap + s] = parts[n][s]
            return carry

        lax.fori_loop(0, cap, join, 0, unroll=4)
    else:
        copies = [
            pltpu.make_async_copy(
                parts[n], bufs[n // 4].at[pl.ds(n % 4 * cap, cap)], sems.at[n]
            )
            for n in range(4 * PARTS)
        ]
        for c in copies:
            c.start()
        for c in copies:
            c.wait()
    row_pair = lax.broadcasted_iota(jnp.int32, (GROUP * TOK, 1), 0) // TOK

    def attended(a, chunk, i):
        start = off_ref[0, a] + chunk * GROUP
        left = off_ref[0, a + 1] - start
        for j in range(GROUP):
            p = jnp.where(j < left, start + j, 0)
            for r in range(PARTS):
                code = code_ref[r, p]
                xs[i, j * TOK : (j + 1) * TOK, STARTS[r] : STARTS[r] + WIDTHS[r]] = bufs[r][
                    (code >> 8) * cap + jnp.minimum(code & 255, cap - 1)
                ]
        x = xs[i]
        s = dot(x, folded[a], ((1,), (1,))).reshape(GROUP, TOK, HEADS * TOK)
        e = jnp.exp(s - jnp.max(s, axis=1, keepdims=True))
        w = (e / jnp.sum(e, axis=1, keepdims=True)).reshape(GROUP * TOK, HEADS * TOK)
        w = jnp.where(row_pair < left, w, 0.0).astype(BF)
        return dot(w, x, ((0,), (0,)))

    def group(step, carry):
        for i in range(WIDE):
            mix[step * WIDE + i] = attended(step * WIDE + i, 0, i).astype(BF)
        return carry

    if cap < HELD:
        for step in range(groups):
            loads[step].wait()
            group(step, 0)
    else:
        for c in loads:
            c.wait()
        lax.fori_loop(0, groups, group, 0)

    def longer(a, carry):
        chunks = (off_ref[0, a + 1] - off_ref[0, a] + GROUP - 1) // GROUP

        @pl.when(chunks > 1)
        def _():
            acc[...] = jnp.zeros_like(acc)

            def more(c, carry):
                acc[...] += attended(a, c, 0)
                return carry

            lax.fori_loop(0, chunks, more, 0)
            mix[a] = acc[...].astype(BF)

        return carry

    lax.fori_loop(0, images, longer, 0)
    value_load.wait()
    for h in range(HEADS):
        u = mix[:, h * TOK : (h + 1) * TOK, :].reshape(images * TOK, D)
        o = dot(u, wv[:, h * DH : (h + 1) * DH])
        mine_ref[:, h * DH : (h + 1) * DH] = o[: IMG * TOK]
        other_ref[:, h * DH : (h + 1) * DH] = o[IMG * TOK :].astype(BF)


def head_kernel(
    mine_ref, other_ref, div_ref, base_ref, cross_out_ref, gain_ref, weight_ref,
    out_ref, weights, staged, in_sems, out_sems,
):
    tile = weight_ref.shape[1] // HEAD_TILES
    loads = [
        pltpu.make_async_copy(
            weight_ref.at[:, pl.ds(t * tile, tile)], weights.at[t], in_sems.at[t]
        )
        for t in range(HEAD_TILES)
    ]
    for c in loads:
        c.start()
    total = mine_ref[...] + other_ref[...].astype(F32)
    mean = (total / div_ref[:, :1]).astype(BF)
    combined = base_ref[...] + dot(mean, cross_out_ref[...])
    rows = norm(combined, gain_ref[...].reshape(1, D)).astype(BF)
    stores = [
        pltpu.make_async_copy(
            staged.at[t], out_ref.at[:, pl.ds(t * tile, tile)], out_sems.at[t]
        )
        for t in range(HEAD_TILES)
    ]
    for t in range(HEAD_TILES):
        loads[t].wait()
        staged[t] = dot(rows, weights[t]).astype(BF)
        stores[t].start()
    for c in stores:
        c.wait()


def from_offset(x, r, phase, offset):
    pairs = []
    for chip in range(64):
        for core in range(2):
            stride = STRIDES[ORDERS[r][core][phase]]
            c = (chip // stride) % 4
            to = chip + ((c - offset) % 4 - c) * stride
            pairs.append((2 * chip + core, 2 * to + core))
    return lax.ppermute(x, ("img", "grp"), pairs)


def tied(values, others):
    values, _ = lax.optimization_barrier((values, others))
    return values


def exchange(blocks, phase, meanwhile=None):
    got = [[b[0], None, None, None] for b in blocks]

    def send(r, o, block):
        got[r][o] = from_offset(block, r, phase, o)

    for r, o in ((0, 2), (1, 1), (1, 3)):
        send(r, o, blocks[r][o])
    for r, early, late in ((0, (2,), (1, 3)), (1, (1, 3), (2,))):
        for o in late:
            waits = [got[r][e] for e in early] + ([] if meanwhile is None else [meanwhile])
            send(r, o, tied(blocks[r][o], waits) if phase else blocks[r][o])
    return got


def body(
    tokens, pair_list, pair_live, gain_self, gain_cross, gain_head,
    self_qkv, self_out, cross_qkv, cross_out, head_weight,
):
    chip = lax.axis_index("img")
    core = lax.axis_index("grp")
    flat_tokens = tokens.reshape(IMG * TOK, D)
    def first_phase(flat_tokens):
        *rows, own_rows = call(
            norm_kernel,
            [sds(IMG * TOK, w) for w in WIDTHS + (D,)],
            [VMEM] * 2,
            [VMEM] * (PARTS + 1),
        )(flat_tokens, gain_cross)
        blocks = [x.reshape(IMG, TOK, -1) for x in rows]
        near = exchange([[blocks[r]] * 4 for r in range(PARTS)], 0)
        other_rows = lax.ppermute(own_rows, "grp", [(0, 1), (1, 0)])
        near, other_rows = lax.optimization_barrier((near, other_rows))
        lines = call(
            join_kernel,
            [sds(4 * IMG, TOK, w) for w in WIDTHS],
            [VMEM] * (4 * PARTS),
            [VMEM] * PARTS,
        )(*[x for row in near for x in row])
        return lines, own_rows, other_rows

    def second_phase(lines, meanwhile=None):
        return exchange([[lines[r]] * 4 for r in range(PARTS)], 1, meanwhile)

    lines, own_rows, other_rows = first_phase(flat_tokens)

    ids = jnp.stack([chip, core]).astype(jnp.int32)
    first, second = pair_list[:, 0], pair_list[:, 1]
    square = [x.reshape(128, 128) for x in (first, second, pair_live)]
    flat = [x.reshape(16, 1024) for x in (first, second, pair_live)]
    lists, codes, offsets, divisor = call(
        plan_kernel,
        [
            sds(HELD, 4 * PARTS, dtype=jnp.int32),
            sds(8, 512, dtype=jnp.int32),
            sds(8, 128, dtype=jnp.int32),
            sds(IMG * TOK, 128, dtype=F32),
        ],
        [SMEM] + [VMEM] * 3,
        [VMEM] * 4,
        limit=6,
    )(ids, *tied(square, lines))
    held = second_phase(lines, lists)
    late_tokens = tied(flat_tokens, [held[0][2], held[1][1]])
    base = call(
        self_kernel,
        sds(IMG * TOK, D, dtype=F32),
        [VMEM] * 4,
        HBM,
        [pltpu.VMEM((IMG * TOK, D), F32), pltpu.SemaphoreType.DMA],
        limit=8,
    )(late_tokens, gain_self, self_qkv, self_out)
    all_weight = lax.all_gather(head_weight, "grp", axis=1, tiled=True)

    def gathered(cap, lists, held):
        shapes = [sds(cap, TOK, w) for w in WIDTHS for o in range(4)]
        bufs = [pltpu.VMEM((HELD, TOK, w), BF) for w in WIDTHS]
        place = [VMEM if cap < HELD else HBM] * (4 * PARTS)
        if cap < HELD:
            kernel, limit = functools.partial(gather_kernel, cap), GATHER_MIB
        else:
            kernel, limit = gather_all_kernel, FULL
            bufs += [pltpu.VMEM((4, cap, TOK, w), BF) for w in WIDTHS]
            bufs += [pltpu.SemaphoreType.DMA((4 * PARTS,))] * 2
        out = call(kernel, shapes, [SMEM] + place, place, bufs, limit)(
            lists, *[x for row in held for x in row]
        )
        return [list(out[r * 4 : r * 4 + 4]) for r in range(PARTS)]

    def crossed(cap, codes, offsets, folded, cross, arrived):
        small = cap < HELD
        scratch = [
            *[pltpu.VMEM((4 * cap, TOK, w), BF) for w in WIDTHS],
            pltpu.VMEM((D, D), BF),
            pltpu.VMEM((2 * IMG, HEADS * TOK, D), BF),
            pltpu.VMEM((WIDE, GROUP * TOK, D), BF),
            pltpu.VMEM((HEADS * TOK, D), F32),
            pltpu.VMEM((2 * IMG, HEADS * TOK, D), BF),
            pltpu.SemaphoreType.DMA((4 * PARTS + 1,)),
            pltpu.SemaphoreType.DMA((2 * IMG // WIDE,)),
        ]
        place = VMEM if small else HBM
        return call(
            functools.partial(cross_kernel, cap),
            [sds(IMG * TOK, D, dtype=F32), sds(IMG * TOK, D)],
            [SMEM] * 2 + [HBM] * 2 + [place] * (4 * PARTS),
            [VMEM] * 2,
            scratch,
            CROSS_MIB if small else FULL,
        )(codes, offsets, folded, cross, *[x for row in arrived for x in row])

    def fold(own_rows, other_rows):
        return call(
            fold_kernel, sds(2 * IMG, HEADS * TOK, D), [VMEM] * 3, VMEM, limit=FOLD_MIB
        )(own_rows, other_rows, cross_qkv)

    chosen = gathered(CAP, tied(lists, base), held)
    own_rows, other_rows = tied([own_rows, other_rows], chosen[0][0])
    folded = fold(own_rows, other_rows)
    arrived = exchange(chosen, 2, folded)
    longest = call(
        count_kernel,
        sds(8, 128, dtype=F32),
        [VMEM] * 3,
        VMEM,
        [pltpu.VMEM((128, 256), F32)],
        limit=6,
    )(*tied(flat, [arrived[0][2], arrived[1][1]]))[0, 0]
    sums = crossed(CAP, codes, offsets, folded, cross_qkv, arrived)

    def redo(state):
        again, own, other = first_phase(tied(flat_tokens, state))
        again = exchange(gathered(HELD, lists, second_phase(again)), 2)
        return (
            jnp.zeros((), F32),
            *crossed(HELD, codes, offsets, fold(own, other), cross_qkv, again),
        )

    _, mine_sum, other_sum = lax.while_loop(lambda state: state[0] > CAP, redo, (longest, *sums))
    size = IMG * TOK
    other_sum = lax.ppermute(other_sum, "grp", [(0, 1), (1, 0)])
    outc = all_weight.shape[1]
    pixel_maps = call(
        head_kernel,
        sds(size, outc),
        [VMEM] * 6 + [HBM],
        HBM,
        [
            pltpu.VMEM((HEAD_TILES, D, outc // HEAD_TILES), BF),
            pltpu.VMEM((HEAD_TILES, size, outc // HEAD_TILES), BF),
            pltpu.SemaphoreType.DMA((HEAD_TILES,)),
            pltpu.SemaphoreType.DMA((HEAD_TILES,)),
        ],
        limit=FULL,
    )(mine_sum, other_sum, divisor, base, cross_out, gain_head, all_weight)
    return pixel_maps.reshape(IMG, TOK, -1)


def solution(mesh):
    placed = (P(("img", "grp"), None, None),) + (P(),) * 9 + (P(None, "grp"),)
    return jax.shard_map(
        body, mesh=mesh, in_specs=placed, out_specs=P(("img", "grp"), None, None), check_vma=False
    )
```

```python
import functools

import jax
import jax.numpy as jnp
from jax import lax
from jax.experimental import pallas as pl
from jax.experimental.pallas import tpu as pltpu
from jax.sharding import PartitionSpec as P

HEADS = 12
DH = 64
D = 768
TOK = 16
IMG = 16
HELD = 256
CAP = 84
PARTS = 2
WIDTHS = (512, 256)
STARTS = (0, 512)
ORDERS = (((2, 0, 1), (0, 1, 2)), ((1, 2, 0), (1, 2, 0)))
GROUP = 12
WIDE = 8
HEAD_TILES = 7
EPSILON = 1e-05
STRIDES = (16, 4, 1)
BF = jnp.bfloat16
F32 = jnp.float32
VMEM = pl.BlockSpec(memory_space=pltpu.VMEM)
HBM = pl.BlockSpec(memory_space=pltpu.HBM)
SMEM = pl.BlockSpec(memory_space=pltpu.SMEM)
MIB = 1024 * 1024
FULL = 62


def dot(a, b, dims=((1,), (0,))):
    return lax.dot_general(a, b, (dims, ((), ())), preferred_element_type=F32)


def norm(values, gain):
    mean_val = jnp.mean(values, axis=-1, keepdims=True)
    centred = values - mean_val
    variance = jnp.mean(centred * centred, axis=-1, keepdims=True)
    return centred * lax.rsqrt(variance + EPSILON) * gain


def sds(*shape, dtype=BF):
    return jax.ShapeDtypeStruct(shape, dtype)


def call(kernel, outs, specs, out_specs, scratch=(), limit=16, flops=0, size=0):
    return pl.pallas_call(
        kernel,
        out_shape=outs,
        in_specs=specs,
        out_specs=out_specs,
        scratch_shapes=list(scratch),
        compiler_params=pltpu.CompilerParams(vmem_limit_bytes=limit * MIB),
        cost_estimate=pl.CostEstimate(flops=flops, bytes_accessed=size, transcendentals=0),
    )


def norm_kernel(tok_ref, gain_ref, *outs):
    rows = norm(tok_ref[...].astype(F32), gain_ref[...].reshape(1, D)).astype(BF)
    for r in range(PARTS):
        outs[r][...] = rows[:, STARTS[r] : STARTS[r] + WIDTHS[r]]
    outs[PARTS][...] = rows


def join_kernel(*refs):
    outs = refs[4 * PARTS :]
    for r in range(PARTS):
        for o in range(4):
            outs[r][o * IMG : (o + 1) * IMG] = refs[r * 4 + o][...]


def self_kernel(tok_ref, gain_ref, qkv_ref, out_ref, base_ref, staged, sem):
    tok = tok_ref[...].astype(F32)
    rows = norm(tok, gain_ref[...].reshape(1, D)).astype(BF)
    proj = dot(rows, qkv_ref[...]).astype(BF)
    n = tok.shape[0]
    same = (lax.broadcasted_iota(jnp.int32, (n, n), 0) // TOK) == (
        lax.broadcasted_iota(jnp.int32, (n, n), 1) // TOK
    )
    total = tok
    mixed = []
    for h in range(HEADS):
        q = proj[:, h * DH : (h + 1) * DH]
        k = proj[:, D + h * DH : D + (h + 1) * DH]
        v = proj[:, 2 * D + h * DH : 2 * D + (h + 1) * DH]
        s = dot(q, k, ((1,), (1,))) * 0.125
        s = jnp.where(same, s, -1e30)
        e = jnp.exp(s - jnp.max(s, axis=1, keepdims=True))
        p = (e / jnp.sum(e, axis=1, keepdims=True)).astype(BF)
        mixed.append(dot(p, v).astype(BF))
    staged[...] = total + dot(jnp.concatenate(mixed, axis=1), out_ref[...])
    copy = pltpu.make_async_copy(staged, base_ref, sem)
    copy.start()
    copy.wait()


def fold_kernel(own_ref, other_ref, qkv_ref, out_ref, staged, sem):
    rows = jnp.concatenate([own_ref[...], other_ref[...]], axis=0)
    q = (dot(rows, qkv_ref[:, :D]).astype(BF).astype(F32) * 0.125).astype(BF)
    images = rows.shape[0] // TOK
    for h in range(HEADS):
        keys = qkv_ref[:, D + h * DH : D + (h + 1) * DH]
        g = dot(q[:, h * DH : (h + 1) * DH], keys, ((1,), (1,)))
        staged[:, h * TOK : (h + 1) * TOK, :] = g.astype(BF).reshape(images, TOK, D)
    copy = pltpu.make_async_copy(staged, out_ref, sem)
    copy.start()
    copy.wait()


def plan_kernel(
    ids_ref, first_ref, second_ref, live_ref, lists_ref, codes_ref, offs_ref, div_ref
):
    chip, core = ids_ref[0], ids_ref[1]
    own = jnp.concatenate([first_ref[...], second_ref[...]], axis=1)
    partner = jnp.concatenate([second_ref[...], first_ref[...]], axis=1)
    live = jnp.concatenate([live_ref[...]] * 2, axis=1)
    groups, sides = own.shape

    def iota(shape, axis):
        return lax.broadcasted_iota(jnp.int32, shape, axis)

    before = (iota((sides, sides), 0) < iota((sides, sides), 1)).astype(F32).astype(BF)
    usable = (live == 1) & (((partner >> 4) & 1) == core)
    owner = jnp.where(usable, own >> 4, -1)
    code = ((((((own >> 4) & 1) ^ core) * IMG + (own & 15)) << 11) + partner + 1).astype(F32)
    my = [(chip >> 4) & 3, (chip >> 2) & 3, chip & 3]

    def pick(r, phase, values):
        zero, one = values[ORDERS[r][0][phase]], values[ORDERS[r][1][phase]]
        return jnp.where(core == 0, zero, one)

    lane = iota((groups, 128), 1)
    table = jnp.zeros((groups, 128), F32)
    for sel in range(1 + 3 * PARTS):
        target = chip
        if sel:
            r, o = (sel - 1) // 3, (sel - 1) % 3 + 1
            at = pick(r, 2, my)
            target = chip + (((at - o) & 3) - at) * pick(r, 2, STRIDES)
        for dev in range(2):
            mine = owner == 2 * target + dev
            rank = dot(mine.astype(F32).astype(BF), before)
            for k in range(2):
                col = jnp.sum(jnp.where(mine & (rank == float(k)), code, 0.0), axis=1, keepdims=True)
                table = jnp.where(lane == sel * 4 + dev * 2 + k, col, table)
    table = table.astype(jnp.int32) - 1
    valid = table >= 0
    partners = table & 2047
    local = partners & 15
    sel = lane >> 2
    lane_r = jnp.where(sel > 3, 1, 0)
    lane_o = jnp.where(sel > 0, sel - 3 * lane_r, 0)
    places, offsets = [], []
    for r in range(PARTS):
        offs = []
        for phase in range(3):
            here = pick(r, phase, my)
            if phase == 2:
                here = here - jnp.where(lane_r == r, lane_o, 0)
            offs.append((((partners >> pick(r, phase, (9, 7, 5))) & 3) - here) & 3)
        places.append((offs[1] * 4 + offs[0]) * IMG + local)
        offsets.append(offs[2])
    ids = iota((groups, HELD), 1)

    def present(r, sel, o):
        spot = jnp.where(valid & (offsets[r] == o), places[r], -1)
        hits = jnp.zeros((groups, HELD), F32)
        for c in range(sel * 4, sel * 4 + 4):
            hits = jnp.where(spot[:, c : c + 1] == ids, 1.0, hits)
        return jnp.max(hits, axis=0, keepdims=True)

    sent = jnp.concatenate(
        [present(r, 1 + 3 * r + o - 1 if o else 0, o) for r in range(PARTS) for o in range(4)],
        axis=0,
    )
    sent_rank = jnp.where(sent > 0.0, dot(sent.astype(BF), before), -1.0)
    spots = iota((HELD, HELD), 0).astype(F32)
    images = iota((HELD, HELD), 1).astype(F32)
    for c in range(4 * PARTS):
        col = jnp.sum(jnp.where(sent_rank[c : c + 1, :] == spots, images, 0.0), axis=1, keepdims=True)
        lists_ref[:, c : c + 1] = col.astype(jnp.int32)
    got = jnp.concatenate(
        [present(r, 0, o) for r in range(PARTS) for o in range(4)], axis=0
    )
    got_rank = dot(got.astype(BF), before)
    key = jnp.where(valid, table >> 11, 127)
    small = iota((groups, 128), 1)
    earlier = (iota((groups, groups), 1) < iota((groups, groups), 0)).astype(F32).astype(BF)
    marks = [(key[:, c : c + 1] == small).astype(F32) for c in range(4)]
    starts = jnp.zeros((1, 128), F32)
    for c in range(4):
        starts = starts + jnp.sum((key[:, c : c + 1] < small).astype(F32), axis=0, keepdims=True)
    offs_ref[...] = jnp.broadcast_to(starts, (8, 128)).astype(jnp.int32)
    long_ids = iota((groups, 512), 1)
    ahead = starts
    ordered = [jnp.zeros((1, 512), F32) for _ in range(PARTS)]
    for c in range(4):
        pos = jnp.sum(marks[c] * (ahead + dot(earlier, marks[c].astype(BF))), axis=1, keepdims=True)
        ahead = ahead + jnp.sum(marks[c], axis=0, keepdims=True)
        pos = jnp.where(valid[:, c : c + 1], pos.astype(jnp.int32), -1)
        chosen = pos == long_ids
        for r in range(PARTS):
            slot = (offsets[r][:, c : c + 1] * HELD).astype(F32)
            for o in range(4):
                spot = jnp.where(valid & (offsets[r] == o), places[r], -1)[:, c : c + 1]
                row = got_rank[r * 4 + o : r * 4 + o + 1, :]
                slot = slot + jnp.sum(jnp.where(spot == ids, row, 0.0), axis=1, keepdims=True)
            ordered[r] = ordered[r] + jnp.sum(jnp.where(chosen, slot, 0.0), axis=0, keepdims=True)
    codes_ref[...] = jnp.concatenate(ordered + [jnp.zeros((8 - PARTS, 512), F32)], axis=0).astype(jnp.int32)
    named = jnp.where(live == 1, own, -1) - (2 * chip + core) * IMG
    for i in range(IMG):
        count = jnp.sum((named == i).astype(F32))
        div_ref[i * TOK : (i + 1) * TOK, :] = jnp.full((TOK, 128), jnp.maximum(count, 1.0), F32)


def count_kernel(first_ref, second_ref, live_ref, longest_ref, seen):
    chips, sources, fields = 64, 128, 4
    width = first_ref.shape[1]

    def iota(shape, axis):
        return lax.broadcasted_iota(jnp.int32, shape, axis)

    wide = iota((chips * fields, width), 0)
    source = iota((sources, width), 0)
    seen[...] = jnp.zeros_like(seen)

    def step(i, carry):
        one, two = first_ref[pl.ds(i, 1), :], second_ref[pl.ds(i, 1), :]
        live = live_ref[pl.ds(i, 1), :] == 1
        for own, partner in ((one, two), (two, one)):
            chip = jnp.where(live, own >> 5, -8)
            local = partner & 15
            weight = jnp.where(
                (local & 2) == 0,
                jnp.where((local & 1) == 0, 1.0, 64.0),
                jnp.where((local & 1) == 0, 4096.0, 262144.0),
            )
            left = jnp.where(chip * fields + (local >> 2) == wide, weight, 0.0).astype(BF)
            right = jnp.where((partner >> 4) == source, 1.0, 0.0).astype(BF)
            seen[...] += dot(right, left, ((1,), (1,)))
        return carry

    lax.fori_loop(0, first_ref.shape[0], step, 0)
    packed = seen[...].astype(jnp.int32)
    found = jnp.zeros(packed.shape, F32)
    digits = jnp.zeros(packed.shape, F32)
    for f in range(fields):
        digit = (packed >> (6 * f)) & 63
        found = found + jnp.where(digit > 0, 1.0, 0.0)
        digits = digits + digit.astype(F32)
    row, col = iota((128, sources), 0), iota((128, sources), 1)
    axis, coord = row >> 3, (row >> 1) & 3
    moved_by = jnp.where(axis == 0, 5, jnp.where(axis == 1, 3, 1))
    member = ((col & 1) == (row & 1)) & (((col >> moved_by) & 3) == coord) & (axis < 3)
    groups = dot(member.astype(F32).astype(BF), found.astype(BF))
    merge = (iota((chips * fields, 128), 0) >> 2) == iota((chips * fields, 128), 1)
    totals = dot(groups.astype(BF), merge.astype(F32).astype(BF))
    named = 2.0 * jnp.sum(live_ref[...].astype(F32))
    crowded = (jnp.max(seen[...]) >= 2.0**24) | (jnp.sum(digits) != named)
    longest_ref[...] = jnp.full(
        longest_ref.shape, jnp.where(crowded, 1000.0, jnp.max(totals)), F32
    )


def gather_kernel(cap, list_ref, *refs):
    held, outs = refs[: 4 * PARTS], refs[4 * PARTS : 8 * PARTS]
    bufs, staged = refs[8 * PARTS : 9 * PARTS], refs[9 * PARTS : 10 * PARTS]
    in_sems, out_sems = refs[10 * PARTS :]
    size = HELD // 4
    loads = [
        pltpu.make_async_copy(held[n], bufs[n // 4].at[pl.ds(n % 4 * size, size)], in_sems.at[n])
        for n in range(4 * PARTS)
    ]
    stores = [
        pltpu.make_async_copy(staged[n // 4].at[n % 4], outs[n], out_sems.at[n])
        for n in range(4 * PARTS)
    ]
    for c in loads:
        c.start()
    for r in range(PARTS):
        for o in range(4):
            loads[r * 4 + o].wait()

        def step(s, carry, r=r):
            for o in range(4):
                staged[r][o, s] = bufs[r][list_ref[s, r * 4 + o]]
            return carry

        lax.fori_loop(0, cap, step, 0, unroll=8)
        for o in range(4):
            stores[r * 4 + o].start()
    for c in stores:
        c.wait()


def cross_kernel(cap, code_ref, off_ref, g_ref, qkv_ref, *refs):
    parts = refs[: 4 * PARTS]
    mine_ref, other_ref = refs[4 * PARTS : 4 * PARTS + 2]
    bufs = refs[4 * PARTS + 2 : 5 * PARTS + 2]
    wv, folded, xs, acc, mix, sems, g_sems = refs[5 * PARTS + 2 :]
    images = folded.shape[0]
    groups = images // WIDE
    copies = [
        pltpu.make_async_copy(
            parts[r * 4 + o], bufs[r].at[pl.ds(o * cap, cap)], sems.at[r * 4 + o]
        )
        for r in range(PARTS)
        for o in range(4)
    ]
    loads = [
        pltpu.make_async_copy(
            g_ref.at[pl.ds(i * WIDE, WIDE)], folded.at[pl.ds(i * WIDE, WIDE)], g_sems.at[i]
        )
        for i in range(groups)
    ]
    value_load = pltpu.make_async_copy(qkv_ref.at[:, pl.ds(2 * D, D)], wv, sems.at[4 * PARTS])
    for c in copies + loads[:1]:
        c.start()
    for c in copies:
        c.wait()
    for c in loads[1:] + [value_load]:
        c.start()
    row_pair = lax.broadcasted_iota(jnp.int32, (GROUP * TOK, 1), 0) // TOK

    def attended(a, chunk, i):
        start = off_ref[0, a] + chunk * GROUP
        left = off_ref[0, a + 1] - start
        for j in range(GROUP):
            p = jnp.where(j < left, start + j, 0)
            for r in range(PARTS):
                code = code_ref[r, p]
                xs[i, j * TOK : (j + 1) * TOK, STARTS[r] : STARTS[r] + WIDTHS[r]] = bufs[r][
                    (code >> 8) * cap + jnp.minimum(code & 255, cap - 1)
                ]
        x = xs[i]
        s = dot(x, folded[a], ((1,), (1,))).reshape(GROUP, TOK, HEADS * TOK)
        e = jnp.exp(s - jnp.max(s, axis=1, keepdims=True))
        w = (e / jnp.sum(e, axis=1, keepdims=True)).reshape(GROUP * TOK, HEADS * TOK)
        w = jnp.where(row_pair < left, w, 0.0).astype(BF)
        return dot(w, x, ((0,), (0,)))

    def group(step, carry):
        for i in range(WIDE):
            mix[step * WIDE + i] = attended(step * WIDE + i, 0, i).astype(BF)
        return carry

    if cap < HELD:
        for step in range(groups):
            loads[step].wait()
            group(step, 0)
    else:
        for c in loads:
            c.wait()
        lax.fori_loop(0, groups, group, 0)

    def longer(a, carry):
        chunks = (off_ref[0, a + 1] - off_ref[0, a] + GROUP - 1) // GROUP

        @pl.when(chunks > 1)
        def _():
            acc[...] = mix[a].astype(F32)

            def more(c, carry):
                acc[...] += attended(a, c, 0)
                return carry

            lax.fori_loop(1, chunks, more, 0)
            mix[a] = acc[...].astype(BF)

        return carry

    lax.fori_loop(0, images, longer, 0)
    value_load.wait()
    for h in range(HEADS):
        u = mix[:, h * TOK : (h + 1) * TOK, :].reshape(images * TOK, D)
        o = dot(u, wv[:, h * DH : (h + 1) * DH])
        mine_ref[:, h * DH : (h + 1) * DH] = o[: IMG * TOK]
        other_ref[:, h * DH : (h + 1) * DH] = o[IMG * TOK :].astype(BF)


def head_kernel(
    mine_ref, other_ref, div_ref, base_ref, cross_out_ref, gain_ref, weight_ref,
    out_ref, weights, staged, in_sems, out_sems,
):
    tile = weight_ref.shape[1] // HEAD_TILES
    loads = [
        pltpu.make_async_copy(
            weight_ref.at[:, pl.ds(t * tile, tile)], weights.at[t], in_sems.at[t]
        )
        for t in range(HEAD_TILES)
    ]
    for c in loads:
        c.start()
    total = mine_ref[...] + other_ref[...].astype(F32)
    mean = (total / div_ref[:, :1]).astype(BF)
    combined = base_ref[...] + dot(mean, cross_out_ref[...])
    rows = norm(combined, gain_ref[...].reshape(1, D)).astype(BF)
    stores = [
        pltpu.make_async_copy(
            staged.at[t], out_ref.at[:, pl.ds(t * tile, tile)], out_sems.at[t]
        )
        for t in range(HEAD_TILES)
    ]
    for t in range(HEAD_TILES):
        loads[t].wait()
        staged[t] = dot(rows, weights[t]).astype(BF)
        stores[t].start()
    for c in stores:
        c.wait()


def from_offset(x, r, phase, offset):
    pairs = []
    for chip in range(64):
        for core in range(2):
            stride = STRIDES[ORDERS[r][core][phase]]
            c = (chip // stride) % 4
            to = chip + ((c - offset) % 4 - c) * stride
            pairs.append((2 * chip + core, 2 * to + core))
    return lax.ppermute(x, ("img", "grp"), pairs)


def tied(values, others):
    values, _ = lax.optimization_barrier((values, others))
    return values


def exchange(blocks, phase, meanwhile=None):
    got = [[b[0], None, None, None] for b in blocks]

    def send(r, o, block):
        got[r][o] = from_offset(block, r, phase, o)

    for r, o in ((0, 2), (1, 1), (1, 3)):
        send(r, o, blocks[r][o])
    for r, early, late in ((0, (2,), (1, 3)), (1, (1, 3), (2,))):
        for o in late:
            waits = [got[r][e] for e in early] + ([] if meanwhile is None else [meanwhile])
            send(r, o, tied(blocks[r][o], waits) if phase else blocks[r][o])
    return got


def body(
    tokens, pair_list, pair_live, gain_self, gain_cross, gain_head,
    self_qkv, self_out, cross_qkv, cross_out, head_weight,
):
    chip = lax.axis_index("img")
    core = lax.axis_index("grp")
    flat_tokens = tokens.reshape(IMG * TOK, D)
    *rows, own_rows = call(
        norm_kernel,
        [sds(IMG * TOK, w) for w in WIDTHS + (D,)],
        [VMEM] * 2,
        [VMEM] * (PARTS + 1),
    )(flat_tokens, gain_cross)
    blocks = [x.reshape(IMG, TOK, -1) for x in rows]
    near = exchange([[blocks[r]] * 4 for r in range(PARTS)], 0)
    near = lax.optimization_barrier(near)
    lines = call(
        join_kernel, [sds(4 * IMG, TOK, w) for w in WIDTHS], [VMEM] * (4 * PARTS), [VMEM] * PARTS
    )(*[x for row in near for x in row])

    ids = jnp.stack([chip, core]).astype(jnp.int32)
    first, second = pair_list[:, 0], pair_list[:, 1]
    square = [x.reshape(128, 128) for x in (first, second, pair_live)]
    flat = [x.reshape(16, 1024) for x in (first, second, pair_live)]
    lists, codes, offsets, divisor = call(
        plan_kernel,
        [
            sds(HELD, 4 * PARTS, dtype=jnp.int32),
            sds(8, 512, dtype=jnp.int32),
            sds(8, 128, dtype=jnp.int32),
            sds(IMG * TOK, 128, dtype=F32),
        ],
        [SMEM] + [VMEM] * 3,
        [VMEM] * 4,
        limit=FULL,
    )(ids, *tied(square, lines))
    held = exchange([[lines[r]] * 4 for r in range(PARTS)], 1, lists)
    own_rows, late_tokens = tied([own_rows, flat_tokens], [held[0][2], held[1][1]])
    other_rows = lax.ppermute(own_rows, "grp", [(0, 1), (1, 0)])
    base = call(
        self_kernel,
        sds(IMG * TOK, D, dtype=F32),
        [VMEM] * 4,
        HBM,
        [pltpu.VMEM((IMG * TOK, D), F32), pltpu.SemaphoreType.DMA],
        limit=FULL,
    )(late_tokens, gain_self, self_qkv, self_out)
    all_weight = lax.all_gather(head_weight, "grp", axis=1, tiled=True)

    def gathered(cap, lists, held):
        out = call(
            functools.partial(gather_kernel, cap),
            [sds(cap, TOK, w) for w in WIDTHS for o in range(4)],
            [SMEM] + [HBM] * (4 * PARTS),
            [HBM] * (4 * PARTS),
            [
                *[pltpu.VMEM((HELD, TOK, w), BF) for w in WIDTHS],
                *[pltpu.VMEM((4, cap, TOK, w), BF) for w in WIDTHS],
                pltpu.SemaphoreType.DMA((4 * PARTS,)),
                pltpu.SemaphoreType.DMA((4 * PARTS,)),
            ],
            limit=60,
        )(lists, *[x for row in held for x in row])
        return [list(out[r * 4 : r * 4 + 4]) for r in range(PARTS)]

    def crossed(cap, codes, offsets, folded, cross, arrived):
        return call(
            functools.partial(cross_kernel, cap),
            [sds(IMG * TOK, D, dtype=F32), sds(IMG * TOK, D)],
            [SMEM] * 2 + [HBM] * (2 + 4 * PARTS),
            [VMEM] * 2,
            [
                *[pltpu.VMEM((4 * cap, TOK, w), BF) for w in WIDTHS],
                pltpu.VMEM((D, D), BF),
                pltpu.VMEM((2 * IMG, HEADS * TOK, D), BF),
                pltpu.VMEM((WIDE, GROUP * TOK, D), BF),
                pltpu.VMEM((HEADS * TOK, D), F32),
                pltpu.VMEM((2 * IMG, HEADS * TOK, D), BF),
                pltpu.SemaphoreType.DMA((4 * PARTS + 1,)),
                pltpu.SemaphoreType.DMA((2 * IMG // WIDE,)),
            ],
            limit=FULL,
        )(codes, offsets, folded, cross, *[x for row in arrived for x in row])

    chosen = gathered(CAP, tied(lists, [base, other_rows]), held)
    own_rows, other_rows = tied([own_rows, other_rows], chosen[0][0])
    folded = call(
        fold_kernel,
        sds(2 * IMG, HEADS * TOK, D),
        [VMEM] * 3,
        HBM,
        [pltpu.VMEM((2 * IMG, HEADS * TOK, D), BF), pltpu.SemaphoreType.DMA],
        limit=FULL,
    )(
        own_rows, other_rows, cross_qkv
    )
    arrived = exchange(chosen, 2, folded)
    longest = call(
        count_kernel,
        sds(8, 128, dtype=F32),
        [VMEM] * 3,
        VMEM,
        [pltpu.VMEM((128, 256), F32)],
        limit=FULL,
    )(*tied(flat, [arrived[0][2], arrived[1][1]]))[0, 0]
    sums = crossed(CAP, codes, offsets, folded, cross_qkv, arrived)

    def redo(state):
        again = exchange(gathered(HELD, lists, held), 2)
        return (jnp.zeros((), F32), *crossed(HELD, codes, offsets, folded, cross_qkv, again))

    _, mine_sum, other_sum = lax.while_loop(lambda state: state[0] > CAP, redo, (longest, *sums))
    size = IMG * TOK
    other_sum = lax.ppermute(other_sum, "grp", [(0, 1), (1, 0)])
    outc = all_weight.shape[1]
    pixel_maps = call(
        head_kernel,
        sds(size, outc),
        [VMEM] * 6 + [HBM],
        HBM,
        [
            pltpu.VMEM((HEAD_TILES, D, outc // HEAD_TILES), BF),
            pltpu.VMEM((HEAD_TILES, size, outc // HEAD_TILES), BF),
            pltpu.SemaphoreType.DMA((HEAD_TILES,)),
            pltpu.SemaphoreType.DMA((HEAD_TILES,)),
        ],
        limit=FULL,
    )(mine_sum, other_sum, divisor, base, cross_out, gain_head, all_weight)
    return pixel_maps.reshape(IMG, TOK, -1)


def solution(mesh):
    placed = (P(("img", "grp"), None, None),) + (P(),) * 9 + (P(None, "grp"),)
    return jax.shard_map(
        body, mesh=mesh, in_specs=placed, out_specs=P(("img", "grp"), None, None), check_vma=False
    )
```

```python
import functools

import jax
import jax.numpy as jnp
from jax import lax
from jax.experimental import pallas as pl
from jax.experimental.pallas import tpu as pltpu
from jax.sharding import PartitionSpec as P

HEADS = 12
DH = 64
D = 768
TOK = 16
IMG = 16
HELD = 256
CAP = 84
PARTS = 2
WIDTHS = (512, 256)
STARTS = (0, 512)
ORDERS = (((2, 0, 1), (0, 1, 2)), ((1, 2, 0), (1, 2, 0)))
GROUP = 12
WIDE = 8
HEAD_TILES = 7
FIRST_ROUND = ((0, 2), (1, 1), (1, 3))
LATER = ((0, 1), (0, 3), (1, 2), (0, 0), (1, 0))
EPSILON = 1e-05
STRIDES = (16, 4, 1)
BF = jnp.bfloat16
F32 = jnp.float32
VMEM = pl.BlockSpec(memory_space=pltpu.VMEM)
HBM = pl.BlockSpec(memory_space=pltpu.HBM)
SMEM = pl.BlockSpec(memory_space=pltpu.SMEM)
MIB = 1024 * 1024
FULL = 62


def dot(a, b, dims=((1,), (0,))):
    return lax.dot_general(a, b, (dims, ((), ())), preferred_element_type=F32)


def norm(values, gain):
    mean_val = jnp.mean(values, axis=-1, keepdims=True)
    centred = values - mean_val
    variance = jnp.mean(centred * centred, axis=-1, keepdims=True)
    return centred * lax.rsqrt(variance + EPSILON) * gain


def sds(*shape, dtype=BF):
    return jax.ShapeDtypeStruct(shape, dtype)


def call(kernel, outs, specs, out_specs, scratch=(), limit=16, flops=0, size=0):
    return pl.pallas_call(
        kernel,
        out_shape=outs,
        in_specs=specs,
        out_specs=out_specs,
        scratch_shapes=list(scratch),
        compiler_params=pltpu.CompilerParams(vmem_limit_bytes=limit * MIB),
        cost_estimate=pl.CostEstimate(flops=flops, bytes_accessed=size, transcendentals=0),
    )


def norm_kernel(tok_ref, gain_ref, *outs):
    rows = norm(tok_ref[...].astype(F32), gain_ref[...].reshape(1, D)).astype(BF)
    for r in range(PARTS):
        outs[r][...] = rows[:, STARTS[r] : STARTS[r] + WIDTHS[r]]
    outs[PARTS][...] = rows


def join_kernel(*refs):
    outs = refs[4 * PARTS :]
    for r in range(PARTS):
        for o in range(4):
            outs[r][o * IMG : (o + 1) * IMG] = refs[r * 4 + o][...]


def self_kernel(tok_ref, gain_ref, qkv_ref, out_ref, base_ref, staged, sem):
    tok = tok_ref[...].astype(F32)
    rows = norm(tok, gain_ref[...].reshape(1, D)).astype(BF)
    proj = dot(rows, qkv_ref[...]).astype(BF)
    n = tok.shape[0]
    same = (lax.broadcasted_iota(jnp.int32, (n, n), 0) // TOK) == (
        lax.broadcasted_iota(jnp.int32, (n, n), 1) // TOK
    )
    total = tok
    mixed = []
    for h in range(HEADS):
        q = proj[:, h * DH : (h + 1) * DH]
        k = proj[:, D + h * DH : D + (h + 1) * DH]
        v = proj[:, 2 * D + h * DH : 2 * D + (h + 1) * DH]
        s = dot(q, k, ((1,), (1,))) * 0.125
        s = jnp.where(same, s, -1e30)
        e = jnp.exp(s - jnp.max(s, axis=1, keepdims=True))
        p = (e / jnp.sum(e, axis=1, keepdims=True)).astype(BF)
        mixed.append(dot(p, v).astype(BF))
    staged[...] = total + dot(jnp.concatenate(mixed, axis=1), out_ref[...])
    copy = pltpu.make_async_copy(staged, base_ref, sem)
    copy.start()
    copy.wait()


def fold_kernel(own_ref, other_ref, qkv_ref, out_ref, staged, sem):
    rows = jnp.concatenate([own_ref[...], other_ref[...]], axis=0)
    q = (dot(rows, qkv_ref[:, :D]).astype(BF).astype(F32) * 0.125).astype(BF)
    images = rows.shape[0] // TOK
    for h in range(HEADS):
        keys = qkv_ref[:, D + h * DH : D + (h + 1) * DH]
        g = dot(q[:, h * DH : (h + 1) * DH], keys, ((1,), (1,)))
        staged[:, h * TOK : (h + 1) * TOK, :] = g.astype(BF).reshape(images, TOK, D)
    copy = pltpu.make_async_copy(staged, out_ref, sem)
    copy.start()
    copy.wait()


def plan_kernel(
    ids_ref, first_ref, second_ref, live_ref, lists_ref, codes_ref, offs_ref, div_ref
):
    chip, core = ids_ref[0], ids_ref[1]
    own = jnp.concatenate([first_ref[...], second_ref[...]], axis=1)
    partner = jnp.concatenate([second_ref[...], first_ref[...]], axis=1)
    live = jnp.concatenate([live_ref[...]] * 2, axis=1)
    groups, sides = own.shape

    def iota(shape, axis):
        return lax.broadcasted_iota(jnp.int32, shape, axis)

    before = (iota((sides, sides), 0) < iota((sides, sides), 1)).astype(F32).astype(BF)
    usable = (live == 1) & (((partner >> 4) & 1) == core)
    owner = jnp.where(usable, own >> 4, -1)
    code = ((((((own >> 4) & 1) ^ core) * IMG + (own & 15)) << 11) + partner + 1).astype(F32)
    my = [(chip >> 4) & 3, (chip >> 2) & 3, chip & 3]

    def pick(r, phase, values):
        zero, one = values[ORDERS[r][0][phase]], values[ORDERS[r][1][phase]]
        return jnp.where(core == 0, zero, one)

    lane = iota((groups, 128), 1)
    table = jnp.zeros((groups, 128), F32)
    for sel in range(1 + 3 * PARTS):
        target = chip
        if sel:
            r, o = (sel - 1) // 3, (sel - 1) % 3 + 1
            at = pick(r, 2, my)
            target = chip + (((at - o) & 3) - at) * pick(r, 2, STRIDES)
        for dev in range(2):
            mine = owner == 2 * target + dev
            rank = dot(mine.astype(F32).astype(BF), before)
            for k in range(2):
                col = jnp.sum(jnp.where(mine & (rank == float(k)), code, 0.0), axis=1, keepdims=True)
                table = jnp.where(lane == sel * 4 + dev * 2 + k, col, table)
    table = table.astype(jnp.int32) - 1
    valid = table >= 0
    partners = table & 2047
    local = partners & 15
    sel = lane >> 2
    lane_r = jnp.where(sel > 3, 1, 0)
    lane_o = jnp.where(sel > 0, sel - 3 * lane_r, 0)
    places, offsets = [], []
    for r in range(PARTS):
        offs = []
        for phase in range(3):
            here = pick(r, phase, my)
            if phase == 2:
                here = here - jnp.where(lane_r == r, lane_o, 0)
            offs.append((((partners >> pick(r, phase, (9, 7, 5))) & 3) - here) & 3)
        places.append((offs[1] * 4 + offs[0]) * IMG + local)
        offsets.append(offs[2])
    ids = iota((groups, HELD), 1)

    def present(r, sel, o):
        spot = jnp.where(valid & (offsets[r] == o), places[r], -1)
        hits = jnp.zeros((groups, HELD), F32)
        for c in range(sel * 4, sel * 4 + 4):
            hits = jnp.where(spot[:, c : c + 1] == ids, 1.0, hits)
        return jnp.max(hits, axis=0, keepdims=True)

    sent = jnp.concatenate(
        [present(r, 1 + 3 * r + o - 1 if o else 0, o) for r in range(PARTS) for o in range(4)],
        axis=0,
    )
    sent_rank = jnp.where(sent > 0.0, dot(sent.astype(BF), before), -1.0)
    spots = iota((HELD, HELD), 0).astype(F32)
    images = iota((HELD, HELD), 1).astype(F32)
    for c in range(4 * PARTS):
        col = jnp.sum(jnp.where(sent_rank[c : c + 1, :] == spots, images, 0.0), axis=1, keepdims=True)
        lists_ref[:, c : c + 1] = col.astype(jnp.int32)
    got = jnp.concatenate(
        [present(r, 0, o) for r in range(PARTS) for o in range(4)], axis=0
    )
    got_rank = dot(got.astype(BF), before)
    key = jnp.where(valid, table >> 11, 127)
    small = iota((groups, 128), 1)
    earlier = (iota((groups, groups), 1) < iota((groups, groups), 0)).astype(F32).astype(BF)
    marks = [(key[:, c : c + 1] == small).astype(F32) for c in range(4)]
    starts = jnp.zeros((1, 128), F32)
    for c in range(4):
        starts = starts + jnp.sum((key[:, c : c + 1] < small).astype(F32), axis=0, keepdims=True)
    offs_ref[...] = jnp.broadcast_to(starts, (8, 128)).astype(jnp.int32)
    long_ids = iota((groups, 512), 1)
    ahead = starts
    ordered = [jnp.zeros((1, 512), F32) for _ in range(PARTS)]
    for c in range(4):
        pos = jnp.sum(marks[c] * (ahead + dot(earlier, marks[c].astype(BF))), axis=1, keepdims=True)
        ahead = ahead + jnp.sum(marks[c], axis=0, keepdims=True)
        pos = jnp.where(valid[:, c : c + 1], pos.astype(jnp.int32), -1)
        chosen = pos == long_ids
        for r in range(PARTS):
            slot = (offsets[r][:, c : c + 1] * HELD).astype(F32)
            for o in range(4):
                spot = jnp.where(valid & (offsets[r] == o), places[r], -1)[:, c : c + 1]
                row = got_rank[r * 4 + o : r * 4 + o + 1, :]
                slot = slot + jnp.sum(jnp.where(spot == ids, row, 0.0), axis=1, keepdims=True)
            ordered[r] = ordered[r] + jnp.sum(jnp.where(chosen, slot, 0.0), axis=0, keepdims=True)
    codes_ref[...] = jnp.concatenate(ordered + [jnp.zeros((8 - PARTS, 512), F32)], axis=0).astype(jnp.int32)
    named = jnp.where(live == 1, own, -1) - (2 * chip + core) * IMG
    for i in range(IMG):
        count = jnp.sum((named == i).astype(F32))
        div_ref[i * TOK : (i + 1) * TOK, :] = jnp.full((TOK, 128), jnp.maximum(count, 1.0), F32)


def count_kernel(first_ref, second_ref, live_ref, longest_ref, seen):
    chips, sources, fields = 64, 128, 4
    width = first_ref.shape[1]

    def iota(shape, axis):
        return lax.broadcasted_iota(jnp.int32, shape, axis)

    wide = iota((chips * fields, width), 0)
    source = iota((sources, width), 0)
    seen[...] = jnp.zeros_like(seen)

    def step(i, carry):
        one, two = first_ref[pl.ds(i, 1), :], second_ref[pl.ds(i, 1), :]
        live = live_ref[pl.ds(i, 1), :] == 1
        for own, partner in ((one, two), (two, one)):
            chip = jnp.where(live, own >> 5, -8)
            local = partner & 15
            weight = jnp.where(
                (local & 2) == 0,
                jnp.where((local & 1) == 0, 1.0, 64.0),
                jnp.where((local & 1) == 0, 4096.0, 262144.0),
            )
            left = jnp.where(chip * fields + (local >> 2) == wide, weight, 0.0).astype(BF)
            right = jnp.where((partner >> 4) == source, 1.0, 0.0).astype(BF)
            seen[...] += dot(right, left, ((1,), (1,)))
        return carry

    lax.fori_loop(0, first_ref.shape[0], step, 0)
    packed = seen[...].astype(jnp.int32)
    found = jnp.zeros(packed.shape, F32)
    digits = jnp.zeros(packed.shape, F32)
    for f in range(fields):
        digit = (packed >> (6 * f)) & 63
        found = found + jnp.where(digit > 0, 1.0, 0.0)
        digits = digits + digit.astype(F32)
    row, col = iota((128, sources), 0), iota((128, sources), 1)
    axis, coord = row >> 3, (row >> 1) & 3
    moved_by = jnp.where(axis == 0, 5, jnp.where(axis == 1, 3, 1))
    member = ((col & 1) == (row & 1)) & (((col >> moved_by) & 3) == coord) & (axis < 3)
    groups = dot(member.astype(F32).astype(BF), found.astype(BF))
    merge = (iota((chips * fields, 128), 0) >> 2) == iota((chips * fields, 128), 1)
    totals = dot(groups.astype(BF), merge.astype(F32).astype(BF))
    named = 2.0 * jnp.sum(live_ref[...].astype(F32))
    crowded = (jnp.max(seen[...]) >= 2.0**24) | (jnp.sum(digits) != named)
    longest_ref[...] = jnp.full(
        longest_ref.shape, jnp.where(crowded, 1000.0, jnp.max(totals)), F32
    )


def gather_kernel(cap, targets, list_ref, *refs):
    held, outs = refs[: 4 * PARTS], refs[4 * PARTS : 4 * PARTS + len(targets)]
    bufs = refs[4 * PARTS + len(targets) :][:PARTS]
    staged = refs[5 * PARTS + len(targets) :][: len(targets)]
    in_sems, out_sems = refs[5 * PARTS + 2 * len(targets) :]
    size = HELD // 4
    loads = [
        pltpu.make_async_copy(held[n], bufs[n // 4].at[pl.ds(n % 4 * size, size)], in_sems.at[n])
        for n in range(4 * PARTS)
    ]
    stores = [
        pltpu.make_async_copy(staged[t], outs[t], out_sems.at[t]) for t in range(len(targets))
    ]
    for c in loads:
        c.start()
    for r in range(PARTS):
        for o in range(4):
            loads[r * 4 + o].wait()
        mine = [(t, o) for t, (block, o) in enumerate(targets) if block == r]

        def step(s, carry, r=r, mine=mine):
            for t, o in mine:
                staged[t][s] = bufs[r][list_ref[s, r * 4 + o]]
            return carry

        lax.fori_loop(0, cap, step, 0, unroll=4)
        for t, _ in mine:
            stores[t].start()
    for c in stores:
        c.wait()


def cross_kernel(cap, code_ref, off_ref, g_ref, qkv_ref, *refs):
    parts = refs[: 4 * PARTS]
    mine_ref, other_ref = refs[4 * PARTS : 4 * PARTS + 2]
    bufs = refs[4 * PARTS + 2 : 5 * PARTS + 2]
    wv, folded, xs, acc, mix, sems, g_sems = refs[5 * PARTS + 2 :]
    images = folded.shape[0]
    groups = images // WIDE
    copies = [
        pltpu.make_async_copy(
            parts[r * 4 + o], bufs[r].at[pl.ds(o * cap, cap)], sems.at[r * 4 + o]
        )
        for r in range(PARTS)
        for o in range(4)
    ]
    loads = [
        pltpu.make_async_copy(
            g_ref.at[pl.ds(i * WIDE, WIDE)], folded.at[pl.ds(i * WIDE, WIDE)], g_sems.at[i]
        )
        for i in range(groups)
    ]
    value_load = pltpu.make_async_copy(qkv_ref.at[:, pl.ds(2 * D, D)], wv, sems.at[4 * PARTS])
    for c in copies + loads[:1]:
        c.start()
    for c in copies:
        c.wait()
    for c in loads[1:] + [value_load]:
        c.start()
    row_pair = lax.broadcasted_iota(jnp.int32, (GROUP * TOK, 1), 0) // TOK

    def attended(a, chunk, i):
        start = off_ref[0, a] + chunk * GROUP
        left = off_ref[0, a + 1] - start
        for j in range(GROUP):
            p = jnp.where(j < left, start + j, 0)
            for r in range(PARTS):
                code = code_ref[r, p]
                xs[i, j * TOK : (j + 1) * TOK, STARTS[r] : STARTS[r] + WIDTHS[r]] = bufs[r][
                    (code >> 8) * cap + jnp.minimum(code & 255, cap - 1)
                ]
        x = xs[i]
        s = dot(x, folded[a], ((1,), (1,))).reshape(GROUP, TOK, HEADS * TOK)
        e = jnp.exp(s - jnp.max(s, axis=1, keepdims=True))
        w = (e / jnp.sum(e, axis=1, keepdims=True)).reshape(GROUP * TOK, HEADS * TOK)
        w = jnp.where(row_pair < left, w, 0.0).astype(BF)
        return dot(w, x, ((0,), (0,)))

    def group(step, carry):
        for i in range(WIDE):
            mix[step * WIDE + i] = attended(step * WIDE + i, 0, i).astype(BF)
        return carry

    if cap < HELD:
        for step in range(groups):
            loads[step].wait()
            group(step, 0)
    else:
        for c in loads:
            c.wait()
        lax.fori_loop(0, groups, group, 0)

    def longer(a, carry):
        chunks = (off_ref[0, a + 1] - off_ref[0, a] + GROUP - 1) // GROUP

        @pl.when(chunks > 1)
        def _():
            acc[...] = mix[a].astype(F32)

            def more(c, carry):
                acc[...] += attended(a, c, 0)
                return carry

            lax.fori_loop(1, chunks, more, 0)
            mix[a] = acc[...].astype(BF)

        return carry

    lax.fori_loop(0, images, longer, 0)
    value_load.wait()
    for h in range(HEADS):
        u = mix[:, h * TOK : (h + 1) * TOK, :].reshape(images * TOK, D)
        o = dot(u, wv[:, h * DH : (h + 1) * DH])
        mine_ref[:, h * DH : (h + 1) * DH] = o[: IMG * TOK]
        other_ref[:, h * DH : (h + 1) * DH] = o[IMG * TOK :].astype(BF)


def head_kernel(
    mine_ref, other_ref, div_ref, base_ref, cross_out_ref, gain_ref, weight_ref,
    out_ref, weights, staged, in_sems, out_sems,
):
    tile = weight_ref.shape[1] // HEAD_TILES
    loads = [
        pltpu.make_async_copy(
            weight_ref.at[:, pl.ds(t * tile, tile)], weights.at[t], in_sems.at[t]
        )
        for t in range(HEAD_TILES)
    ]
    for c in loads:
        c.start()
    total = mine_ref[...] + other_ref[...].astype(F32)
    mean = (total / div_ref[:, :1]).astype(BF)
    combined = base_ref[...] + dot(mean, cross_out_ref[...])
    rows = norm(combined, gain_ref[...].reshape(1, D)).astype(BF)
    stores = [
        pltpu.make_async_copy(
            staged.at[t], out_ref.at[:, pl.ds(t * tile, tile)], out_sems.at[t]
        )
        for t in range(HEAD_TILES)
    ]
    for t in range(HEAD_TILES):
        loads[t].wait()
        staged[t] = dot(rows, weights[t]).astype(BF)
        stores[t].start()
    for c in stores:
        c.wait()


def from_offset(x, r, phase, offset):
    pairs = []
    for chip in range(64):
        for core in range(2):
            stride = STRIDES[ORDERS[r][core][phase]]
            c = (chip // stride) % 4
            to = chip + ((c - offset) % 4 - c) * stride
            pairs.append((2 * chip + core, 2 * to + core))
    return lax.ppermute(x, ("img", "grp"), pairs)


def tied(values, others):
    values, _ = lax.optimization_barrier((values, others))
    return values


def exchange(blocks, phase, meanwhile=None):
    got = [[b[0], None, None, None] for b in blocks]

    def send(r, o, block):
        got[r][o] = from_offset(block, r, phase, o)

    for r, o in FIRST_ROUND:
        send(r, o, blocks[r][o])
    for r, early, late in ((0, (2,), (1, 3)), (1, (1, 3), (2,))):
        for o in late:
            waits = [got[r][e] for e in early] + ([] if meanwhile is None else [meanwhile])
            send(r, o, tied(blocks[r][o], waits) if phase else blocks[r][o])
    return got


def body(
    tokens, pair_list, pair_live, gain_self, gain_cross, gain_head,
    self_qkv, self_out, cross_qkv, cross_out, head_weight,
):
    chip = lax.axis_index("img")
    core = lax.axis_index("grp")
    flat_tokens = tokens.reshape(IMG * TOK, D)
    *rows, own_rows = call(
        norm_kernel,
        [sds(IMG * TOK, w) for w in WIDTHS + (D,)],
        [VMEM] * 2,
        [VMEM] * (PARTS + 1),
    )(flat_tokens, gain_cross)
    blocks = [x.reshape(IMG, TOK, -1) for x in rows]
    near = exchange([[blocks[r]] * 4 for r in range(PARTS)], 0)
    near = lax.optimization_barrier(near)
    lines = call(
        join_kernel, [sds(4 * IMG, TOK, w) for w in WIDTHS], [VMEM] * (4 * PARTS), [VMEM] * PARTS
    )(*[x for row in near for x in row])

    ids = jnp.stack([chip, core]).astype(jnp.int32)
    first, second = pair_list[:, 0], pair_list[:, 1]
    square = [x.reshape(128, 128) for x in (first, second, pair_live)]
    flat = [x.reshape(16, 1024) for x in (first, second, pair_live)]
    lists, codes, offsets, divisor = call(
        plan_kernel,
        [
            sds(HELD, 4 * PARTS, dtype=jnp.int32),
            sds(8, 512, dtype=jnp.int32),
            sds(8, 128, dtype=jnp.int32),
            sds(IMG * TOK, 128, dtype=F32),
        ],
        [SMEM] + [VMEM] * 3,
        [VMEM] * 4,
        limit=FULL,
    )(ids, *tied(square, lines))
    held = exchange([[lines[r]] * 4 for r in range(PARTS)], 1, lists)
    own_rows, late_tokens = tied([own_rows, flat_tokens], [held[0][2], held[1][1]])
    other_rows = lax.ppermute(own_rows, "grp", [(0, 1), (1, 0)])
    base = call(
        self_kernel,
        sds(IMG * TOK, D, dtype=F32),
        [VMEM] * 4,
        HBM,
        [pltpu.VMEM((IMG * TOK, D), F32), pltpu.SemaphoreType.DMA],
        limit=FULL,
    )(late_tokens, gain_self, self_qkv, self_out)
    all_weight = lax.all_gather(head_weight, "grp", axis=1, tiled=True)

    def gathered(cap, targets, lists, held):
        widths = [WIDTHS[r] for r, _ in targets]
        return call(
            functools.partial(gather_kernel, cap, targets),
            [sds(cap, TOK, w) for w in widths],
            [SMEM] + [HBM] * (4 * PARTS),
            [HBM] * len(targets),
            [
                *[pltpu.VMEM((HELD, TOK, w), BF) for w in WIDTHS],
                *[pltpu.VMEM((cap, TOK, w), BF) for w in widths],
                pltpu.SemaphoreType.DMA((4 * PARTS,)),
                pltpu.SemaphoreType.DMA((len(targets),)),
            ],
            limit=FULL,
        )(lists, *[x for row in held for x in row])

    def grid_of(targets, values):
        found = dict(zip(targets, values))
        return [[found[r, o] for o in range(4)] for r in range(PARTS)]

    def crossed(cap, codes, offsets, folded, cross, arrived):
        return call(
            functools.partial(cross_kernel, cap),
            [sds(IMG * TOK, D, dtype=F32), sds(IMG * TOK, D)],
            [SMEM] * 2 + [HBM] * (2 + 4 * PARTS),
            [VMEM] * 2,
            [
                *[pltpu.VMEM((4 * cap, TOK, w), BF) for w in WIDTHS],
                pltpu.VMEM((D, D), BF),
                pltpu.VMEM((2 * IMG, HEADS * TOK, D), BF),
                pltpu.VMEM((WIDE, GROUP * TOK, D), BF),
                pltpu.VMEM((HEADS * TOK, D), F32),
                pltpu.VMEM((2 * IMG, HEADS * TOK, D), BF),
                pltpu.SemaphoreType.DMA((4 * PARTS + 1,)),
                pltpu.SemaphoreType.DMA((2 * IMG // WIDE,)),
            ],
            limit=FULL,
        )(codes, offsets, folded, cross, *[x for row in arrived for x in row])

    sent_first = gathered(CAP, FIRST_ROUND, tied(lists, [base, other_rows]), held)
    sent_later = gathered(CAP, LATER, tied(lists, sent_first), held)
    chosen = grid_of(FIRST_ROUND + LATER, [*sent_first, *sent_later])
    own_rows, other_rows = tied([own_rows, other_rows], sent_first)
    folded = call(
        fold_kernel,
        sds(2 * IMG, HEADS * TOK, D),
        [VMEM] * 3,
        HBM,
        [pltpu.VMEM((2 * IMG, HEADS * TOK, D), BF), pltpu.SemaphoreType.DMA],
        limit=FULL,
    )(
        own_rows, other_rows, cross_qkv
    )
    arrived = exchange(chosen, 2, folded)
    longest = call(
        count_kernel,
        sds(8, 128, dtype=F32),
        [VMEM] * 3,
        VMEM,
        [pltpu.VMEM((128, 256), F32)],
        limit=FULL,
    )(*tied(flat, [arrived[0][2], arrived[1][1]]))[0, 0]
    sums = crossed(CAP, codes, offsets, folded, cross_qkv, arrived)

    def redo(state):
        targets = FIRST_ROUND + LATER
        again = exchange(grid_of(targets, gathered(HELD, targets, lists, held)), 2)
        return (jnp.zeros((), F32), *crossed(HELD, codes, offsets, folded, cross_qkv, again))

    _, mine_sum, other_sum = lax.while_loop(lambda state: state[0] > CAP, redo, (longest, *sums))
    size = IMG * TOK
    other_sum = lax.ppermute(other_sum, "grp", [(0, 1), (1, 0)])
    outc = all_weight.shape[1]
    pixel_maps = call(
        head_kernel,
        sds(size, outc),
        [VMEM] * 6 + [HBM],
        HBM,
        [
            pltpu.VMEM((HEAD_TILES, D, outc // HEAD_TILES), BF),
            pltpu.VMEM((HEAD_TILES, size, outc // HEAD_TILES), BF),
            pltpu.SemaphoreType.DMA((HEAD_TILES,)),
            pltpu.SemaphoreType.DMA((HEAD_TILES,)),
        ],
        limit=FULL,
    )(mine_sum, other_sum, divisor, base, cross_out, gain_head, all_weight)
    return pixel_maps.reshape(IMG, TOK, -1)


def solution(mesh):
    placed = (P(("img", "grp"), None, None),) + (P(),) * 9 + (P(None, "grp"),)
    return jax.shard_map(
        body, mesh=mesh, in_specs=placed, out_specs=P(("img", "grp"), None, None), check_vma=False
    )
```

```python
import functools

import jax
import jax.numpy as jnp
from jax import lax
from jax.experimental import pallas as pl
from jax.experimental.pallas import tpu as pltpu
from jax.sharding import PartitionSpec as P

HEADS = 12
DH = 64
D = 768
TOK = 16
IMG = 16
HELD = 256
CAP = 84
PARTS = 2
WIDTHS = (512, 256)
STARTS = (0, 512)
ORDERS = (((2, 0, 1), (0, 1, 2)), ((1, 2, 0), (1, 2, 0)))
GROUP = 12
WIDE = 8
HEAD_TILES = 7
FIRST_ROUND = ((0, 2), (1, 1), (1, 3))
LATER = ((0, 1), (0, 3), (1, 2), (0, 0), (1, 0))
EPSILON = 1e-05
STRIDES = (16, 4, 1)
BF = jnp.bfloat16
F32 = jnp.float32
VMEM = pl.BlockSpec(memory_space=pltpu.VMEM)
HBM = pl.BlockSpec(memory_space=pltpu.HBM)
SMEM = pl.BlockSpec(memory_space=pltpu.SMEM)
MIB = 1024 * 1024
FULL = 62


def dot(a, b, dims=((1,), (0,))):
    return lax.dot_general(a, b, (dims, ((), ())), preferred_element_type=F32)


def norm(values, gain):
    mean_val = jnp.mean(values, axis=-1, keepdims=True)
    centred = values - mean_val
    variance = jnp.mean(centred * centred, axis=-1, keepdims=True)
    return centred * lax.rsqrt(variance + EPSILON) * gain


def sds(*shape, dtype=BF):
    return jax.ShapeDtypeStruct(shape, dtype)


def call(kernel, outs, specs, out_specs, scratch=(), limit=16, flops=0, size=0):
    return pl.pallas_call(
        kernel,
        out_shape=outs,
        in_specs=specs,
        out_specs=out_specs,
        scratch_shapes=list(scratch),
        compiler_params=pltpu.CompilerParams(vmem_limit_bytes=limit * MIB),
        cost_estimate=pl.CostEstimate(flops=flops, bytes_accessed=size, transcendentals=0),
    )


def norm_kernel(tok_ref, gain_ref, *outs):
    rows = norm(tok_ref[...].astype(F32), gain_ref[...].reshape(1, D)).astype(BF)
    for r in range(PARTS):
        outs[r][...] = rows[:, STARTS[r] : STARTS[r] + WIDTHS[r]]
    outs[PARTS][...] = rows


def join_kernel(*refs):
    outs = refs[4 * PARTS :]
    for r in range(PARTS):
        for o in range(4):
            outs[r][o * IMG : (o + 1) * IMG] = refs[r * 4 + o][...]


def self_kernel(tok_ref, gain_ref, qkv_ref, out_ref, base_ref, staged, sem):
    tok = tok_ref[...].astype(F32)
    rows = norm(tok, gain_ref[...].reshape(1, D)).astype(BF)
    proj = dot(rows, qkv_ref[...]).astype(BF)
    n = tok.shape[0]
    same = (lax.broadcasted_iota(jnp.int32, (n, n), 0) // TOK) == (
        lax.broadcasted_iota(jnp.int32, (n, n), 1) // TOK
    )
    total = tok
    mixed = []
    for h in range(HEADS):
        q = proj[:, h * DH : (h + 1) * DH]
        k = proj[:, D + h * DH : D + (h + 1) * DH]
        v = proj[:, 2 * D + h * DH : 2 * D + (h + 1) * DH]
        s = dot(q, k, ((1,), (1,))) * 0.125
        s = jnp.where(same, s, -1e30)
        e = jnp.exp(s - jnp.max(s, axis=1, keepdims=True))
        p = (e / jnp.sum(e, axis=1, keepdims=True)).astype(BF)
        mixed.append(dot(p, v).astype(BF))
    staged[...] = total + dot(jnp.concatenate(mixed, axis=1), out_ref[...])
    copy = pltpu.make_async_copy(staged, base_ref, sem)
    copy.start()
    copy.wait()


def fold_kernel(own_ref, other_ref, qkv_ref, out_ref, staged, sem):
    rows = jnp.concatenate([own_ref[...], other_ref[...]], axis=0)
    q = (dot(rows, qkv_ref[:, :D]).astype(BF).astype(F32) * 0.125).astype(BF)
    images = rows.shape[0] // TOK
    for h in range(HEADS):
        keys = qkv_ref[:, D + h * DH : D + (h + 1) * DH]
        g = dot(q[:, h * DH : (h + 1) * DH], keys, ((1,), (1,)))
        staged[:, h * TOK : (h + 1) * TOK, :] = g.astype(BF).reshape(images, TOK, D)
    copy = pltpu.make_async_copy(staged, out_ref, sem)
    copy.start()
    copy.wait()


def plan_kernel(
    ids_ref, first_ref, second_ref, live_ref, lists_ref, codes_ref, offs_ref, div_ref
):
    chip, core = ids_ref[0], ids_ref[1]
    own = jnp.concatenate([first_ref[...], second_ref[...]], axis=1)
    partner = jnp.concatenate([second_ref[...], first_ref[...]], axis=1)
    live = jnp.concatenate([live_ref[...]] * 2, axis=1)
    groups, sides = own.shape

    def iota(shape, axis):
        return lax.broadcasted_iota(jnp.int32, shape, axis)

    before = (iota((sides, sides), 0) < iota((sides, sides), 1)).astype(F32).astype(BF)
    usable = (live == 1) & (((partner >> 4) & 1) == core)
    owner = jnp.where(usable, own >> 4, -1)
    code = ((((((own >> 4) & 1) ^ core) * IMG + (own & 15)) << 11) + partner + 1).astype(F32)
    my = [(chip >> 4) & 3, (chip >> 2) & 3, chip & 3]

    def pick(r, phase, values):
        zero, one = values[ORDERS[r][0][phase]], values[ORDERS[r][1][phase]]
        return jnp.where(core == 0, zero, one)

    lane = iota((groups, 128), 1)
    table = jnp.zeros((groups, 128), F32)
    for sel in range(1 + 3 * PARTS):
        target = chip
        if sel:
            r, o = (sel - 1) // 3, (sel - 1) % 3 + 1
            at = pick(r, 2, my)
            target = chip + (((at - o) & 3) - at) * pick(r, 2, STRIDES)
        for dev in range(2):
            mine = owner == 2 * target + dev
            rank = dot(mine.astype(F32).astype(BF), before)
            for k in range(2):
                col = jnp.sum(jnp.where(mine & (rank == float(k)), code, 0.0), axis=1, keepdims=True)
                table = jnp.where(lane == sel * 4 + dev * 2 + k, col, table)
    table = table.astype(jnp.int32) - 1
    valid = table >= 0
    partners = table & 2047
    local = partners & 15
    sel = lane >> 2
    lane_r = jnp.where(sel > 3, 1, 0)
    lane_o = jnp.where(sel > 0, sel - 3 * lane_r, 0)
    places, offsets = [], []
    for r in range(PARTS):
        offs = []
        for phase in range(3):
            here = pick(r, phase, my)
            if phase == 2:
                here = here - jnp.where(lane_r == r, lane_o, 0)
            offs.append((((partners >> pick(r, phase, (9, 7, 5))) & 3) - here) & 3)
        places.append((offs[1] * 4 + offs[0]) * IMG + local)
        offsets.append(offs[2])
    ids = iota((groups, HELD), 1)

    def present(r, sel, o):
        spot = jnp.where(valid & (offsets[r] == o), places[r], -1)
        hits = jnp.zeros((groups, HELD), F32)
        for c in range(sel * 4, sel * 4 + 4):
            hits = jnp.where(spot[:, c : c + 1] == ids, 1.0, hits)
        return jnp.max(hits, axis=0, keepdims=True)

    sent = jnp.concatenate(
        [present(r, 1 + 3 * r + o - 1 if o else 0, o) for r in range(PARTS) for o in range(4)],
        axis=0,
    )
    sent_rank = jnp.where(sent > 0.0, dot(sent.astype(BF), before), -1.0)
    spots = iota((HELD, HELD), 0).astype(F32)
    images = iota((HELD, HELD), 1).astype(F32)
    for c in range(4 * PARTS):
        col = jnp.sum(jnp.where(sent_rank[c : c + 1, :] == spots, images, 0.0), axis=1, keepdims=True)
        lists_ref[:, c : c + 1] = col.astype(jnp.int32)
    got = jnp.concatenate(
        [present(r, 0, o) for r in range(PARTS) for o in range(4)], axis=0
    )
    got_rank = dot(got.astype(BF), before)
    key = jnp.where(valid, table >> 11, 127)
    small = iota((groups, 128), 1)
    earlier = (iota((groups, groups), 1) < iota((groups, groups), 0)).astype(F32).astype(BF)
    marks = [(key[:, c : c + 1] == small).astype(F32) for c in range(4)]
    starts = jnp.zeros((1, 128), F32)
    for c in range(4):
        starts = starts + jnp.sum((key[:, c : c + 1] < small).astype(F32), axis=0, keepdims=True)
    offs_ref[...] = jnp.broadcast_to(starts, (8, 128)).astype(jnp.int32)
    long_ids = iota((groups, 512), 1)
    ahead = starts
    ordered = [jnp.zeros((1, 512), F32) for _ in range(PARTS)]
    for c in range(4):
        pos = jnp.sum(marks[c] * (ahead + dot(earlier, marks[c].astype(BF))), axis=1, keepdims=True)
        ahead = ahead + jnp.sum(marks[c], axis=0, keepdims=True)
        pos = jnp.where(valid[:, c : c + 1], pos.astype(jnp.int32), -1)
        chosen = pos == long_ids
        for r in range(PARTS):
            slot = (offsets[r][:, c : c + 1] * HELD).astype(F32)
            for o in range(4):
                spot = jnp.where(valid & (offsets[r] == o), places[r], -1)[:, c : c + 1]
                row = got_rank[r * 4 + o : r * 4 + o + 1, :]
                slot = slot + jnp.sum(jnp.where(spot == ids, row, 0.0), axis=1, keepdims=True)
            ordered[r] = ordered[r] + jnp.sum(jnp.where(chosen, slot, 0.0), axis=0, keepdims=True)
    codes_ref[...] = jnp.concatenate(ordered + [jnp.zeros((8 - PARTS, 512), F32)], axis=0).astype(jnp.int32)
    named = jnp.where(live == 1, own, -1) - (2 * chip + core) * IMG
    for i in range(IMG):
        count = jnp.sum((named == i).astype(F32))
        div_ref[i * TOK : (i + 1) * TOK, :] = jnp.full((TOK, 128), jnp.maximum(count, 1.0), F32)


def count_kernel(first_ref, second_ref, live_ref, longest_ref, seen):
    chips, sources, fields = 64, 128, 4
    width = first_ref.shape[1]

    def iota(shape, axis):
        return lax.broadcasted_iota(jnp.int32, shape, axis)

    wide = iota((chips * fields, width), 0)
    source = iota((sources, width), 0)
    seen[...] = jnp.zeros_like(seen)

    def step(i, carry):
        one, two = first_ref[pl.ds(i, 1), :], second_ref[pl.ds(i, 1), :]
        live = live_ref[pl.ds(i, 1), :] == 1
        for own, partner in ((one, two), (two, one)):
            chip = jnp.where(live, own >> 5, -8)
            local = partner & 15
            weight = jnp.where(
                (local & 2) == 0,
                jnp.where((local & 1) == 0, 1.0, 64.0),
                jnp.where((local & 1) == 0, 4096.0, 262144.0),
            )
            left = jnp.where(chip * fields + (local >> 2) == wide, weight, 0.0).astype(BF)
            right = jnp.where((partner >> 4) == source, 1.0, 0.0).astype(BF)
            seen[...] += dot(right, left, ((1,), (1,)))
        return carry

    lax.fori_loop(0, first_ref.shape[0], step, 0)
    packed = seen[...].astype(jnp.int32)
    found = jnp.zeros(packed.shape, F32)
    digits = jnp.zeros(packed.shape, F32)
    for f in range(fields):
        digit = (packed >> (6 * f)) & 63
        found = found + jnp.where(digit > 0, 1.0, 0.0)
        digits = digits + digit.astype(F32)
    row, col = iota((128, sources), 0), iota((128, sources), 1)
    axis, coord = row >> 3, (row >> 1) & 3
    moved_by = jnp.where(axis == 0, 5, jnp.where(axis == 1, 3, 1))
    member = ((col & 1) == (row & 1)) & (((col >> moved_by) & 3) == coord) & (axis < 3)
    groups = dot(member.astype(F32).astype(BF), found.astype(BF))
    merge = (iota((chips * fields, 128), 0) >> 2) == iota((chips * fields, 128), 1)
    totals = dot(groups.astype(BF), merge.astype(F32).astype(BF))
    named = 2.0 * jnp.sum(live_ref[...].astype(F32))
    crowded = (jnp.max(seen[...]) >= 2.0**24) | (jnp.sum(digits) != named)
    longest_ref[...] = jnp.full(
        longest_ref.shape, jnp.where(crowded, 1000.0, jnp.max(totals)), F32
    )


def gather_kernel(cap, targets, list_ref, *refs):
    held, outs = refs[: 4 * PARTS], refs[4 * PARTS : 4 * PARTS + len(targets)]
    bufs = refs[4 * PARTS + len(targets) :][:PARTS]
    staged = refs[5 * PARTS + len(targets) :][: len(targets)]
    in_sems, out_sems = refs[5 * PARTS + 2 * len(targets) :]
    size = HELD // 4
    loads = [
        pltpu.make_async_copy(held[n], bufs[n // 4].at[pl.ds(n % 4 * size, size)], in_sems.at[n])
        for n in range(4 * PARTS)
    ]
    stores = [
        pltpu.make_async_copy(staged[t], outs[t], out_sems.at[t]) for t in range(len(targets))
    ]
    for c in loads:
        c.start()
    for r in range(PARTS):
        for o in range(4):
            loads[r * 4 + o].wait()
        mine = [(t, o) for t, (block, o) in enumerate(targets) if block == r]

        def step(s, carry, r=r, mine=mine):
            for t, o in mine:
                staged[t][s] = bufs[r][list_ref[s, r * 4 + o]]
            return carry

        lax.fori_loop(0, cap, step, 0, unroll=4)
        for t, _ in mine:
            stores[t].start()
    for c in stores:
        c.wait()


def cross_kernel(cap, code_ref, off_ref, g_ref, qkv_ref, *refs):
    parts = refs[: 4 * PARTS]
    mine_ref, other_ref = refs[4 * PARTS : 4 * PARTS + 2]
    bufs = refs[4 * PARTS + 2 : 5 * PARTS + 2]
    wv, folded, xs, acc, mix, sems, g_sems = refs[5 * PARTS + 2 :]
    images = folded.shape[0]
    groups = images // WIDE
    copies = [
        pltpu.make_async_copy(
            parts[r * 4 + o], bufs[r].at[pl.ds(o * cap, cap)], sems.at[r * 4 + o]
        )
        for r in range(PARTS)
        for o in range(4)
    ]
    loads = [
        pltpu.make_async_copy(
            g_ref.at[pl.ds(i * WIDE, WIDE)], folded.at[pl.ds(i * WIDE, WIDE)], g_sems.at[i]
        )
        for i in range(groups)
    ]
    value_load = pltpu.make_async_copy(qkv_ref.at[:, pl.ds(2 * D, D)], wv, sems.at[4 * PARTS])
    for c in copies + loads[:1]:
        c.start()
    for c in copies:
        c.wait()
    for c in loads[1:] + [value_load]:
        c.start()
    row_pair = lax.broadcasted_iota(jnp.int32, (GROUP * TOK, 1), 0) // TOK

    def attended(a, chunk, i):
        start = off_ref[0, a] + chunk * GROUP
        left = off_ref[0, a + 1] - start
        for j in range(GROUP):
            p = jnp.where(j < left, start + j, 0)
            for r in range(PARTS):
                code = code_ref[r, p]
                xs[i, j * TOK : (j + 1) * TOK, STARTS[r] : STARTS[r] + WIDTHS[r]] = bufs[r][
                    (code >> 8) * cap + jnp.minimum(code & 255, cap - 1)
                ]
        x = xs[i]
        s = dot(x, folded[a], ((1,), (1,))).reshape(GROUP, TOK, HEADS * TOK)
        e = jnp.exp(s - jnp.max(s, axis=1, keepdims=True))
        w = (e / jnp.sum(e, axis=1, keepdims=True)).reshape(GROUP * TOK, HEADS * TOK)
        w = jnp.where(row_pair < left, w, 0.0).astype(BF)
        return dot(w, x, ((0,), (0,)))

    def group(step, carry):
        for i in range(WIDE):
            mix[step * WIDE + i] = attended(step * WIDE + i, 0, i).astype(BF)
        return carry

    if cap < HELD:
        for step in range(groups):
            loads[step].wait()
            group(step, 0)
    else:
        for c in loads:
            c.wait()
        lax.fori_loop(0, groups, group, 0)

    def longer(a, carry):
        chunks = (off_ref[0, a + 1] - off_ref[0, a] + GROUP - 1) // GROUP

        @pl.when(chunks > 1)
        def _():
            acc[...] = mix[a].astype(F32)

            def more(c, carry):
                acc[...] += attended(a, c, 0)
                return carry

            lax.fori_loop(1, chunks, more, 0)
            mix[a] = acc[...].astype(BF)

        return carry

    lax.fori_loop(0, images, longer, 0)
    value_load.wait()
    for h in range(HEADS):
        u = mix[:, h * TOK : (h + 1) * TOK, :].reshape(images * TOK, D)
        o = dot(u, wv[:, h * DH : (h + 1) * DH])
        mine_ref[:, h * DH : (h + 1) * DH] = o[: IMG * TOK]
        other_ref[:, h * DH : (h + 1) * DH] = o[IMG * TOK :].astype(BF)


def head_kernel(
    mine_ref, other_ref, div_ref, base_ref, cross_out_ref, gain_ref, weight_ref,
    out_ref, weights, staged, in_sems, out_sems,
):
    tile = weight_ref.shape[1] // HEAD_TILES
    loads = [
        pltpu.make_async_copy(
            weight_ref.at[:, pl.ds(t * tile, tile)], weights.at[t], in_sems.at[t]
        )
        for t in range(HEAD_TILES)
    ]
    for c in loads:
        c.start()
    total = mine_ref[...] + other_ref[...].astype(F32)
    mean = (total / div_ref[:, :1]).astype(BF)
    combined = base_ref[...] + dot(mean, cross_out_ref[...])
    rows = norm(combined, gain_ref[...].reshape(1, D)).astype(BF)
    stores = [
        pltpu.make_async_copy(
            staged.at[t], out_ref.at[:, pl.ds(t * tile, tile)], out_sems.at[t]
        )
        for t in range(HEAD_TILES)
    ]
    for t in range(HEAD_TILES):
        loads[t].wait()
        staged[t] = dot(rows, weights[t]).astype(BF)
        stores[t].start()
    for c in stores:
        c.wait()


def from_offset(x, r, phase, offset):
    pairs = []
    for chip in range(64):
        for core in range(2):
            stride = STRIDES[ORDERS[r][core][phase]]
            c = (chip // stride) % 4
            to = chip + ((c - offset) % 4 - c) * stride
            pairs.append((2 * chip + core, 2 * to + core))
    return lax.ppermute(x, ("img", "grp"), pairs)


def tied(values, others):
    values, _ = lax.optimization_barrier((values, others))
    return values


def exchange(blocks, phase, meanwhile=None):
    got = [[b[0], None, None, None] for b in blocks]

    def send(r, o, block):
        got[r][o] = from_offset(block, r, phase, o)

    for r, o in FIRST_ROUND:
        send(r, o, blocks[r][o])
    for r, early, late in ((0, (2,), (1, 3)), (1, (1, 3), (2,))):
        for o in late:
            waits = [got[r][e] for e in early] + ([] if meanwhile is None else [meanwhile])
            send(r, o, tied(blocks[r][o], waits) if phase else blocks[r][o])
    return got


def body(
    tokens, pair_list, pair_live, gain_self, gain_cross, gain_head,
    self_qkv, self_out, cross_qkv, cross_out, head_weight,
):
    chip = lax.axis_index("img")
    core = lax.axis_index("grp")
    flat_tokens = tokens.reshape(IMG * TOK, D)
    *rows, own_rows = call(
        norm_kernel,
        [sds(IMG * TOK, w) for w in WIDTHS + (D,)],
        [VMEM] * 2,
        [VMEM] * (PARTS + 1),
    )(flat_tokens, gain_cross)
    blocks = [x.reshape(IMG, TOK, -1) for x in rows]
    near = exchange([[blocks[r]] * 4 for r in range(PARTS)], 0)
    near = lax.optimization_barrier(near)
    lines = call(
        join_kernel, [sds(4 * IMG, TOK, w) for w in WIDTHS], [VMEM] * (4 * PARTS), [VMEM] * PARTS
    )(*[x for row in near for x in row])

    ids = jnp.stack([chip, core]).astype(jnp.int32)
    first, second = pair_list[:, 0], pair_list[:, 1]
    square = [x.reshape(128, 128) for x in (first, second, pair_live)]
    flat = [x.reshape(16, 1024) for x in (first, second, pair_live)]
    lists, codes, offsets, divisor = call(
        plan_kernel,
        [
            sds(HELD, 4 * PARTS, dtype=jnp.int32),
            sds(8, 512, dtype=jnp.int32),
            sds(8, 128, dtype=jnp.int32),
            sds(IMG * TOK, 128, dtype=F32),
        ],
        [SMEM] + [VMEM] * 3,
        [VMEM] * 4,
        limit=FULL,
    )(ids, *tied(square, lines))
    held = exchange([[lines[r]] * 4 for r in range(PARTS)], 1, lists)
    own_rows, late_tokens = tied([own_rows, flat_tokens], [held[0][2], held[1][1]])
    other_rows = lax.ppermute(own_rows, "grp", [(0, 1), (1, 0)])
    base = call(
        self_kernel,
        sds(IMG * TOK, D, dtype=F32),
        [VMEM] * 4,
        HBM,
        [pltpu.VMEM((IMG * TOK, D), F32), pltpu.SemaphoreType.DMA],
        limit=FULL,
    )(late_tokens, gain_self, self_qkv, self_out)

    def gathered(cap, targets, lists, held):
        widths = [WIDTHS[r] for r, _ in targets]
        return call(
            functools.partial(gather_kernel, cap, targets),
            [sds(cap, TOK, w) for w in widths],
            [SMEM] + [HBM] * (4 * PARTS),
            [HBM] * len(targets),
            [
                *[pltpu.VMEM((HELD, TOK, w), BF) for w in WIDTHS],
                *[pltpu.VMEM((cap, TOK, w), BF) for w in widths],
                pltpu.SemaphoreType.DMA((4 * PARTS,)),
                pltpu.SemaphoreType.DMA((len(targets),)),
            ],
            limit=FULL,
        )(lists, *[x for row in held for x in row])

    def grid_of(targets, values):
        found = dict(zip(targets, values))
        return [[found[r, o] for o in range(4)] for r in range(PARTS)]

    def crossed(cap, codes, offsets, folded, cross, arrived):
        return call(
            functools.partial(cross_kernel, cap),
            [sds(IMG * TOK, D, dtype=F32), sds(IMG * TOK, D)],
            [SMEM] * 2 + [HBM] * (2 + 4 * PARTS),
            [VMEM] * 2,
            [
                *[pltpu.VMEM((4 * cap, TOK, w), BF) for w in WIDTHS],
                pltpu.VMEM((D, D), BF),
                pltpu.VMEM((2 * IMG, HEADS * TOK, D), BF),
                pltpu.VMEM((WIDE, GROUP * TOK, D), BF),
                pltpu.VMEM((HEADS * TOK, D), F32),
                pltpu.VMEM((2 * IMG, HEADS * TOK, D), BF),
                pltpu.SemaphoreType.DMA((4 * PARTS + 1,)),
                pltpu.SemaphoreType.DMA((2 * IMG // WIDE,)),
            ],
            limit=FULL,
        )(codes, offsets, folded, cross, *[x for row in arrived for x in row])

    sent_first = gathered(CAP, FIRST_ROUND, tied(lists, [base, other_rows]), held)
    all_weight = lax.all_gather(tied(head_weight, sent_first), "grp", axis=1, tiled=True)
    sent_later = gathered(CAP, LATER, tied(lists, sent_first), held)
    chosen = grid_of(FIRST_ROUND + LATER, [*sent_first, *sent_later])
    own_rows, other_rows = tied([own_rows, other_rows], sent_first)
    folded = call(
        fold_kernel,
        sds(2 * IMG, HEADS * TOK, D),
        [VMEM] * 3,
        HBM,
        [pltpu.VMEM((2 * IMG, HEADS * TOK, D), BF), pltpu.SemaphoreType.DMA],
        limit=FULL,
    )(
        own_rows, other_rows, cross_qkv
    )
    arrived = exchange(chosen, 2, folded)
    longest = call(
        count_kernel,
        sds(8, 128, dtype=F32),
        [VMEM] * 3,
        VMEM,
        [pltpu.VMEM((128, 256), F32)],
        limit=FULL,
    )(*tied(flat, [arrived[0][2], arrived[1][1]]))[0, 0]
    sums = crossed(CAP, codes, offsets, folded, cross_qkv, arrived)

    def redo(state):
        targets = FIRST_ROUND + LATER
        again = exchange(grid_of(targets, gathered(HELD, targets, lists, held)), 2)
        return (jnp.zeros((), F32), *crossed(HELD, codes, offsets, folded, cross_qkv, again))

    _, mine_sum, other_sum = lax.while_loop(lambda state: state[0] > CAP, redo, (longest, *sums))
    size = IMG * TOK
    other_sum = lax.ppermute(other_sum, "grp", [(0, 1), (1, 0)])
    outc = all_weight.shape[1]
    pixel_maps = call(
        head_kernel,
        sds(size, outc),
        [VMEM] * 6 + [HBM],
        HBM,
        [
            pltpu.VMEM((HEAD_TILES, D, outc // HEAD_TILES), BF),
            pltpu.VMEM((HEAD_TILES, size, outc // HEAD_TILES), BF),
            pltpu.SemaphoreType.DMA((HEAD_TILES,)),
            pltpu.SemaphoreType.DMA((HEAD_TILES,)),
        ],
        limit=FULL,
    )(mine_sum, other_sum, divisor, base, cross_out, gain_head, all_weight)
    return pixel_maps.reshape(IMG, TOK, -1)


def solution(mesh):
    placed = (P(("img", "grp"), None, None),) + (P(),) * 9 + (P(None, "grp"),)
    return jax.shard_map(
        body, mesh=mesh, in_specs=placed, out_specs=P(("img", "grp"), None, None), check_vma=False
    )
```
